256 devices in a mesh: frames: 8 (over z_lo, x), dp: 32 (over y, z_hi, core).
Axes of the slice: x: 4, y: 4, z: 8 (z_hi: 4, z_lo: 2; z = z_hi * 2 + z_lo), core: 2. Of those that a mesh axis runs over, the one named last changes fastest.
Arguments:
- latents: bfloat16 [32, 16, 144, 640], P('dp', 'frames'), may hold values from -80 to 80
- pose: int32 [32, 16, 144], P('dp', 'frames'), may hold values from 0 to 18
- timesteps: int32 [32], P('dp'), may hold values from 0 to 999
- norm_gain: float32 [640], replicated, may hold values from 0.1 to 1.9
- norm_bias: float32 [640], replicated, may hold values from -0.5 to 0.5
- pose_table: float32 [19, 640], replicated, may hold values from -6 to 6
- time_weight: float32 [320, 640], replicated, may hold values from -0.3125 to 0.3125
- spatial_weight: bfloat16 [5760, 640], P('dp'), may hold values from -0.078125 to 0.078125
- temporal_weight: bfloat16 [1920, 640], P('dp'), may hold values from -0.125 to 0.125
- cotangent: bfloat16 [32, 16, 144, 640], P('dp', 'frames'), may hold values from -16 to 16
Outputs:
- mixed: float32 [32, 16, 144, 640], P('dp', 'frames')
- latent_grad: float32 [32, 16, 144, 640], P('dp', 'frames')
- temporal_grad: float32 [1920, 640], P('dp')
The draws below stay inside these ranges and needn't reach their ends.
All inputs are finite; a program needn't handle non-finite values.
Results may differ from the reference program's by a relative error of at most 0.0053.
Values may be sent and summed in bfloat16 or wider, within the bound.
No kernel may reach another device: no remote copies, remote signals or barrier semaphores. Data moves between devices by JAX's collectives and lax.ppermute only.
A program may use at most 128 MiB of HBM per device.

```python
import math
import jax
import jax.numpy as jnp
import numpy as np
from jax import lax

C = 640
GROUP_CH = 40
HT = 9
WD = 16
TE = 320
KP = 19
PIX = 144
FRAMES = 16
CLIPS = 32


def frame_ramp(power):
    positions = jnp.arange(FRAMES, dtype=jnp.float32) / max(FRAMES - 1, 1)
    return jnp.exp(math.log(power) * positions)


def draw_latents(key, part):
    channel_key = jax.random.fold_in(key, 11)
    noise_key = jax.random.fold_in(key, 12)
    channel_scale = jnp.exp(jax.random.uniform(channel_key, (C,), jnp.float32, math.log(0.3), math.log(3.0)))
    noise = jnp.clip(jax.random.normal(noise_key, (CLIPS, FRAMES, PIX, C), jnp.float32), -4.0, 4.0)
    values = noise * channel_scale * frame_ramp(3.0)[None, :, None, None]
    return values.astype(jnp.bfloat16)


def draw_cotangent(key, part):
    noise_key = jax.random.fold_in(key, 21)
    noise = jnp.clip(jax.random.normal(noise_key, (CLIPS, FRAMES, PIX, C), jnp.float32), -4.0, 4.0)
    values = noise * frame_ramp(3.0)[None, :, None, None]
    return values.astype(jnp.bfloat16)


def with_ends(array, key, smallest, high):
    longest = array.shape.index(max(array.shape))
    spots = []
    for shift in (0, 1):
        where = [jax.random.randint(jax.random.fold_in(key, axis), (), 0, length) for axis, length in enumerate(array.shape)]
        where[longest] = (where[longest] + shift) % array.shape[longest]
        spots.append(tuple(where))
    return array.at[spots[0]].set(smallest).at[spots[1]].set(high)


def shard_levels(stream_key, shape, cuts, smallest, largest):
    factor_of = 1.0
    for dim, blocks in cuts:
        steps = jax.random.uniform(jax.random.fold_in(jax.random.fold_in(stream_key, 6), dim), (blocks,), jnp.float32, smallest / len(cuts), largest / len(cuts))
        factor_of = factor_of * jnp.repeat(jnp.exp(steps), shape[dim] // blocks).reshape((-1,) + (1,) * (len(shape) - 1 - dim))
    return factor_of


def rank_table(amount, lean):
    weights = [(1 << 20) // math.isqrt(standing ** lean) + 1 for standing in range(1, amount + 1)]
    scale = 1 + sum(weights) // (1 << 30)
    return np.cumsum(np.array([max(1, weight // scale) for weight in weights]))


def skewed_ids(rng, shape, count, slope):
    grid = rank_table(count, slope)
    lot = jax.random.randint(jax.random.fold_in(rng, 1), shape, 0, int(grid[count - 1]))
    standing = jnp.searchsorted(jnp.asarray(grid, jnp.int32), lot, side="right")
    return jax.random.permutation(jax.random.fold_in(rng, 2), count)[standing].astype(jnp.int32)


def normal_values(own_key, shape, deviation, most, cuts=(), kind=jnp.bfloat16):
    drawn = jax.random.normal(own_key, shape, jnp.float32) * deviation
    if len(cuts) > 0:
        drawn = shard_levels(own_key, shape, cuts, -0.22, 0.18) * drawn
    return jnp.clip(drawn, min=-most, max=most).astype(kind)


def setup_inputs(seed: int = 0) -> dict:
    key_of = jax.random.split(jax.random.key(seed), 11)
    latents = draw_latents(jax.random.fold_in(key_of[10], 71), 0)
    pose = with_ends(skewed_ids(key_of[1], (CLIPS, FRAMES, PIX), KP, 2), jax.random.fold_in(key_of[1], 3), 0, KP - 1).astype(jnp.int32)
    timesteps = with_ends(jax.random.randint(key_of[2], (CLIPS,), 0, 1000), jax.random.fold_in(key_of[2], 1), 0, 999).astype(jnp.int32)
    norm_gain = jnp.clip(1.0 + 0.18 * jax.random.normal(key_of[3], (C,), jnp.float32), 0.1, 1.9)
    norm_bias = jnp.clip(jax.random.uniform(key_of[4], (C,), jnp.float32, -0.5, 0.5), -0.5, 0.5)
    pose_table = normal_values(key_of[5], (KP, C), 1.0, 6.0, (), jnp.float32)
    time_weight = normal_values(key_of[6], (TE, C), TE ** -0.5, 0.3125, (), jnp.float32)
    spatial_weight = normal_values(key_of[7], (9 * C, C), (9 * C) ** -0.5, 0.078125, ((0, 32),))
    temporal_weight = normal_values(key_of[8], (3 * C, C), (3 * C) ** -0.5, 0.125, ((0, 32),))
    cotangent = draw_cotangent(jax.random.fold_in(key_of[10], 71), 0)
    return {"latents": latents, "pose": pose, "timesteps": timesteps, "norm_gain": norm_gain, "norm_bias": norm_bias, "pose_table": pose_table, "time_weight": time_weight, "spatial_weight": spatial_weight, "temporal_weight": temporal_weight, "cotangent": cotangent}


def silu_slope(value):
    gate = jax.nn.sigmoid(value)
    return gate * (1.0 + value * (1.0 - gate))

def spatial_cols(field, sign):
    count_n, height, width, chans = field.shape
    padded = jnp.pad(field, ((0, 0), (1, 1), (1, 1), (0, 0)))
    pieces = []
    for row_tap in range(3):
        for col_tap in range(3):
            top = 1 + sign * (row_tap - 1)
            left = 1 + sign * (col_tap - 1)
            pieces.append(padded[:, top:top + height, left:left + width, :])
    return jnp.concatenate(pieces, axis=-1).reshape(count_n * height * width, 9 * chans)

def temporal_cols(extended, frame_span, sign):
    pieces = []
    for tap in range(3):
        begin = 1 + sign * (tap - 1)
        pieces.append(extended[:, begin:begin + frame_span])
    joined = jnp.concatenate(pieces, axis=-1)
    return joined.reshape(-1, joined.shape[-1])

def time_shift(timesteps, time_weight):
    half = time_weight.shape[0] // 2
    positions = jnp.arange(half, dtype=jnp.float32)
    frequencies = jnp.exp(-math.log(10000.0) * positions / half)
    angles = timesteps.astype(jnp.float32)[:, None] * frequencies[None, :]
    embedding = jnp.concatenate([jnp.cos(angles), jnp.sin(angles)], axis=-1)
    return jnp.dot(embedding, time_weight, precision=lax.Precision.HIGHEST)

def pose_rows(pose, pose_table):
    kinds = jnp.arange(pose_table.shape[0], dtype=jnp.int32)
    onehot = (pose[..., None] == kinds).astype(jnp.float32)
    return jnp.dot(onehot, pose_table, precision=lax.Precision.HIGHEST)

def reference(latents, pose, timesteps, norm_gain, norm_bias, pose_table, time_weight, spatial_weight, temporal_weight, cotangent):
    groups = C // GROUP_CH
    entries = float(PIX * GROUP_CH)
    factor = 1.0 / math.sqrt(CLIPS * FRAMES * PIX)
    shifts = time_shift(timesteps, time_weight)
    spatial_three = spatial_weight.astype(jnp.float32).reshape(9, C, C)
    temporal_three = temporal_weight.astype(jnp.float32).reshape(3, C, C)

    def one_clip(running, items):
        clip_x, clip_pose, clip_shift, clip_grad = items
        shifted = clip_x.astype(jnp.float32) + pose_rows(clip_pose, pose_table)
        grouped = shifted.reshape(FRAMES, PIX, groups, GROUP_CH)
        center = lax.optimization_barrier(jnp.sum(grouped, axis=(1, 3))) / entries
        variance = lax.optimization_barrier(jnp.sum(grouped * grouped, axis=(1, 3))) / entries - center * center
        inv_std = lax.rsqrt(variance + 1e-05)[:, None, :, None]
        normed_g = (grouped - center[:, None, :, None]) * inv_std
        normed = normed_g.reshape(FRAMES, PIX, C)
        before = normed * norm_gain + norm_bias
        activated = jax.nn.silu(before).astype(jnp.bfloat16)
        act_cols = spatial_cols(activated.reshape(FRAMES, HT, WD, C), 1)
        convolved = jnp.dot(act_cols, spatial_weight, preferred_element_type=jnp.float32)
        spatial_out = (convolved.reshape(FRAMES, PIX, C) + clip_shift).astype(jnp.bfloat16)
        extended = jnp.pad(spatial_out[None], ((0, 0), (1, 1), (0, 0), (0, 0)))
        moved_ext = jax.nn.silu(extended.astype(jnp.float32)).astype(jnp.bfloat16)
        moved_cols = temporal_cols(moved_ext, FRAMES, 1)
        temporal_out = jnp.dot(moved_cols, temporal_weight, preferred_element_type=jnp.float32)
        mixed = spatial_out.astype(jnp.float32) + temporal_out.reshape(FRAMES, PIX, C)
        grad_ext = jnp.pad(clip_grad[None], ((0, 0), (1, 1), (0, 0), (0, 0)))
        grad_cols = temporal_cols(grad_ext, FRAMES, -1)
        back_moved = jnp.einsum('rtc,tkc->rk', grad_cols.astype(jnp.float32).reshape(-1, 3, C), temporal_three, precision=lax.Precision.HIGHEST)
        back_spatial = (clip_grad.astype(jnp.float32) + back_moved.reshape(FRAMES, PIX, C) * silu_slope(spatial_out.astype(jnp.float32))).astype(jnp.bfloat16)
        partial_grad = lax.dot_general(moved_cols, clip_grad.reshape(-1, C), (((0,), (0,)), ((), ())), preferred_element_type=jnp.float32)
        back_cols = spatial_cols(back_spatial.reshape(FRAMES, HT, WD, C), -1)
        back_act = jnp.einsum('rtc,tkc->rk', back_cols.astype(jnp.float32).reshape(-1, 9, C), spatial_three, precision=lax.Precision.HIGHEST)
        back_normed = back_act.reshape(FRAMES, PIX, C) * silu_slope(before) * norm_gain
        back_grouped = back_normed.reshape(FRAMES, PIX, groups, GROUP_CH)
        first_mean = lax.optimization_barrier(jnp.sum(back_grouped, axis=(1, 3))) / entries
        second_mean = lax.optimization_barrier(jnp.sum(back_grouped * normed_g, axis=(1, 3))) / entries
        latent_grad = inv_std * (back_grouped - first_mean[:, None, :, None] - normed_g * second_mean[:, None, :, None])
        latent_grad = latent_grad.reshape(FRAMES, PIX, C)
        return (running + partial_grad, (mixed, latent_grad))
    start_grad = jnp.zeros((3 * C, C), jnp.float32)
    summed, (mixed, latent_grad) = lax.scan(one_clip, start_grad, (latents, pose, shifts, cotangent))
    return (mixed, latent_grad, summed * factor)
```

```python
import math

import jax
import jax.numpy as jnp
from jax import lax
from jax.experimental import pallas as pl
from jax.experimental.pallas import tpu as pltpu
from jax.sharding import PartitionSpec as P

GROUP_CH = 40
HT = 9
WD = 16
PIX = HT * WD
C = 640
NX, NY, NZH, NZL, NC = 4, 4, 4, 2, 2
AXES = ("frames", "dp")
SROWS, SPAD, SQ = 180, 192, 48
TROWS, TPAD, TQ = 60, 64, 16
QROWS = SQ + TQ
ROWS = 2 * PIX
F32 = jnp.float32
BF16 = jnp.bfloat16
VLIM = 58 * 1024 * 1024


def coords():
    for zl in range(NZL):
        for x in range(NX):
            for y in range(NY):
                for zh in range(NZH):
                    for c in range(NC):
                        yield zl, x, y, zh, c


def index_of(zl, x, y, zh, c):
    return (zl * NX + x) * (NY * NZH * NC) + (y * NZH + zh) * NC + c


def routes(move):
    return [(index_of(*at), index_of(*move(*at))) for at in coords()]


def send(value, move):
    return lax.ppermute(value, AXES, routes(move))


def core_swap(zl, x, y, zh, c):
    return zl, x, y, zh, 1 - c


def zl_swap(zl, x, y, zh, c):
    return 1 - zl, x, y, zh, c


def zh_step(k):
    return lambda zl, x, y, zh, c: (zl, x, y, (zh + k) % NZH, c)


def x_step(k):
    return lambda zl, x, y, zh, c: (zl, (x + k) % NX, y, zh, c)


def xy_step(k):
    return lambda zl, x, y, zh, c: (
        (zl, (x + k) % NX, y, zh, c) if c == 0 else (zl, x, (y + k) % NY, zh, c)
    )


def yx_step(k):
    return lambda zl, x, y, zh, c: (
        (zl, x, (y + k) % NY, zh, c) if c == 0 else (zl, (x + k) % NX, y, zh, c)
    )


def in_order(own, received, place):
    parts = [received[2], received[1], received[0], own]
    stacked = jnp.stack(parts + parts)
    return lax.dynamic_slice_in_dim(stacked, (3 - place) % 4, 4, axis=0)


def silu_slope(value):
    gate = jax.nn.sigmoid(value)
    return gate * (1.0 + value * (1.0 - gate))


def spatial_cols(field, sign):
    count_n, height, width, chans = field.shape
    padded = jnp.pad(field, ((0, 0), (1, 1), (1, 1), (0, 0)))
    pieces = []
    for row_tap in range(3):
        for col_tap in range(3):
            top = 1 + sign * (row_tap - 1)
            left = 1 + sign * (col_tap - 1)
            pieces.append(padded[:, top : top + height, left : left + width, :])
    return jnp.concatenate(pieces, axis=-1).reshape(count_n * height * width, 9 * chans)


def time_shift(timesteps, time_weight):
    half = time_weight.shape[0] // 2
    positions = jnp.arange(half, dtype=jnp.float32)
    frequencies = jnp.exp(-math.log(10000.0) * positions / half)
    angles = timesteps.astype(jnp.float32)[:, None] * frequencies[None, :]
    embedding = jnp.concatenate([jnp.cos(angles), jnp.sin(angles)], axis=-1)
    return jnp.dot(embedding, time_weight, precision=lax.Precision.HIGHEST)


def pose_rows(pose, pose_table):
    kinds = jnp.arange(pose_table.shape[0], dtype=jnp.int32)
    onehot = (pose[..., None] == kinds).astype(jnp.float32)
    return jnp.dot(onehot, pose_table, precision=lax.Precision.HIGHEST)


def load_copies(place, pieces, whole, sems, rows, offset):
    x, y, core = place[0], place[1], place[3]
    copies = []
    for own in (0, 1):
        flow = core if own == 0 else 1 - core
        for far in range(4):
            for near in range(4):
                from_y = lax.rem(y + 4 - jnp.where(flow == 0, far, near), 4)
                from_x = lax.rem(x + 4 - jnp.where(flow == 0, near, far), 4)
                copies.append(
                    pltpu.make_async_copy(
                        pieces[own * 4 + far].at[near, :, pl.ds(offset, rows), :],
                        whole.at[from_y, flow, :, pl.ds(pl.multiple_of(from_x * rows, rows), rows), :],
                        sems.at[len(copies)],
                    )
                )
    return copies


def forward_kernel(place, cols, shift, *rest):
    pieces, (spatial_out, moved, whole, total, sems) = rest[:8], rest[8:]
    copies = load_copies(place, pieces, whole, sems, SQ, 0)
    for copy in copies:
        copy.start()
    for copy in copies:
        copy.wait()
    for part in range(8):
        y, core = divmod(part, 2)
        product = jnp.dot(
            cols[y, core],
            whole[y, core].reshape(NZH * SPAD, C),
            preferred_element_type=F32,
        )
        if part == 0:
            total[...] = product + shift[...]
        else:
            total[...] += product
    rounded = total[...].astype(BF16)
    spatial_out[...] = rounded
    wide = rounded.astype(F32)
    moved[...] = (wide * jax.nn.sigmoid(wide)).astype(BF16)


def any_specs(count):
    return [pl.BlockSpec(memory_space=pl.ANY)] * count


def vmem_specs(count):
    return [pl.BlockSpec(memory_space=pltpu.VMEM)] * count


SMEM_SPEC = [pl.BlockSpec(memory_space=pltpu.SMEM)]


def cost(flops, moved):
    return pl.CostEstimate(flops=flops, bytes_accessed=moved, transcendentals=0)


def forward(place, cols, shift, pieces):
    return pl.pallas_call(
        forward_kernel,
        out_shape=(jax.ShapeDtypeStruct((ROWS, C), BF16), jax.ShapeDtypeStruct((ROWS, C), BF16)),
        in_specs=SMEM_SPEC + vmem_specs(2) + any_specs(8),
        out_specs=tuple(vmem_specs(2)),
        scratch_shapes=[
            pltpu.VMEM((NY, NC, NZH, SPAD, C), BF16),
            pltpu.VMEM((ROWS, C), F32),
            pltpu.SemaphoreType.DMA((32,)),
        ],
        compiler_params=pltpu.CompilerParams(vmem_limit_bytes=VLIM),
        cost_estimate=cost(2 * ROWS * 6144 * C, 12_000_000),
        name="spatial_forward",
    )(place, cols, shift, *pieces)


def grad_kernel(place, moved, cot_ext, mine, other, total):
    core = place[3]
    left = moved[...]
    for tap in range(3):
        right = cot_ext[pl.ds((2 - tap) * PIX, ROWS), :]
        total[pl.ds(tap * C, C), :] = lax.dot_general(
            left, right, (((0,), (0,)), ((), ())), preferred_element_type=F32
        )
    total[pl.ds(3 * C, 8), :] = jnp.zeros((8, C), F32)
    for block in range(32):
        spot = block // 2
        rows = total[pl.ds(block * TROWS, TPAD), :]

        @pl.when(core == block % 2)
        def _():
            mine[spot // 4, spot % 4] = rows

        @pl.when(core != block % 2)
        def _():
            other[spot // 4, spot % 4] = rows.astype(BF16)


def grad_terms(place, moved, cot_ext):
    shape = (NY, NZH, TPAD, C)
    return pl.pallas_call(
        grad_kernel,
        out_shape=(jax.ShapeDtypeStruct(shape, F32), jax.ShapeDtypeStruct(shape, BF16)),
        in_specs=SMEM_SPEC + vmem_specs(2),
        out_specs=tuple(vmem_specs(2)),
        scratch_shapes=[pltpu.VMEM((3 * C + 8, C), F32)],
        compiler_params=pltpu.CompilerParams(vmem_limit_bytes=VLIM),
        cost_estimate=cost(2 * ROWS * 3 * C * C, 5_000_000),
        name="temporal_grad_terms",
    )(place, moved, cot_ext)


def split_first_kernel(place, mine, came, own, *sends):
    x, y, core = place[0], place[1], place[3]

    @pl.when(core == 0)
    def _():
        for k in range(4):
            part = lax.rem(y + k, 4)
            value = (mine[part] + came[part].astype(F32)).reshape(4 * TPAD, C)
            if k == 0:
                own[...] = value
            else:
                sends[k - 1][...] = value.astype(BF16)

    @pl.when(core != 0)
    def _():
        for k in range(4):
            rows = pl.ds(pl.multiple_of(lax.rem(x + k, 4) * TQ, TQ), TQ)
            value = (mine[:, :, rows, :] + came[:, :, rows, :].astype(F32)).reshape(16 * TQ, C)
            if k == 0:
                own[...] = value
            else:
                sends[k - 1][...] = value.astype(BF16)


def split_first(place, mine, came):
    shape = (4 * TPAD, C)
    return pl.pallas_call(
        split_first_kernel,
        out_shape=(jax.ShapeDtypeStruct(shape, F32),) + (jax.ShapeDtypeStruct(shape, BF16),) * 3,
        in_specs=SMEM_SPEC + vmem_specs(2),
        out_specs=tuple(vmem_specs(4)),
        compiler_params=pltpu.CompilerParams(vmem_limit_bytes=VLIM),
        cost_estimate=cost(0, 4_000_000),
        name="grad_split_first",
    )(place, mine, came)


def split_second_kernel(place, held, first, second, third, own, *sends):
    x, y, core = place[0], place[1], place[3]
    own_sends = (own,) + tuple(sends)

    @pl.when(core == 0)
    def _():
        for k in range(4):
            for zh in range(NZH):
                start = zh * TPAD + lax.rem(x + k, 4) * TQ
                rows = pl.ds(pl.multiple_of(start, TQ), TQ)
                value = held[rows, :]
                for term in (first, second, third):
                    value += term[rows, :].astype(F32)
                own_sends[k][zh] = value

    @pl.when(core != 0)
    def _():
        for k in range(4):
            rows = pl.ds(pl.multiple_of(lax.rem(y + k, 4) * TPAD, TPAD), TPAD)
            value = held[rows, :]
            for term in (first, second, third):
                value += term[rows, :].astype(F32)
            own_sends[k][...] = value.reshape(NZH, TQ, C)


def split_second(place, held, terms):
    shape = (NZH, TQ, C)
    return pl.pallas_call(
        split_second_kernel,
        out_shape=(jax.ShapeDtypeStruct(shape, F32),) * 4,
        in_specs=SMEM_SPEC + vmem_specs(4),
        out_specs=tuple(vmem_specs(4)),
        compiler_params=pltpu.CompilerParams(vmem_limit_bytes=VLIM),
        cost_estimate=cost(0, 2_000_000),
        name="grad_split_second",
    )(place, held, *terms)


def split_third_kernel(place, held, first, second, third, *parts):
    zh = place[2]
    for k in range(4):
        part = lax.rem(zh + k, 4)
        parts[k][...] = held[part] + first[part] + second[part] + third[part]


def split_third(place, held, terms):
    return pl.pallas_call(
        split_third_kernel,
        out_shape=(jax.ShapeDtypeStruct((TQ, C), F32),) * 4,
        in_specs=SMEM_SPEC + vmem_specs(4),
        out_specs=tuple(vmem_specs(4)),
        cost_estimate=cost(0, 800_000),
        name="grad_split_third",
    )(place, held, *terms)


def slope_of(value):
    gate = jax.nn.sigmoid(value)
    return gate * (1.0 + value * (1.0 - gate))


def temporal_kernel(place, cot_ext, moved_ext, spatial_out, *rest):
    pieces, (mixed, back_spatial, whole, wide, sems) = rest[:8], rest[8:]
    copies = load_copies(place, pieces, whole, sems, TQ, SQ)
    for copy in copies:
        copy.start()
    for copy in copies:
        copy.wait()
    for block in range(32):
        pair, core = divmod(block, 2)
        wide[pl.ds(block * TROWS, TPAD), :] = whole[pair // 4, core, pair % 4].astype(F32)
    ahead = spatial_out[...].astype(F32)
    back = jnp.zeros((ROWS, C), F32)
    for tap in range(3):
        weight = wide[pl.ds(tap * C, C), :].astype(BF16)
        ahead += jnp.dot(
            moved_ext[pl.ds(tap * PIX, ROWS), :], weight, preferred_element_type=F32
        )
        back += lax.dot_general(
            cot_ext[pl.ds((2 - tap) * PIX, ROWS), :],
            weight,
            (((1,), (1,)), ((), ())),
            preferred_element_type=F32,
        )
    mixed[...] = ahead
    slope = slope_of(spatial_out[...].astype(F32))
    cot = cot_ext[pl.ds(PIX, ROWS), :].astype(F32)
    back_spatial[...] = (cot + back * slope).astype(BF16)


def temporal(place, cot_ext, moved_ext, spatial_out, pieces):
    return pl.pallas_call(
        temporal_kernel,
        out_shape=(jax.ShapeDtypeStruct((ROWS, C), F32), jax.ShapeDtypeStruct((ROWS, C), BF16)),
        in_specs=SMEM_SPEC + vmem_specs(3) + any_specs(8),
        out_specs=tuple(vmem_specs(2)),
        scratch_shapes=[
            pltpu.VMEM((NY, NC, NZH, TPAD, C), BF16),
            pltpu.VMEM((3 * C + 8, C), F32),
            pltpu.SemaphoreType.DMA((32,)),
        ],
        compiler_params=pltpu.CompilerParams(vmem_limit_bytes=VLIM),
        cost_estimate=cost(12 * ROWS * C * C, 8_000_000),
        name="temporal_both",
    )(place, cot_ext, moved_ext, spatial_out, *pieces)


def backward_kernel(place, back_spatial, normed, scale, inv_std, *rest):
    pieces, (latent_grad, whole, wide, sums, sems) = rest[:8], rest[8:]
    copies = load_copies(place, pieces, whole, sems, SQ, 0)
    for copy in copies:
        copy.start()
    for copy in copies:
        copy.wait()
    for block in range(32):
        pair, core = divmod(block, 2)
        wide[pl.ds(block * SROWS, SPAD), :] = whole[pair // 4, core, pair % 4].astype(F32)
    sums[...] = jnp.zeros_like(sums)
    for tap in range(9):
        dy, dx = divmod(tap, 3)
        product = lax.dot_general(
            back_spatial[...],
            wide[pl.ds(tap * C, C), :].astype(BF16),
            (((1,), (1,)), ((), ())),
            preferred_element_type=F32,
        )
        for frame in range(2):
            base = frame * PIX
            to = base + max(dy - 1, 0) * WD
            at = max(1 - dy, 0) * WD
            count = PIX - abs(dy - 1) * WD
            sums[dx, pl.ds(to, count), :] += product[base + at : base + at + count, :]
    column = lax.rem(lax.broadcasted_iota(jnp.int32, (PIX, C), 0), WD)
    group_r = lax.broadcasted_iota(jnp.int32, (C, C), 0) // GROUP_CH
    group_c = lax.broadcasted_iota(jnp.int32, (C, C), 1) // GROUP_CH
    spread = jnp.where(group_r == group_c, 1.0 / (PIX * GROUP_CH), 0.0).astype(F32)
    for frame in range(2):
        rows = pl.ds(frame * PIX, PIX)
        left = pltpu.roll(sums[0, rows, :], PIX - 1, 0)
        right = pltpu.roll(sums[2, rows, :], 1, 0)
        back_act = (
            sums[1, rows, :]
            + jnp.where(column < WD - 1, left, 0.0)
            + jnp.where(column > 0, right, 0.0)
        )
        back_normed = back_act * scale[rows, :]
        unit = normed[rows, :]
        first = jnp.sum(back_normed, axis=0, keepdims=True)
        second = jnp.sum(back_normed * unit, axis=0, keepdims=True)
        both = jnp.concatenate([first, second, jnp.zeros((6, C), F32)], axis=0)
        means = jnp.dot(
            both, spread, precision=lax.Precision.HIGHEST, preferred_element_type=F32
        )
        latent_grad[rows, :] = inv_std[pl.ds(frame, 1), :] * (
            back_normed - means[0:1] - unit * means[1:2]
        )


def backward(place, back_spatial, normed, scale, inv_std, pieces):
    return pl.pallas_call(
        backward_kernel,
        out_shape=jax.ShapeDtypeStruct((ROWS, C), F32),
        in_specs=SMEM_SPEC + vmem_specs(4) + any_specs(8),
        out_specs=vmem_specs(1)[0],
        scratch_shapes=[
            pltpu.VMEM((NY, NC, NZH, SPAD, C), BF16),
            pltpu.VMEM((9 * C + 16, C), F32),
            pltpu.VMEM((3, ROWS, C), F32),
            pltpu.SemaphoreType.DMA((32,)),
        ],
        compiler_params=pltpu.CompilerParams(vmem_limit_bytes=VLIM),
        cost_estimate=cost(18 * ROWS * C * C, 12_000_000),
        name="spatial_backward",
    )(place, back_spatial, normed, scale, inv_std, *pieces)


def halo_ext(own):
    size = NX * NZL
    before = lax.ppermute(own[1], "frames", [(k, k + 1) for k in range(size - 1)])
    after = lax.ppermute(own[0], "frames", [(k + 1, k) for k in range(size - 1)])
    return jnp.concatenate([before[None], own, after[None]]).reshape(4 * PIX, C)


def gather_weights(place_x, spatial_weight, temporal_weight):
    x = place_x
    spatial = jnp.pad(spatial_weight, ((0, SPAD - SROWS), (0, 0)))
    temporal_rows = jnp.pad(temporal_weight, ((0, TPAD - TROWS), (0, 0)))
    quarter = jnp.concatenate(
        [
            lax.dynamic_slice_in_dim(spatial, x * SQ, SQ, 0),
            lax.dynamic_slice_in_dim(temporal_rows, x * TQ, TQ, 0),
        ]
    )
    return quarter


def per_device(
    latents,
    pose,
    timesteps,
    norm_gain,
    norm_bias,
    pose_table,
    time_weight,
    spatial_weight,
    temporal_weight,
    cotangent,
):
    frame_at = lax.axis_index("frames")
    row_at = lax.axis_index("dp")
    x = frame_at % NX
    y = row_at // (NZH * NC)
    zh = (row_at // NC) % NZH
    core = row_at % NC
    place = jnp.stack([x, y, zh, core]).astype(jnp.int32)

    quarter = gather_weights(x, spatial_weight, temporal_weight)
    came = [send(quarter, zh_step(k)) for k in (1, 2, 3)]
    column = in_order(quarter, came, zh)
    came = [send(column, xy_step(k)) for k in (1, 2, 3)]
    plane = jnp.stack([column] + came)
    came = [send(plane, yx_step(k)) for k in (1, 2, 3)]
    owned_pieces = [plane] + came
    pieces = owned_pieces + [send(piece, core_swap) for piece in owned_pieces]

    cot_ext = halo_ext(cotangent[0])

    _, frames_dev, pixels, chans = latents.shape
    groups = chans // GROUP_CH
    entries = float(pixels * GROUP_CH)
    factor = 1.0 / math.sqrt(lax.axis_size("dp") * frames_dev * lax.axis_size("frames") * pixels)
    shifted = latents[0].astype(F32) + pose_rows(pose[0], pose_table)
    sum_c = jnp.sum(shifted, axis=1).reshape(frames_dev, groups, GROUP_CH)
    square_c = jnp.sum(shifted * shifted, axis=1).reshape(frames_dev, groups, GROUP_CH)
    center = jnp.sum(sum_c, axis=2) / entries
    variance = jnp.sum(square_c, axis=2) / entries - center * center
    inv_std = jnp.repeat(lax.rsqrt(variance + 1e-05), GROUP_CH, axis=1)
    center = jnp.repeat(center, GROUP_CH, axis=1)
    normed = (shifted - center[:, None, :]) * inv_std[:, None, :]
    before = normed * norm_gain + norm_bias
    activated = jax.nn.silu(before).astype(BF16)
    scale = silu_slope(before) * norm_gain
    cols = spatial_cols(activated.reshape(frames_dev, HT, WD, chans), 1)
    cols = jnp.pad(cols.reshape(ROWS, 32, SROWS), ((0, 0), (0, 0), (0, SPAD - SROWS)))
    cols = cols.reshape(ROWS, NY, NZH, NC, SPAD).transpose(1, 3, 0, 2, 4)
    cols = cols.reshape(NY, NC, ROWS, NZH * SPAD)
    shift = time_shift(timesteps, time_weight)

    spatial_out, moved = forward(place, cols, shift, pieces)
    moved_ext = halo_ext(moved.reshape(2, PIX, C))

    mine, other = grad_terms(place, moved, cot_ext)
    came = send(other, core_swap)
    held, *parts = split_first(place, mine, came)
    came = [send(part, yx_step(k + 1)) for k, part in enumerate(parts)]
    held, *parts = split_second(place, held, came)
    came = [send(part, xy_step(k + 1)) for k, part in enumerate(parts)]
    held, *parts = split_third(place, held, came)
    came = [send(part, zh_step(k + 1)) for k, part in enumerate(parts)]
    held = held + came[0] + came[1] + came[2]
    held = (held + send(held, zl_swap)) * factor
    came = [send(held, x_step(k)) for k in (1, 2, 3)]
    temporal_grad = in_order(held, came, x).reshape(TPAD, C)[:TROWS]

    mixed, back_spatial = temporal(place, cot_ext, moved_ext, spatial_out, pieces)
    latent_grad = backward(
        place, back_spatial, normed.reshape(ROWS, C), scale.reshape(ROWS, C), inv_std, pieces
    )
    shape = latents.shape
    return mixed.reshape(shape), latent_grad.reshape(shape), temporal_grad


def solution(mesh):
    placed = (
        P("dp", "frames", None, None),
        P("dp", "frames", None),
        P("dp"),
        P(),
        P(),
        P(),
        P(),
        P("dp", None),
        P("dp", None),
        P("dp", "frames", None, None),
    )
    return jax.shard_map(
        per_device,
        mesh=mesh,
        in_specs=placed,
        out_specs=(P("dp", "frames", None, None), P("dp", "frames", None, None), P("dp", None)),
        check_vma=False,
    )
```

```python
import math

import jax
import jax.numpy as jnp
from jax import lax
from jax.experimental import pallas as pl
from jax.experimental.pallas import tpu as pltpu
from jax.sharding import PartitionSpec as P

GROUP_CH = 40
HT = 9
WD = 16
PIX = HT * WD
C = 640
NX, NY, NZH, NZL, NC = 4, 4, 4, 2, 2
AXES = ("frames", "dp")
SROWS, SPAD, SQ = 180, 192, 48
TROWS, TPAD, TQ = 60, 64, 16
QROWS = SQ + TQ
ROWS = 2 * PIX
F32 = jnp.float32
BF16 = jnp.bfloat16
VLIM = 58 * 1024 * 1024


def coords():
    for zl in range(NZL):
        for x in range(NX):
            for y in range(NY):
                for zh in range(NZH):
                    for c in range(NC):
                        yield zl, x, y, zh, c


def index_of(zl, x, y, zh, c):
    return (zl * NX + x) * (NY * NZH * NC) + (y * NZH + zh) * NC + c


def routes(move):
    return [(index_of(*at), index_of(*move(*at))) for at in coords()]


def send(value, move):
    return lax.ppermute(value, AXES, routes(move))


def core_swap(zl, x, y, zh, c):
    return zl, x, y, zh, 1 - c


def zl_swap(zl, x, y, zh, c):
    return 1 - zl, x, y, zh, c


def zh_step(k):
    return lambda zl, x, y, zh, c: (zl, x, y, (zh + k) % NZH, c)


def x_step(k):
    return lambda zl, x, y, zh, c: (zl, (x + k) % NX, y, zh, c)


def xy_step(k):
    return lambda zl, x, y, zh, c: (
        (zl, (x + k) % NX, y, zh, c) if c == 0 else (zl, x, (y + k) % NY, zh, c)
    )


def yx_step(k):
    return lambda zl, x, y, zh, c: (
        (zl, x, (y + k) % NY, zh, c) if c == 0 else (zl, (x + k) % NX, y, zh, c)
    )


def in_order(own, received, place):
    parts = [received[2], received[1], received[0], own]
    stacked = jnp.stack(parts + parts)
    return lax.dynamic_slice_in_dim(stacked, (3 - place) % 4, 4, axis=0)


def time_shift(timesteps, time_weight):
    half = time_weight.shape[0] // 2
    positions = jnp.arange(half, dtype=jnp.float32)
    frequencies = jnp.exp(-math.log(10000.0) * positions / half)
    angles = timesteps.astype(jnp.float32)[:, None] * frequencies[None, :]
    embedding = jnp.concatenate([jnp.cos(angles), jnp.sin(angles)], axis=-1)
    return jnp.dot(embedding, time_weight, precision=lax.Precision.HIGHEST)


def piece_of(pieces, own, far, near):
    base = own * 5
    if far == 2:
        return pieces[base + 2 + near // 2], near % 2
    return pieces[base + (0, 1, None, 4)[far]], near


def origin(place, own, far, near):
    x, y, core = place[0], place[1], place[3]
    flow = core if own == 0 else 1 - core
    from_y = lax.rem(y + 4 - jnp.where(flow == 0, far, near), 4)
    from_x = lax.rem(x + 4 - jnp.where(flow == 0, near, far), 4)
    return from_y, flow, from_x


def load_copies(place, pieces, whole, sems, rows, offset):
    copies = []
    for own in (0, 1):
        for far in range(4):
            for near in range(4):
                from_y, flow, from_x = origin(place, own, far, near)
                piece, slot = piece_of(pieces, own, far, near)
                copies.append(
                    pltpu.make_async_copy(
                        piece.at[slot, :, pl.ds(offset, rows), :],
                        whole.at[from_y, flow, :, pl.ds(pl.multiple_of(from_x * rows, rows), rows), :],
                        sems.at[len(copies)],
                    )
                )
    return copies


def conv_parts(cols, pieces, layout, scratch, sems):
    copies = []
    for k, (own, far, half) in enumerate(layout):
        lanes = pl.ds(0, 1024) if half is None else pl.ds(half * 512, 512)
        copies.append(
            (
                pltpu.make_async_copy(pieces[k], scratch[2 * k], sems.at[2 * k]),
                pltpu.make_async_copy(
                    cols.at[own, far, :, lanes], scratch[2 * k + 1], sems.at[2 * k + 1]
                ),
            )
        )
    for pair in copies:
        for copy in pair:
            copy.start()
    for k, pair in enumerate(copies):
        for copy in pair:
            copy.wait()
        rows = scratch[2 * k][...].reshape(-1, C)
        yield jnp.dot(scratch[2 * k + 1][...], rows, preferred_element_type=F32)


FIRST_PART = ((0, 0, None), (0, 1, None), (0, 3, None), (1, 0, None))
SECOND_PART = ((1, 1, None), (1, 3, None), (0, 2, 0), (0, 2, 1), (1, 2, 0), (1, 2, 1))


def forward_first_kernel(shift, cols, *rest):
    count = len(FIRST_PART)
    pieces, total, sems, scratch = rest[:count], rest[count], rest[count + 1], rest[count + 2 :]
    for k, product in enumerate(conv_parts(cols, pieces, FIRST_PART, scratch, sems)):
        if k == 0:
            total[...] = product + shift[...]
        else:
            total[...] += product


def forward_second_kernel(start, cols, *rest):
    count = len(SECOND_PART)
    pieces, (spatial_out, moved, total, sems) = rest[:count], rest[count : count + 4]
    scratch = rest[count + 4 :]
    for k, product in enumerate(conv_parts(cols, pieces, SECOND_PART, scratch, sems)):
        if k == 0:
            total[...] = product + start[...]
        else:
            total[...] += product
    rounded = total[...].astype(BF16)
    spatial_out[...] = rounded
    wide = rounded.astype(F32)
    moved[...] = (wide * jax.nn.sigmoid(wide)).astype(BF16)


def any_specs(count):
    return [pl.BlockSpec(memory_space=pl.ANY)] * count


def vmem_specs(count):
    return [pl.BlockSpec(memory_space=pltpu.VMEM)] * count


SMEM_SPEC = [pl.BlockSpec(memory_space=pltpu.SMEM)]


def cost(flops, moved):
    return pl.CostEstimate(flops=flops, bytes_accessed=moved, transcendentals=0)


def group_spread():
    group_r = lax.broadcasted_iota(jnp.int32, (C, C), 0) // GROUP_CH
    group_c = lax.broadcasted_iota(jnp.int32, (C, C), 1) // GROUP_CH
    return jnp.where(group_r == group_c, 1.0 / (PIX * GROUP_CH), 0.0).astype(F32)


def group_means(first, second, spread):
    both = jnp.concatenate([first, second, jnp.zeros((6, C), F32)], axis=0)
    return jnp.dot(both, spread, precision=lax.Precision.HIGHEST, preferred_element_type=F32)


def segments():
    found = {}
    for y in range(NY):
        for core in range(NC):
            for x in range(NX):
                parts = []
                for zh in range(NZH):
                    block = (y * NZH + zh) * NC + core
                    start = SROWS * block + SQ * x
                    end = min(start + SQ, SROWS * (block + 1))
                    lane = zh * QROWS
                    while start < end:
                        tap, channel = divmod(start, C)
                        count = min(end - start, C - channel)
                        parts.append((lane, tap, channel, count))
                        start += count
                        lane += count
                found[y, core, x] = parts
    return found


def before_kernel(place, latents, pose, table, gain, bias, cols, normed, scale, inv_std, padded, chunk):
    at_x, at_y, core = place[0], place[1], place[3]
    kinds = lax.broadcasted_iota(jnp.int32, (table.shape[0], PIX), 0)
    gains = gain[...].reshape(1, C)
    biases = bias[...].reshape(1, C)
    column = lax.rem(lax.broadcasted_iota(jnp.int32, (PIX, C), 0), WD)
    spread = group_spread()
    for frame in range(2):
        rows = pl.ds(frame * PIX, PIX)
        onehot = (pose[pl.ds(frame, 1), :] == kinds).astype(F32)
        shifted = latents[rows, :].astype(F32) + lax.dot_general(
            onehot,
            table[...],
            (((0,), (0,)), ((), ())),
            precision=lax.Precision.HIGHEST,
            preferred_element_type=F32,
        )
        means = group_means(
            jnp.sum(shifted, axis=0, keepdims=True),
            jnp.sum(shifted * shifted, axis=0, keepdims=True),
            spread,
        )
        center = means[0:1]
        inverse = lax.rsqrt(means[1:2] - center * center + 1e-05)
        inv_std[pl.ds(frame, 1), :] = inverse
        unit = (shifted - center) * inverse
        normed[rows, :] = unit
        value = unit * gains + biases
        gate = jax.nn.sigmoid(value)
        scale[rows, :] = gate * (1.0 + value * (1.0 - gate)) * gains
        active = value * gate
        for dx in range(3):
            if dx == 0:
                moved = jnp.where(column > 0, pltpu.roll(active, 1, 0), 0.0)
            elif dx == 1:
                moved = active
            else:
                moved = jnp.where(column < WD - 1, pltpu.roll(active, PIX - 1, 0), 0.0)
            padded[dx, frame, pl.ds(0, WD), :] = jnp.zeros((WD, C), BF16)
            padded[dx, frame, pl.ds(WD, PIX), :] = moved.astype(BF16)
            padded[dx, frame, pl.ds(WD + PIX, WD), :] = jnp.zeros((WD, C), BF16)
    chunk[...] = jnp.zeros_like(chunk)
    for number, ((y, flow, x), parts) in enumerate(segments().items()):
        slot = number % 2
        if x == NX - 1:
            chunk[slot] = jnp.zeros((ROWS, NZH * QROWS), BF16)
        for lane, tap, channel, count in parts:
            dy, dx = divmod(tap, 3)
            for frame in range(2):
                chunk[slot, frame * PIX : (frame + 1) * PIX, lane : lane + count] = padded[
                    dx, frame, dy * WD : dy * WD + PIX, channel : channel + count
                ]
        far_y, far_x = lax.rem(at_y + 4 - y, 4), lax.rem(at_x + 4 - x, 4)
        far, near = (far_y, far_x) if flow == 0 else (far_x, far_y)
        own = jnp.where(core == flow, 0, 1)
        cols[own, far, :, pl.ds(pl.multiple_of(near * 256, 256), 256)] = chunk[slot]


def prepare(place, latents, pose, table, gain, bias):
    return pl.pallas_call(
        before_kernel,
        out_shape=(
            jax.ShapeDtypeStruct((NC, 4, ROWS, 4 * NZH * QROWS), BF16),
            jax.ShapeDtypeStruct((ROWS, C), F32),
            jax.ShapeDtypeStruct((ROWS, C), F32),
            jax.ShapeDtypeStruct((2, C), F32),
        ),
        in_specs=SMEM_SPEC + vmem_specs(5),
        out_specs=tuple(vmem_specs(4)),
        scratch_shapes=[
            pltpu.VMEM((3, 2, PIX + 2 * WD, C), BF16),
            pltpu.VMEM((2, ROWS, NZH * QROWS), BF16),
        ],
        compiler_params=pltpu.CompilerParams(vmem_limit_bytes=VLIM),
        cost_estimate=cost(2_000_000_000, 8_000_000),
        name="norm_and_columns",
    )(place, latents, pose, table, gain, bias)


def conv_scratch(pieces):
    shapes = [pltpu.SemaphoreType.DMA((2 * len(pieces),))]
    for piece in pieces:
        shapes.append(pltpu.VMEM(piece.shape, BF16))
        shapes.append(pltpu.VMEM((ROWS, 256 * piece.shape[0]), BF16))
    return shapes


def forward_first(shift, cols, pieces):
    return pl.pallas_call(
        forward_first_kernel,
        out_shape=jax.ShapeDtypeStruct((ROWS, C), F32),
        in_specs=vmem_specs(1) + any_specs(1 + len(pieces)),
        out_specs=vmem_specs(1)[0],
        scratch_shapes=conv_scratch(pieces),
        compiler_params=pltpu.CompilerParams(vmem_limit_bytes=VLIM),
        cost_estimate=cost(2 * ROWS * 4096 * C, 8_000_000),
        name="spatial_forward_first",
    )(shift, cols, *pieces)


def forward_second(start, cols, pieces):
    return pl.pallas_call(
        forward_second_kernel,
        out_shape=(jax.ShapeDtypeStruct((ROWS, C), BF16),) * 2,
        in_specs=vmem_specs(1) + any_specs(1 + len(pieces)),
        out_specs=tuple(vmem_specs(2)),
        scratch_shapes=[pltpu.VMEM((ROWS, C), F32)] + conv_scratch(pieces),
        compiler_params=pltpu.CompilerParams(vmem_limit_bytes=VLIM),
        cost_estimate=cost(2 * ROWS * 4096 * C, 8_000_000),
        name="spatial_forward_second",
    )(start, cols, *pieces)


def grad_kernel(place, moved, cot_ext, mine, other, total):
    core = place[3]
    right = jnp.concatenate([cot_ext[pl.ds((2 - tap) * PIX, ROWS), :] for tap in range(3)], axis=1)
    product = lax.dot_general(
        moved[...], right, (((0,), (0,)), ((), ())), preferred_element_type=F32
    )
    for tap in range(3):
        total[pl.ds(tap * C, C), :] = product[:, tap * C : (tap + 1) * C]
    total[pl.ds(3 * C, 8), :] = jnp.zeros((8, C), F32)
    for block in range(32):
        spot = block // 2
        rows = total[pl.ds(block * TROWS, TPAD), :]

        @pl.when(core == block % 2)
        def _():
            mine[spot // 4, spot % 4] = rows.astype(BF16)

        @pl.when(core != block % 2)
        def _():
            other[spot // 4, spot % 4] = rows.astype(BF16)


def grad_terms(place, moved, cot_ext):
    shape = (NY, NZH, TPAD, C)
    return pl.pallas_call(
        grad_kernel,
        out_shape=(jax.ShapeDtypeStruct(shape, BF16),) * 2,
        in_specs=SMEM_SPEC + vmem_specs(2),
        out_specs=tuple(vmem_specs(2)),
        scratch_shapes=[pltpu.VMEM((3 * C + 8, C), F32)],
        compiler_params=pltpu.CompilerParams(vmem_limit_bytes=VLIM),
        cost_estimate=cost(2 * ROWS * 3 * C * C, 5_000_000),
        name="temporal_grad_terms",
    )(place, moved, cot_ext)


def split_first_kernel(place, mine, came, own, *sends):
    x, y, core = place[0], place[1], place[3]

    @pl.when(core == 0)
    def _():
        for k in range(4):
            part = lax.rem(y + k, 4)
            value = (mine[part].astype(F32) + came[part].astype(F32)).reshape(4 * TPAD, C)
            if k == 0:
                own[...] = value
            else:
                sends[k - 1][...] = value.astype(BF16)

    @pl.when(core != 0)
    def _():
        for k in range(4):
            rows = pl.ds(pl.multiple_of(lax.rem(x + k, 4) * TQ, TQ), TQ)
            value = (mine[:, :, rows, :].astype(F32) + came[:, :, rows, :].astype(F32)).reshape(16 * TQ, C)
            if k == 0:
                own[...] = value
            else:
                sends[k - 1][...] = value.astype(BF16)


def split_first(place, mine, came):
    shape = (4 * TPAD, C)
    return pl.pallas_call(
        split_first_kernel,
        out_shape=(jax.ShapeDtypeStruct(shape, F32),) + (jax.ShapeDtypeStruct(shape, BF16),) * 3,
        in_specs=SMEM_SPEC + vmem_specs(2),
        out_specs=tuple(vmem_specs(4)),
        compiler_params=pltpu.CompilerParams(vmem_limit_bytes=VLIM),
        cost_estimate=cost(0, 4_000_000),
        name="grad_split_first",
    )(place, mine, came)


def split_second_kernel(place, held, first, second, third, own, *sends):
    x, y, core = place[0], place[1], place[3]
    own_sends = (own,) + tuple(sends)

    @pl.when(core == 0)
    def _():
        for k in range(4):
            for zh in range(NZH):
                start = zh * TPAD + lax.rem(x + k, 4) * TQ
                rows = pl.ds(pl.multiple_of(start, TQ), TQ)
                value = held[rows, :]
                for term in (first, second, third):
                    value += term[rows, :].astype(F32)
                own_sends[k][zh] = value

    @pl.when(core != 0)
    def _():
        for k in range(4):
            rows = pl.ds(pl.multiple_of(lax.rem(y + k, 4) * TPAD, TPAD), TPAD)
            value = held[rows, :]
            for term in (first, second, third):
                value += term[rows, :].astype(F32)
            own_sends[k][...] = value.reshape(NZH, TQ, C)


def split_second(place, held, terms):
    shape = (NZH, TQ, C)
    return pl.pallas_call(
        split_second_kernel,
        out_shape=(jax.ShapeDtypeStruct(shape, F32),) * 4,
        in_specs=SMEM_SPEC + vmem_specs(4),
        out_specs=tuple(vmem_specs(4)),
        compiler_params=pltpu.CompilerParams(vmem_limit_bytes=VLIM),
        cost_estimate=cost(0, 2_000_000),
        name="grad_split_second",
    )(place, held, *terms)


def split_third_kernel(place, held, first, second, third, *parts):
    zh = place[2]
    for k in range(4):
        part = lax.rem(zh + k, 4)
        parts[k][...] = held[part] + first[part] + second[part] + third[part]


def split_third(place, held, terms):
    return pl.pallas_call(
        split_third_kernel,
        out_shape=(jax.ShapeDtypeStruct((TQ, C), F32),) * 4,
        in_specs=SMEM_SPEC + vmem_specs(4),
        out_specs=tuple(vmem_specs(4)),
        cost_estimate=cost(0, 800_000),
        name="grad_split_third",
    )(place, held, *terms)


def slope_of(value):
    gate = jax.nn.sigmoid(value)
    return gate * (1.0 + value * (1.0 - gate))


def temporal_kernel(place, cot_ext, moved_ext, spatial_out, *rest):
    pieces, (mixed, back_spatial, whole, wide, sems) = rest[:10], rest[10:]
    copies = load_copies(place, pieces, whole, sems, TQ, SQ)
    for copy in copies:
        copy.start()
    for copy in copies:
        copy.wait()
    for block in range(32):
        pair, core = divmod(block, 2)
        wide[pl.ds(block * TROWS, TPAD), :] = whole[pair // 4, core, pair % 4].astype(F32)
    ahead = spatial_out[...].astype(F32)
    back = jnp.zeros((ROWS, C), F32)
    for tap in range(3):
        weight = wide[pl.ds(tap * C, C), :].astype(BF16)
        ahead += jnp.dot(
            moved_ext[pl.ds(tap * PIX, ROWS), :], weight, preferred_element_type=F32
        )
        back += lax.dot_general(
            cot_ext[pl.ds((2 - tap) * PIX, ROWS), :],
            weight,
            (((1,), (1,)), ((), ())),
            preferred_element_type=F32,
        )
    mixed[...] = ahead
    slope = slope_of(spatial_out[...].astype(F32))
    cot = cot_ext[pl.ds(PIX, ROWS), :].astype(F32)
    back_spatial[...] = (cot + back * slope).astype(BF16)


def temporal(place, cot_ext, moved_ext, spatial_out, pieces):
    return pl.pallas_call(
        temporal_kernel,
        out_shape=(jax.ShapeDtypeStruct((ROWS, C), F32), jax.ShapeDtypeStruct((ROWS, C), BF16)),
        in_specs=SMEM_SPEC + vmem_specs(3) + any_specs(10),
        out_specs=tuple(vmem_specs(2)),
        scratch_shapes=[
            pltpu.VMEM((NY, NC, NZH, TPAD, C), BF16),
            pltpu.VMEM((3 * C + 8, C), F32),
            pltpu.SemaphoreType.DMA((32,)),
        ],
        compiler_params=pltpu.CompilerParams(vmem_limit_bytes=VLIM),
        cost_estimate=cost(12 * ROWS * C * C, 8_000_000),
        name="temporal_both",
    )(place, cot_ext, moved_ext, spatial_out, *pieces)


def tap_range(first, last):
    return first * C // SROWS, -(-last * C // SROWS)


def add_taps(first, last, place, back_spatial, pieces, sums, whole, wide, sems):
    copies = load_copies(place, pieces, whole, sems, SQ, 0)
    for copy in copies:
        copy.start()
    for copy in copies:
        copy.wait()
    low, high = tap_range(first, last)
    for block in range(low, high):
        pair, core = divmod(block, 2)
        wide[pl.ds((block - low) * SROWS, SPAD), :] = whole[pair // 4, core, pair % 4].astype(F32)
    for tap in range(first, last):
        dy, dx = divmod(tap, 3)
        product = lax.dot_general(
            back_spatial[...],
            wide[pl.ds(tap * C - low * SROWS, C), :].astype(BF16),
            (((1,), (1,)), ((), ())),
            preferred_element_type=F32,
        )
        for frame in range(2):
            base = frame * PIX
            to = base + max(dy - 1, 0) * WD
            at = base + max(1 - dy, 0) * WD
            count = PIX - abs(dy - 1) * WD
            sums[dx, pl.ds(to, count), :] += product[at : at + count, :]


TAPS_FIRST = 4


def backward_first_kernel(place, back_spatial, *rest):
    pieces, (sums, whole, wide, sems) = rest[:10], rest[10:]
    sums[...] = jnp.zeros_like(sums)
    add_taps(0, TAPS_FIRST, place, back_spatial, pieces, sums, whole, wide, sems)


def backward_second_kernel(place, back_spatial, start, normed, scale, inv_std, *rest):
    pieces, (latent_grad, sums, whole, wide, sems) = rest[:10], rest[10:]
    sums[...] = start[...]
    add_taps(TAPS_FIRST, 9, place, back_spatial, pieces, sums, whole, wide, sems)
    column = lax.rem(lax.broadcasted_iota(jnp.int32, (PIX, C), 0), WD)
    spread = group_spread()
    for frame in range(2):
        rows = pl.ds(frame * PIX, PIX)
        left = pltpu.roll(sums[0, rows, :], PIX - 1, 0)
        right = pltpu.roll(sums[2, rows, :], 1, 0)
        back_act = (
            sums[1, rows, :]
            + jnp.where(column < WD - 1, left, 0.0)
            + jnp.where(column > 0, right, 0.0)
        )
        back_normed = back_act * scale[rows, :]
        unit = normed[rows, :]
        first = jnp.sum(back_normed, axis=0, keepdims=True)
        second = jnp.sum(back_normed * unit, axis=0, keepdims=True)
        means = group_means(first, second, spread)
        latent_grad[rows, :] = inv_std[pl.ds(frame, 1), :] * (
            back_normed - means[0:1] - unit * means[1:2]
        )


def tap_scratch(first, last):
    low, high = tap_range(first, last)
    return [
        pltpu.VMEM((NY, NC, NZH, SPAD, C), BF16),
        pltpu.VMEM(((high - low) * SROWS + 20, C), F32),
        pltpu.SemaphoreType.DMA((32,)),
    ]


def backward_first(place, back_spatial, pieces):
    return pl.pallas_call(
        backward_first_kernel,
        out_shape=jax.ShapeDtypeStruct((3, ROWS, C), F32),
        in_specs=SMEM_SPEC + vmem_specs(1) + any_specs(10),
        out_specs=vmem_specs(1)[0],
        scratch_shapes=tap_scratch(0, TAPS_FIRST),
        compiler_params=pltpu.CompilerParams(vmem_limit_bytes=VLIM),
        cost_estimate=cost(2 * TAPS_FIRST * ROWS * C * C, 8_000_000),
        name="spatial_backward_first",
    )(place, back_spatial, *pieces)


def backward_second(place, back_spatial, start, normed, scale, inv_std, pieces):
    return pl.pallas_call(
        backward_second_kernel,
        out_shape=jax.ShapeDtypeStruct((ROWS, C), F32),
        in_specs=SMEM_SPEC + vmem_specs(5) + any_specs(10),
        out_specs=vmem_specs(1)[0],
        scratch_shapes=[pltpu.VMEM((3, ROWS, C), F32)] + tap_scratch(TAPS_FIRST, 9),
        compiler_params=pltpu.CompilerParams(vmem_limit_bytes=VLIM),
        cost_estimate=cost(2 * (9 - TAPS_FIRST) * ROWS * C * C, 8_000_000),
        name="spatial_backward_second",
    )(place, back_spatial, start, normed, scale, inv_std, *pieces)


def halo_ext(own):
    size = NX * NZL
    before = lax.ppermute(own[1], "frames", [(k, (k + 1) % size) for k in range(size)])
    after = lax.ppermute(own[0], "frames", [((k + 1) % size, k) for k in range(size)])
    at = lax.axis_index("frames")
    before = jnp.where(at > 0, before, 0)
    after = jnp.where(at < size - 1, after, 0)
    return jnp.concatenate([before[None], own, after[None]]).reshape(4 * PIX, C)


def gather_weights(place_x, spatial_weight, temporal_weight):
    x = place_x
    spatial = jnp.pad(spatial_weight, ((0, SPAD - SROWS), (0, 0)))
    temporal_rows = jnp.pad(temporal_weight, ((0, TPAD - TROWS), (0, 0)))
    quarter = jnp.concatenate(
        [
            lax.dynamic_slice_in_dim(spatial, x * SQ, SQ, 0),
            lax.dynamic_slice_in_dim(temporal_rows, x * TQ, TQ, 0),
        ]
    )
    return quarter


def per_device(
    latents,
    pose,
    timesteps,
    norm_gain,
    norm_bias,
    pose_table,
    time_weight,
    spatial_weight,
    temporal_weight,
    cotangent,
):
    frame_at = lax.axis_index("frames")
    row_at = lax.axis_index("dp")
    x = frame_at % NX
    y = row_at // (NZH * NC)
    zh = (row_at // NC) % NZH
    core = row_at % NC
    place = jnp.stack([x, y, zh, core]).astype(jnp.int32)

    quarter = gather_weights(x, spatial_weight, temporal_weight)
    came = [send(quarter, zh_step(k)) for k in (1, 2, 3)]
    column = in_order(quarter, came, zh)
    came = [send(column, xy_step(k)) for k in (1, 2, 3)]
    plane = jnp.stack([column] + came)
    one, three = send(plane, yx_step(1)), send(plane, yx_step(3))

    _, frames_dev, pixels, _ = latents.shape
    factor = 1.0 / math.sqrt(lax.axis_size("dp") * frames_dev * lax.axis_size("frames") * pixels)
    cols, normed, scale, inv_std = prepare(
        place, latents.reshape(ROWS, C), pose[0], pose_table, norm_gain, norm_bias
    )
    shift = time_shift(timesteps, time_weight)
    plane_swapped = send(plane, core_swap)
    one, three, cols, shift = lax.optimization_barrier((one, three, cols, shift))
    two_low, two_high = send(one[:2], yx_step(1)), send(three[2:], yx_step(3))
    cotangent, _ = lax.optimization_barrier((cotangent, one))
    cot_ext = halo_ext(cotangent[0])
    one_swapped, three_swapped = send(one, core_swap), send(three, core_swap)
    low_swapped, high_swapped = send(two_low, core_swap), send(two_high, core_swap)
    pieces = [plane, one, two_low, two_high, three]
    pieces += [plane_swapped, one_swapped, low_swapped, high_swapped, three_swapped]

    total = forward_first(shift, cols, [plane, one, three, plane_swapped])
    spatial_out, moved = forward_second(
        total, cols, [one_swapped, three_swapped, two_low, two_high, low_swapped, high_swapped]
    )

    mine, other = grad_terms(place, moved, cot_ext)
    moved_ext = halo_ext(moved.reshape(2, PIX, C))
    came = send(other, core_swap)
    held, *parts = split_first(place, mine, came)
    came = [send(part, yx_step(k + 1)) for k, part in enumerate(parts)]
    moved_ext, _ = lax.optimization_barrier((moved_ext, held))
    mixed, back_spatial = temporal(place, cot_ext, moved_ext, spatial_out, pieces)
    *came, back_spatial = lax.optimization_barrier((*came, back_spatial))

    held, *parts = split_second(place, held, came)
    came = [send(part, xy_step(k + 1)) for k, part in enumerate(parts)]
    ready, _ = lax.optimization_barrier((back_spatial, held))
    sums = backward_first(place, ready, pieces)
    *came, sums = lax.optimization_barrier((*came, sums))

    held, *parts = split_third(place, held, came)
    came = [send(part, zh_step(k + 1)) for k, part in enumerate(parts)]
    sums, _ = lax.optimization_barrier((sums, held))
    latent_grad = backward_second(place, ready, sums, normed, scale, inv_std, pieces)
    *came, latent_grad = lax.optimization_barrier((*came, latent_grad))

    held = held + came[0] + came[1] + came[2]
    held = (held + send(held, zl_swap)) * factor
    came = [send(held, x_step(k)) for k in (1, 2, 3)]
    temporal_grad = in_order(held, came, x).reshape(TPAD, C)[:TROWS]
    shape = latents.shape
    return mixed.reshape(shape), latent_grad.reshape(shape), temporal_grad


def solution(mesh):
    placed = (
        P("dp", "frames", None, None),
        P("dp", "frames", None),
        P("dp"),
        P(),
        P(),
        P(),
        P(),
        P("dp", None),
        P("dp", None),
        P("dp", "frames", None, None),
    )
    return jax.shard_map(
        per_device,
        mesh=mesh,
        in_specs=placed,
        out_specs=(P("dp", "frames", None, None), P("dp", "frames", None, None), P("dp", None)),
        check_vma=False,
    )
```

```python
import math

import jax
import jax.numpy as jnp
from jax import lax
from jax.experimental import pallas as pl
from jax.experimental.pallas import tpu as pltpu
from jax.sharding import PartitionSpec as P

GROUP_CH = 40
HT = 9
WD = 16
PIX = HT * WD
C = 640
NX, NY, NZH, NZL, NC = 4, 4, 4, 2, 2
AXES = ("frames", "dp")
SROWS, SPAD, SQ = 180, 192, 48
TROWS, TPAD, TQ = 60, 64, 16
QROWS = SQ + TQ
ROWS = 2 * PIX
F32 = jnp.float32
BF16 = jnp.bfloat16
VLIM = 58 * 1024 * 1024


def coords():
    for zl in range(NZL):
        for x in range(NX):
            for y in range(NY):
                for zh in range(NZH):
                    for c in range(NC):
                        yield zl, x, y, zh, c


def index_of(zl, x, y, zh, c):
    return (zl * NX + x) * (NY * NZH * NC) + (y * NZH + zh) * NC + c


def routes(move):
    return [(index_of(*at), index_of(*move(*at))) for at in coords()]


def send(value, move):
    return lax.ppermute(value, AXES, routes(move))


def core_swap(zl, x, y, zh, c):
    return zl, x, y, zh, 1 - c


def zl_swap(zl, x, y, zh, c):
    return 1 - zl, x, y, zh, c


def zh_step(k):
    return lambda zl, x, y, zh, c: (zl, x, y, (zh + k) % NZH, c)


def x_step(k):
    return lambda zl, x, y, zh, c: (zl, (x + k) % NX, y, zh, c)


def xy_step(k):
    return lambda zl, x, y, zh, c: (
        (zl, (x + k) % NX, y, zh, c) if c == 0 else (zl, x, (y + k) % NY, zh, c)
    )


def yx_step(k):
    return lambda zl, x, y, zh, c: (
        (zl, x, (y + k) % NY, zh, c) if c == 0 else (zl, (x + k) % NX, y, zh, c)
    )


def in_order(own, received, place):
    parts = [received[2], received[1], received[0], own]
    stacked = jnp.stack(parts + parts)
    return lax.dynamic_slice_in_dim(stacked, (3 - place) % 4, 4, axis=0)


def time_shift(timesteps, time_weight):
    half = time_weight.shape[0] // 2
    positions = jnp.arange(half, dtype=jnp.float32)
    frequencies = jnp.exp(-math.log(10000.0) * positions / half)
    angles = timesteps.astype(jnp.float32)[:, None] * frequencies[None, :]
    embedding = jnp.concatenate([jnp.cos(angles), jnp.sin(angles)], axis=-1)
    return jnp.dot(embedding, time_weight, precision=lax.Precision.HIGHEST)


def piece_of(pieces, own, far, near):
    return pieces[own * 8 + far * 2 + near // 2], near % 2


def origin(place, own, far, near):
    x, y, core = place[0], place[1], place[3]
    flow = core if own == 0 else 1 - core
    from_y = lax.rem(y + 4 - jnp.where(flow == 0, far, near), 4)
    from_x = lax.rem(x + 4 - jnp.where(flow == 0, near, far), 4)
    return from_y, flow, from_x


def load_copies(place, pieces, whole, sems, rows, offset):
    copies = []
    for own in (0, 1):
        for far in range(4):
            for near in range(4):
                from_y, flow, from_x = origin(place, own, far, near)
                piece, slot = piece_of(pieces, own, far, near)
                copies.append(
                    pltpu.make_async_copy(
                        piece.at[slot, :, pl.ds(offset, rows), :],
                        whole.at[from_y, flow, :, pl.ds(pl.multiple_of(from_x * rows, rows), rows), :],
                        sems.at[len(copies)],
                    )
                )
    return copies


def conv_parts(cols, pieces, layout, scratch, sems):
    copies = []
    for k, (own, far) in enumerate(layout):
        rows, columns = scratch[2 * k], scratch[2 * k + 1]
        copies.append(
            (
                pltpu.make_async_copy(pieces[2 * k], rows.at[pl.ds(0, 2)], sems.at[3 * k]),
                pltpu.make_async_copy(pieces[2 * k + 1], rows.at[pl.ds(2, 2)], sems.at[3 * k + 1]),
                pltpu.make_async_copy(cols.at[own, far], columns, sems.at[3 * k + 2]),
            )
        )
    for group in copies:
        for copy in group:
            copy.start()
    for k, group in enumerate(copies):
        for copy in group:
            copy.wait()
        rows = scratch[2 * k][...].reshape(4 * NZH * QROWS, C)
        yield jnp.dot(scratch[2 * k + 1][...], rows, preferred_element_type=F32)


FIRST_PART = ((0, 0), (0, 1), (0, 3), (1, 0))
MIDDLE_PART = ((1, 1), (1, 3), (0, 2))
LAST_PART = ((1, 2),)


def forward_first_kernel(shift, cols, *rest):
    pieces, total, sems, scratch = rest[:8], rest[8], rest[9], rest[10:]
    for k, product in enumerate(conv_parts(cols, pieces, FIRST_PART, scratch, sems)):
        if k == 0:
            total[...] = product + shift[...]
        else:
            total[...] += product


def forward_middle_kernel(start, cols, *rest):
    pieces, total, sems, scratch = rest[:6], rest[6], rest[7], rest[8:]
    for k, product in enumerate(conv_parts(cols, pieces, MIDDLE_PART, scratch, sems)):
        if k == 0:
            total[...] = product + start[...]
        else:
            total[...] += product


def forward_last_kernel(place, start, before, own, after, cols, *rest):
    pieces, (spatial_out, moved, mine, other, total, sems), scratch = rest[:2], rest[2:8], rest[8:]
    (product,) = conv_parts(cols, pieces, LAST_PART, scratch, sems)
    rounded = (product + start[...]).astype(BF16)
    spatial_out[...] = rounded
    wide = rounded.astype(F32)
    left = (wide * jax.nn.sigmoid(wide)).astype(BF16)
    moved[...] = left
    core = place[3]
    right = jnp.concatenate(
        [neighbour_rows(place, before, own, after, 2 - tap) for tap in range(3)], axis=1
    )
    product = lax.dot_general(left, right, (((0,), (0,)), ((), ())), preferred_element_type=F32)
    for tap in range(3):
        total[pl.ds(tap * C, C), :] = product[:, tap * C : (tap + 1) * C]
    total[pl.ds(3 * C, 8), :] = jnp.zeros((8, C), F32)
    for block in range(32):
        spot = block // 2
        rows = total[pl.ds(block * TROWS, TPAD), :].astype(BF16)

        @pl.when(core == block % 2)
        def _():
            mine[spot // 4, spot % 4] = rows

        @pl.when(core != block % 2)
        def _():
            other[spot // 4, spot % 4] = rows


def neighbour_rows(place, before, own, after, tap):
    if tap == 1:
        return own[...]
    if tap == 0:
        edge = jnp.where(place[4] > 0, before[...], jnp.zeros((PIX, C), BF16))
        return jnp.concatenate([edge, own[pl.ds(0, PIX), :]], axis=0)
    edge = jnp.where(place[5] > 0, after[...], jnp.zeros((PIX, C), BF16))
    return jnp.concatenate([own[pl.ds(PIX, PIX), :], edge], axis=0)


def any_specs(count):
    return [pl.BlockSpec(memory_space=pl.ANY)] * count


def vmem_specs(count):
    return [pl.BlockSpec(memory_space=pltpu.VMEM)] * count


SMEM_SPEC = [pl.BlockSpec(memory_space=pltpu.SMEM)]


def cost(flops, moved):
    return pl.CostEstimate(flops=flops, bytes_accessed=moved, transcendentals=0)


def group_spread():
    group_r = lax.broadcasted_iota(jnp.int32, (C, C), 0) // GROUP_CH
    group_c = lax.broadcasted_iota(jnp.int32, (C, C), 1) // GROUP_CH
    return jnp.where(group_r == group_c, 1.0 / (PIX * GROUP_CH), 0.0).astype(F32)


def group_means(first, second, spread):
    both = jnp.concatenate([first, second, jnp.zeros((6, C), F32)], axis=0)
    return jnp.dot(both, spread, precision=lax.Precision.HIGHEST, preferred_element_type=F32)


def segments():
    found = {}
    for y in range(NY):
        for core in range(NC):
            for x in range(NX):
                parts = []
                for zh in range(NZH):
                    block = (y * NZH + zh) * NC + core
                    start = SROWS * block + SQ * x
                    end = min(start + SQ, SROWS * (block + 1))
                    lane = zh * QROWS
                    while start < end:
                        tap, channel = divmod(start, C)
                        count = min(end - start, C - channel)
                        parts.append((lane, tap, channel, count))
                        start += count
                        lane += count
                found[y, core, x] = parts
    return found


def before_kernel(place, latents, pose, table, gain, bias, cols, normed, scale, inv_std, padded, chunk):
    at_x, at_y, core = place[0], place[1], place[3]
    kinds = lax.broadcasted_iota(jnp.int32, (table.shape[0], PIX), 0)
    gains = gain[...].reshape(1, C)
    biases = bias[...].reshape(1, C)
    column = lax.rem(lax.broadcasted_iota(jnp.int32, (PIX, C), 0), WD)
    spread = group_spread()
    for frame in range(2):
        rows = pl.ds(frame * PIX, PIX)
        onehot = (pose[pl.ds(frame, 1), :] == kinds).astype(F32)
        shifted = latents[rows, :].astype(F32) + lax.dot_general(
            onehot,
            table[...],
            (((0,), (0,)), ((), ())),
            precision=lax.Precision.HIGHEST,
            preferred_element_type=F32,
        )
        means = group_means(
            jnp.sum(shifted, axis=0, keepdims=True),
            jnp.sum(shifted * shifted, axis=0, keepdims=True),
            spread,
        )
        center = means[0:1]
        inverse = lax.rsqrt(means[1:2] - center * center + 1e-05)
        inv_std[pl.ds(frame, 1), :] = inverse
        unit = (shifted - center) * inverse
        normed[rows, :] = unit
        value = unit * gains + biases
        gate = jax.nn.sigmoid(value)
        scale[rows, :] = gate * (1.0 + value * (1.0 - gate)) * gains
        active = value * gate
        for dx in range(3):
            if dx == 0:
                moved = jnp.where(column > 0, pltpu.roll(active, 1, 0), 0.0)
            elif dx == 1:
                moved = active
            else:
                moved = jnp.where(column < WD - 1, pltpu.roll(active, PIX - 1, 0), 0.0)
            padded[dx, frame, pl.ds(0, WD), :] = jnp.zeros((WD, C), BF16)
            padded[dx, frame, pl.ds(WD, PIX), :] = moved.astype(BF16)
            padded[dx, frame, pl.ds(WD + PIX, WD), :] = jnp.zeros((WD, C), BF16)
    chunk[...] = jnp.zeros_like(chunk)
    for number, ((y, flow, x), parts) in enumerate(segments().items()):
        slot = number % 2
        if x == NX - 1:
            chunk[slot] = jnp.zeros((ROWS, NZH * QROWS), BF16)
        for lane, tap, channel, count in parts:
            dy, dx = divmod(tap, 3)
            for frame in range(2):
                chunk[slot, frame * PIX : (frame + 1) * PIX, lane : lane + count] = padded[
                    dx, frame, dy * WD : dy * WD + PIX, channel : channel + count
                ]
        far_y, far_x = lax.rem(at_y + 4 - y, 4), lax.rem(at_x + 4 - x, 4)
        far, near = (far_y, far_x) if flow == 0 else (far_x, far_y)
        own = jnp.where(core == flow, 0, 1)
        cols[own, far, :, pl.ds(pl.multiple_of(near * 256, 256), 256)] = chunk[slot]


def prepare(place, latents, pose, table, gain, bias):
    return pl.pallas_call(
        before_kernel,
        out_shape=(
            jax.ShapeDtypeStruct((NC, 4, ROWS, 4 * NZH * QROWS), BF16),
            jax.ShapeDtypeStruct((ROWS, C), F32),
            jax.ShapeDtypeStruct((ROWS, C), F32),
            jax.ShapeDtypeStruct((2, C), F32),
        ),
        in_specs=SMEM_SPEC + vmem_specs(5),
        out_specs=tuple(vmem_specs(4)),
        scratch_shapes=[
            pltpu.VMEM((3, 2, PIX + 2 * WD, C), BF16),
            pltpu.VMEM((2, ROWS, NZH * QROWS), BF16),
        ],
        compiler_params=pltpu.CompilerParams(vmem_limit_bytes=VLIM),
        cost_estimate=cost(2_000_000_000, 8_000_000),
        name="norm_and_columns",
    )(place, latents, pose, table, gain, bias)


def conv_scratch(count):
    shapes = [pltpu.SemaphoreType.DMA((3 * count,))]
    for _ in range(count):
        shapes.append(pltpu.VMEM((4, NZH, QROWS, C), BF16))
        shapes.append(pltpu.VMEM((ROWS, 4 * NZH * QROWS), BF16))
    return shapes


def forward_start(kernel, layout, start, cols, pieces):
    return pl.pallas_call(
        kernel,
        out_shape=jax.ShapeDtypeStruct((ROWS, C), F32),
        in_specs=vmem_specs(1) + any_specs(1 + len(pieces)),
        out_specs=vmem_specs(1)[0],
        scratch_shapes=conv_scratch(len(layout)),
        compiler_params=pltpu.CompilerParams(vmem_limit_bytes=VLIM),
        cost_estimate=cost(2 * ROWS * 1024 * len(layout) * C, 2_000_000 * len(layout)),
        name="spatial_forward_" + str(len(layout)),
    )(start, cols, *pieces)


def forward_last(place, start, cot_frames, cols, pieces):
    shape = (NY, NZH, TPAD, C)
    return pl.pallas_call(
        forward_last_kernel,
        out_shape=(jax.ShapeDtypeStruct((ROWS, C), BF16),) * 2
        + (jax.ShapeDtypeStruct(shape, BF16),) * 2,
        in_specs=SMEM_SPEC + vmem_specs(4) + any_specs(1 + len(pieces)),
        out_specs=tuple(vmem_specs(4)),
        scratch_shapes=[pltpu.VMEM((3 * C + 8, C), F32)] + conv_scratch(1),
        compiler_params=pltpu.CompilerParams(vmem_limit_bytes=VLIM),
        cost_estimate=cost(2 * ROWS * (1024 + 3 * C) * C, 9_000_000),
        name="spatial_forward_last_and_grad",
    )(place, start, *cot_frames, cols, *pieces)


def split_first_kernel(place, mine, came, own, *sends):
    x, y, core = place[0], place[1], place[3]

    @pl.when(core == 0)
    def _():
        for k in range(4):
            part = lax.rem(y + k, 4)
            value = (mine[part].astype(F32) + came[part].astype(F32)).reshape(4 * TPAD, C)
            if k == 0:
                own[...] = value
            else:
                sends[k - 1][...] = value.astype(BF16)

    @pl.when(core != 0)
    def _():
        for k in range(4):
            rows = pl.ds(pl.multiple_of(lax.rem(x + k, 4) * TQ, TQ), TQ)
            value = (mine[:, :, rows, :].astype(F32) + came[:, :, rows, :].astype(F32)).reshape(16 * TQ, C)
            if k == 0:
                own[...] = value
            else:
                sends[k - 1][...] = value.astype(BF16)


def split_first(place, mine, came):
    shape = (4 * TPAD, C)
    return pl.pallas_call(
        split_first_kernel,
        out_shape=(jax.ShapeDtypeStruct(shape, F32),) + (jax.ShapeDtypeStruct(shape, BF16),) * 3,
        in_specs=SMEM_SPEC + vmem_specs(2),
        out_specs=tuple(vmem_specs(4)),
        compiler_params=pltpu.CompilerParams(vmem_limit_bytes=VLIM),
        cost_estimate=cost(0, 4_000_000),
        name="grad_split_first",
    )(place, mine, came)


def split_second_kernel(place, held, first, second, third, own, *sends):
    x, y, core = place[0], place[1], place[3]
    own_sends = (own,) + tuple(sends)

    @pl.when(core == 0)
    def _():
        for k in range(4):
            for zh in range(NZH):
                start = zh * TPAD + lax.rem(x + k, 4) * TQ
                rows = pl.ds(pl.multiple_of(start, TQ), TQ)
                value = held[rows, :]
                for term in (first, second, third):
                    value += term[rows, :].astype(F32)
                own_sends[k][zh] = value

    @pl.when(core != 0)
    def _():
        for k in range(4):
            rows = pl.ds(pl.multiple_of(lax.rem(y + k, 4) * TPAD, TPAD), TPAD)
            value = held[rows, :]
            for term in (first, second, third):
                value += term[rows, :].astype(F32)
            own_sends[k][...] = value.reshape(NZH, TQ, C)


def split_second(place, held, terms):
    shape = (NZH, TQ, C)
    return pl.pallas_call(
        split_second_kernel,
        out_shape=(jax.ShapeDtypeStruct(shape, F32),) * 4,
        in_specs=SMEM_SPEC + vmem_specs(4),
        out_specs=tuple(vmem_specs(4)),
        compiler_params=pltpu.CompilerParams(vmem_limit_bytes=VLIM),
        cost_estimate=cost(0, 2_000_000),
        name="grad_split_second",
    )(place, held, *terms)


def split_third_kernel(place, held, first, second, third, *parts):
    zh = place[2]
    for k in range(4):
        part = lax.rem(zh + k, 4)
        parts[k][...] = held[part] + first[part] + second[part] + third[part]


def split_third(place, held, terms):
    return pl.pallas_call(
        split_third_kernel,
        out_shape=(jax.ShapeDtypeStruct((TQ, C), F32),) * 4,
        in_specs=SMEM_SPEC + vmem_specs(4),
        out_specs=tuple(vmem_specs(4)),
        cost_estimate=cost(0, 800_000),
        name="grad_split_third",
    )(place, held, *terms)


def slope_of(value):
    gate = jax.nn.sigmoid(value)
    return gate * (1.0 + value * (1.0 - gate))


def temporal_back_kernel(place, before, own, after, spatial_out, *rest):
    pieces, (back_spatial, weights, whole, wide, sems) = rest[:16], rest[16:]
    copies = load_copies(place, pieces, whole, sems, TQ, SQ)
    for copy in copies:
        copy.start()
    for copy in copies:
        copy.wait()
    for block in range(32):
        pair, core = divmod(block, 2)
        wide[pl.ds(block * TROWS, TPAD), :] = whole[pair // 4, core, pair % 4].astype(F32)
    back = jnp.zeros((ROWS, C), F32)
    for tap in range(3):
        weight = wide[pl.ds(tap * C, C), :].astype(BF16)
        weights[tap] = weight
        back += lax.dot_general(
            neighbour_rows(place, before, own, after, 2 - tap),
            weight,
            (((1,), (1,)), ((), ())),
            preferred_element_type=F32,
        )
    slope = slope_of(spatial_out[...].astype(F32))
    cot = own[...].astype(F32)
    back_spatial[...] = (cot + back * slope).astype(BF16)


def temporal_back(place, cot_frames, spatial_out, pieces):
    return pl.pallas_call(
        temporal_back_kernel,
        out_shape=(jax.ShapeDtypeStruct((ROWS, C), BF16), jax.ShapeDtypeStruct((3, C, C), BF16)),
        in_specs=SMEM_SPEC + vmem_specs(4) + any_specs(16),
        out_specs=tuple(vmem_specs(2)),
        scratch_shapes=[
            pltpu.VMEM((NY, NC, NZH, TPAD, C), BF16),
            pltpu.VMEM((3 * C + 8, C), F32),
            pltpu.SemaphoreType.DMA((32,)),
        ],
        compiler_params=pltpu.CompilerParams(vmem_limit_bytes=VLIM),
        cost_estimate=cost(6 * ROWS * C * C, 8_000_000),
        name="temporal_back",
    )(place, *cot_frames, spatial_out, *pieces)


def temporal_ahead_kernel(place, before, own, after, spatial_out, weights, mixed):
    ahead = spatial_out[...].astype(F32)
    for tap in range(3):
        ahead += jnp.dot(
            neighbour_rows(place, before, own, after, tap), weights[tap], preferred_element_type=F32
        )
    mixed[...] = ahead


def temporal_ahead(place, moved_frames, spatial_out, weights):
    return pl.pallas_call(
        temporal_ahead_kernel,
        out_shape=jax.ShapeDtypeStruct((ROWS, C), F32),
        in_specs=SMEM_SPEC + vmem_specs(5),
        out_specs=vmem_specs(1)[0],
        compiler_params=pltpu.CompilerParams(vmem_limit_bytes=VLIM),
        cost_estimate=cost(6 * ROWS * C * C, 5_000_000),
        name="temporal_ahead",
    )(place, *moved_frames, spatial_out, weights)


def tap_range(first, last):
    return first * C // SROWS, -(-last * C // SROWS)


def add_taps(dy, place, back_spatial, pieces, sums, whole, wide, sems):
    low, high = tap_range(3 * dy, 3 * dy + 3)
    first_y, last_y = low // (NZH * NC), (high - 1) // (NZH * NC)
    copies = load_copies(place, pieces, whole, sems, SQ, 0)
    needed = []
    for own in (0, 1):
        for far in range(4):
            for near in range(4):
                from_y = origin(place, own, far, near)[0]
                needed.append(jnp.logical_and(from_y >= first_y, from_y <= last_y))
    for copy, need in zip(copies, needed):
        pl.when(need)(copy.start)
    for copy, need in zip(copies, needed):
        pl.when(need)(copy.wait)
    for block in range(low, high):
        pair, core = divmod(block, 2)
        wide[pl.ds((block - low) * SROWS, SPAD), :] = whole[pair // 4, core, pair % 4].astype(F32)
    column = lax.rem(lax.broadcasted_iota(jnp.int32, (ROWS, C), 0), WD)
    for dx in range(3):
        product = lax.dot_general(
            back_spatial[...],
            wide[pl.ds((3 * dy + dx) * C - low * SROWS, C), :].astype(BF16),
            (((1,), (1,)), ((), ())),
            preferred_element_type=F32,
        )
        if dx == 0:
            product = jnp.where(column < WD - 1, pltpu.roll(product, ROWS - 1, 0), 0.0)
        elif dx == 2:
            product = jnp.where(column > 0, pltpu.roll(product, 1, 0), 0.0)
        for frame in range(2):
            base = frame * PIX
            to = base + max(dy - 1, 0) * WD
            at = base + max(1 - dy, 0) * WD
            count = PIX - abs(dy - 1) * WD
            sums[pl.ds(to, count), :] += product[at : at + count, :]


def backward_first_kernel(place, back_spatial, *rest):
    pieces, (sums, whole, wide, sems) = rest[:16], rest[16:]
    sums[...] = jnp.zeros_like(sums)
    add_taps(0, place, back_spatial, pieces, sums, whole, wide, sems)


def backward_middle_kernel(place, back_spatial, start, *rest):
    pieces, (sums, whole, wide, sems) = rest[:16], rest[16:]
    sums[...] = start[...]
    add_taps(1, place, back_spatial, pieces, sums, whole, wide, sems)


def backward_last_kernel(place, back_spatial, start, normed, scale, inv_std, *rest):
    pieces, (latent_grad, sums, whole, wide, sems) = rest[:16], rest[16:]
    sums[...] = start[...]
    add_taps(2, place, back_spatial, pieces, sums, whole, wide, sems)
    spread = group_spread()
    for frame in range(2):
        rows = pl.ds(frame * PIX, PIX)
        back_normed = sums[rows, :] * scale[rows, :]
        unit = normed[rows, :]
        first = jnp.sum(back_normed, axis=0, keepdims=True)
        second = jnp.sum(back_normed * unit, axis=0, keepdims=True)
        means = group_means(first, second, spread)
        latent_grad[rows, :] = inv_std[pl.ds(frame, 1), :] * (
            back_normed - means[0:1] - unit * means[1:2]
        )


def tap_scratch(first, last):
    low, high = tap_range(first, last)
    return [
        pltpu.VMEM((NY, NC, NZH, SPAD, C), BF16),
        pltpu.VMEM(((high - low) * SROWS + 20, C), F32),
        pltpu.SemaphoreType.DMA((32,)),
    ]


def backward_taps(kernel, first, place, operands, pieces):
    last = first + 3
    shape = (ROWS, C)
    ends = last == 9
    return pl.pallas_call(
        kernel,
        out_shape=jax.ShapeDtypeStruct(shape, F32),
        in_specs=SMEM_SPEC + vmem_specs(len(operands)) + any_specs(16),
        out_specs=vmem_specs(1)[0],
        scratch_shapes=([pltpu.VMEM(shape, F32)] if ends else []) + tap_scratch(first, last),
        compiler_params=pltpu.CompilerParams(vmem_limit_bytes=VLIM),
        cost_estimate=cost(6 * ROWS * C * C, 8_000_000),
        name="spatial_backward_" + str(first),
    )(place, *operands, *pieces)


def halos(own):
    size = NX * NZL
    before = lax.ppermute(own[1], "frames", [(k, (k + 1) % size) for k in range(size)])
    after = lax.ppermute(own[0], "frames", [((k + 1) % size, k) for k in range(size)])
    return before, after


def gather_weights(place_x, spatial_weight, temporal_weight):
    x = place_x
    spatial = jnp.pad(spatial_weight, ((0, SPAD - SROWS), (0, 0)))
    temporal_rows = jnp.pad(temporal_weight, ((0, TPAD - TROWS), (0, 0)))
    quarter = jnp.concatenate(
        [
            lax.dynamic_slice_in_dim(spatial, x * SQ, SQ, 0),
            lax.dynamic_slice_in_dim(temporal_rows, x * TQ, TQ, 0),
        ]
    )
    return quarter


def per_device(
    latents,
    pose,
    timesteps,
    norm_gain,
    norm_bias,
    pose_table,
    time_weight,
    spatial_weight,
    temporal_weight,
    cotangent,
):
    frame_at = lax.axis_index("frames")
    row_at = lax.axis_index("dp")
    x = frame_at % NX
    y = row_at // (NZH * NC)
    zh = (row_at // NC) % NZH
    core = row_at % NC
    place = jnp.stack(
        [x, y, zh, core, frame_at > 0, frame_at < NX * NZL - 1], dtype=jnp.int32
    )

    quarter = gather_weights(x, spatial_weight, temporal_weight)
    came = [send(quarter, zh_step(k)) for k in (1, 2, 3)]
    column = in_order(quarter, came, zh)
    came = [send(column, xy_step(k)) for k in (1, 2, 3)]
    low, high = jnp.stack([column, came[0]]), jnp.stack([came[1], came[2]])
    frames_own, _ = lax.optimization_barrier((cotangent[0], low))
    cot_before, cot_after = halos(frames_own)
    cot_frames = cot_before, cotangent.reshape(ROWS, C), cot_after
    one_low, three_high = send(low, yx_step(1)), send(high, yx_step(3))
    one_high, three_low = send(high, yx_step(1)), send(low, yx_step(3))

    _, frames_dev, pixels, _ = latents.shape
    factor = 1.0 / math.sqrt(lax.axis_size("dp") * frames_dev * lax.axis_size("frames") * pixels)
    cols, normed, scale, inv_std = prepare(
        place, latents.reshape(ROWS, C), pose[0], pose_table, norm_gain, norm_bias
    )
    shift = time_shift(timesteps, time_weight)
    swapped = {}
    swapped[0] = send(low, core_swap), send(high, core_swap)
    one_low, three_high, cols, shift = lax.optimization_barrier((one_low, three_high, cols, shift))
    two_low, two_high = send(one_low, yx_step(1)), send(three_high, yx_step(3))
    swapped[1] = send(one_low, core_swap), send(one_high, core_swap)
    swapped[3] = send(three_low, core_swap), send(three_high, core_swap)
    total = forward_start(
        forward_first_kernel,
        FIRST_PART,
        shift,
        cols,
        [low, high, one_low, one_high, three_low, three_high, *swapped[0]],
    )
    two_low, two_high, total = lax.optimization_barrier((two_low, two_high, total))
    swapped[2] = send(two_low, core_swap), send(two_high, core_swap)
    total = forward_start(
        forward_middle_kernel,
        MIDDLE_PART,
        total,
        cols,
        [*swapped[1], *swapped[3], two_low, two_high],
    )
    pieces = [low, high, one_low, one_high, two_low, two_high, three_low, three_high]
    for far in range(4):
        pieces.extend(swapped[far])
    spatial_out, moved, mine, other = forward_last(place, total, cot_frames, cols, swapped[2])

    came = send(other, core_swap)
    held, *parts = split_first(place, mine, came)
    came = [send(part, yx_step(k + 1)) for k, part in enumerate(parts)]
    ready, _ = lax.optimization_barrier((spatial_out, held))
    back_spatial, weights = temporal_back(place, cot_frames, ready, pieces)
    *came, back_spatial = lax.optimization_barrier((*came, back_spatial))

    held, *parts = split_second(place, held, came)
    came = [send(part, xy_step(k + 1)) for k, part in enumerate(parts)]
    ready, moved, _ = lax.optimization_barrier((back_spatial, moved, held))
    sums = backward_taps(backward_first_kernel, 0, place, [ready], pieces)
    moved_before, moved_after = halos(moved.reshape(2, PIX, C))
    *came, sums = lax.optimization_barrier((*came, sums))

    held, *parts = split_third(place, held, came)
    came = [send(part, zh_step(k + 1)) for k, part in enumerate(parts)]
    sums, _ = lax.optimization_barrier((sums, held))
    sums = backward_taps(backward_middle_kernel, 3, place, [ready, sums], pieces)
    *came, sums = lax.optimization_barrier((*came, sums))

    held = held + came[0] + came[1] + came[2]
    came = send(held, zl_swap)
    sums, _ = lax.optimization_barrier((sums, held))
    latent_grad = backward_taps(
        backward_last_kernel, 6, place, [ready, sums, normed, scale, inv_std], pieces
    )
    came, latent_grad = lax.optimization_barrier((came, latent_grad))
    held = (held + came) * factor
    came = [send(held, x_step(k)) for k in (1, 2, 3)]
    moved_before, _ = lax.optimization_barrier((moved_before, held))
    mixed = temporal_ahead(place, (moved_before, moved, moved_after), spatial_out, weights)
    *came, mixed = lax.optimization_barrier((*came, mixed))
    temporal_grad = in_order(held, came, x).reshape(TPAD, C)[:TROWS]
    shape = latents.shape
    return mixed.reshape(shape), latent_grad.reshape(shape), temporal_grad


def solution(mesh):
    placed = (
        P("dp", "frames", None, None),
        P("dp", "frames", None),
        P("dp"),
        P(),
        P(),
        P(),
        P(),
        P("dp", None),
        P("dp", None),
        P("dp", "frames", None, None),
    )
    return jax.shard_map(
        per_device,
        mesh=mesh,
        in_specs=placed,
        out_specs=(P("dp", "frames", None, None), P("dp", "frames", None, None), P("dp", None)),
        check_vma=False,
    )
```

```python
import math

import jax
import jax.numpy as jnp
from jax import lax
from jax.experimental import pallas as pl
from jax.experimental.pallas import tpu as pltpu
from jax.sharding import PartitionSpec as P

GROUP_CH = 40
HT = 9
WD = 16
PIX = HT * WD
C = 640
NX, NY, NZH, NZL, NC = 4, 4, 4, 2, 2
AXES = ("frames", "dp")
SROWS, SPAD, SQ = 180, 192, 48
TROWS, TPAD, TQ = 60, 64, 16
QROWS = SQ + TQ
ROWS = 2 * PIX
F32 = jnp.float32
BF16 = jnp.bfloat16
VLIM = 58 * 1024 * 1024


def coords():
    for zl in range(NZL):
        for x in range(NX):
            for y in range(NY):
                for zh in range(NZH):
                    for c in range(NC):
                        yield zl, x, y, zh, c


def index_of(zl, x, y, zh, c):
    return (zl * NX + x) * (NY * NZH * NC) + (y * NZH + zh) * NC + c


def routes(move):
    return [(index_of(*at), index_of(*move(*at))) for at in coords()]


def send(value, move):
    return lax.ppermute(value, AXES, routes(move))


def core_swap(zl, x, y, zh, c):
    return zl, x, y, zh, 1 - c


def zl_swap(zl, x, y, zh, c):
    return 1 - zl, x, y, zh, c


def zh_step(k):
    return lambda zl, x, y, zh, c: (zl, x, y, (zh + k) % NZH, c)


def x_step(k):
    return lambda zl, x, y, zh, c: (zl, (x + k) % NX, y, zh, c)


def xy_step(k):
    return lambda zl, x, y, zh, c: (
        (zl, (x + k) % NX, y, zh, c) if c == 0 else (zl, x, (y + k) % NY, zh, c)
    )


def yx_step(k):
    return lambda zl, x, y, zh, c: (
        (zl, x, (y + k) % NY, zh, c) if c == 0 else (zl, (x + k) % NX, y, zh, c)
    )


def in_order(own, received, place):
    parts = [received[2], received[1], received[0], own]
    stacked = jnp.stack(parts + parts)
    return lax.dynamic_slice_in_dim(stacked, (3 - place) % 4, 4, axis=0)


def time_shift(timesteps, time_weight):
    half = time_weight.shape[0] // 2
    positions = jnp.arange(half, dtype=jnp.float32)
    frequencies = jnp.exp(-math.log(10000.0) * positions / half)
    angles = timesteps.astype(jnp.float32)[:, None] * frequencies[None, :]
    embedding = jnp.concatenate([jnp.cos(angles), jnp.sin(angles)], axis=-1)
    return jnp.dot(embedding, time_weight, precision=lax.Precision.HIGHEST)


FIRST_PART = (0, 1, 3)
LAST_PART = (2,)


def piece_of(pieces, own, far, near):
    if far in LAST_PART:
        return pieces[own * 2 + 1].at[LAST_PART.index(far), near]
    return pieces[own * 2].at[FIRST_PART.index(far), near]


def origin(place, own, far, near):
    x, y, core = place[0], place[1], place[3]
    flow = core if own == 0 else 1 - core
    from_y = lax.rem(y + 4 - jnp.where(flow == 0, far, near), 4)
    from_x = lax.rem(x + 4 - jnp.where(flow == 0, near, far), 4)
    return from_y, flow, from_x


def load_copies(place, pieces, whole, sems, rows):
    copies = []
    for own in (0, 1):
        for far in range(4):
            for near in range(4):
                from_y, flow, from_x = origin(place, own, far, near)
                copies.append(
                    pltpu.make_async_copy(
                        piece_of(pieces, own, far, near).at[:, pl.ds(0, rows), :],
                        whole.at[from_y, flow, :, pl.ds(pl.multiple_of(from_x * rows, rows), rows), :],
                        sems.at[len(copies)],
                    )
                )
    return copies


def conv_parts(cols, pieces, layout, rows, columns, kept, temporal_rows, sems):
    copies, keeps = [], []
    for k, far in enumerate(layout):
        copies.append(
            (
                pltpu.make_async_copy(pieces[2 * k], rows.at[k, pl.ds(0, 2)], sems.at[4 * k]),
                pltpu.make_async_copy(pieces[2 * k + 1], rows.at[k, pl.ds(2, 2)], sems.at[4 * k + 1]),
                pltpu.make_async_copy(cols.at[far], columns.at[k], sems.at[4 * k + 2]),
            )
        )
        keeps.append(pltpu.make_async_copy(rows.at[k], kept.at[k], sems.at[4 * k + 3]))
    for group in copies:
        for copy in group:
            copy.start()
    for k, group in enumerate(copies):
        for copy in group:
            copy.wait()
        keeps[k].start()
        temporal_rows[k] = rows[k, :, :, pl.ds(SQ, TQ), :]
        yield jnp.dot(
            columns[k], rows[k].reshape(4 * NZH * QROWS, C), preferred_element_type=F32
        )
    for keep in keeps:
        keep.wait()


def forward_first_kernel(cols, *rest):
    pieces, (total, kept, temporal_rows, rows, columns, sems) = rest[:6], rest[6:]
    parts = conv_parts(cols, pieces, FIRST_PART, rows, columns, kept, temporal_rows, sems)
    for k, product in enumerate(parts):
        if k == 0:
            total[...] = product
        else:
            total[...] += product


def forward_last_kernel(start, cols, *rest):
    pieces, (own, other, kept, temporal_rows, rows, columns, sems) = rest[:2], rest[2:]
    for product in conv_parts(cols, pieces, LAST_PART, rows, columns, kept, temporal_rows, sems):
        own[...] = product[:ROWS] + start[pl.ds(0, ROWS), :]
        other[...] = product[ROWS:] + start[pl.ds(ROWS, ROWS), :]


def grad_kernel(place, shift, part, came, before, own, after, spatial_out, moved, mine, other, total):
    rounded = (part[...] + came[...] + shift[...]).astype(BF16)
    spatial_out[...] = rounded
    wide = rounded.astype(F32)
    left = (wide * jax.nn.sigmoid(wide)).astype(BF16)
    moved[...] = left
    core = place[3]
    right = jnp.concatenate(
        [neighbour_rows(place, before, own, after, 2 - tap) for tap in range(3)], axis=1
    )
    product = lax.dot_general(left, right, (((0,), (0,)), ((), ())), preferred_element_type=F32)
    for tap in range(3):
        total[pl.ds(tap * C, C), :] = product[:, tap * C : (tap + 1) * C]
    total[pl.ds(3 * C, 8), :] = jnp.zeros((8, C), F32)
    for block in range(32):
        spot = block // 2
        rows = total[pl.ds(block * TROWS, TPAD), :].astype(BF16)

        @pl.when(core == block % 2)
        def _():
            mine[spot // 4, spot % 4] = rows

        @pl.when(core != block % 2)
        def _():
            other[spot // 4, spot % 4] = rows


def neighbour_rows(place, before, own, after, tap):
    if tap == 1:
        return own[...]
    if tap == 0:
        edge = jnp.where(place[4] > 0, before[...], jnp.zeros((PIX, C), BF16))
        return jnp.concatenate([edge, own[pl.ds(0, PIX), :]], axis=0)
    edge = jnp.where(place[5] > 0, after[...], jnp.zeros((PIX, C), BF16))
    return jnp.concatenate([own[pl.ds(PIX, PIX), :], edge], axis=0)


def any_specs(count):
    return [pl.BlockSpec(memory_space=pl.ANY)] * count


def vmem_specs(count):
    return [pl.BlockSpec(memory_space=pltpu.VMEM)] * count


SMEM_SPEC = [pl.BlockSpec(memory_space=pltpu.SMEM)]


def cost(flops, moved):
    return pl.CostEstimate(flops=flops, bytes_accessed=moved, transcendentals=0)


def group_spread():
    group_r = lax.broadcasted_iota(jnp.int32, (C, C), 0) // GROUP_CH
    group_c = lax.broadcasted_iota(jnp.int32, (C, C), 1) // GROUP_CH
    return jnp.where(group_r == group_c, 1.0 / (PIX * GROUP_CH), 0.0).astype(F32)


def group_means(first, second, spread):
    both = jnp.concatenate([first, second, jnp.zeros((6, C), F32)], axis=0)
    return jnp.dot(both, spread, precision=lax.Precision.HIGHEST, preferred_element_type=F32)


def segments(core):
    found = {}
    for y in range(NY):
        for x in range(NX):
            parts = []
            for zh in range(NZH):
                block = (y * NZH + zh) * NC + core
                start = SROWS * block + SQ * x
                end = min(start + SQ, SROWS * (block + 1))
                lane = zh * QROWS
                while start < end:
                    tap, channel = divmod(start, C)
                    count = min(end - start, C - channel)
                    parts.append((lane, tap, channel, count))
                    start += count
                    lane += count
            found[y, x] = parts
    return found


def norm_kernel(latents, pose, table, gain, bias, activated, normed, scale, inv_std):
    kinds = lax.broadcasted_iota(jnp.int32, (table.shape[0], PIX), 0)
    gains = gain[...].reshape(1, C)
    biases = bias[...].reshape(1, C)
    spread = group_spread()
    for frame in range(2):
        rows = pl.ds(frame * PIX, PIX)
        onehot = (pose[pl.ds(frame, 1), :] == kinds).astype(F32)
        shifted = latents[rows, :].astype(F32) + lax.dot_general(
            onehot,
            table[...],
            (((0,), (0,)), ((), ())),
            precision=lax.Precision.HIGHEST,
            preferred_element_type=F32,
        )
        means = group_means(
            jnp.sum(shifted, axis=0, keepdims=True),
            jnp.sum(shifted * shifted, axis=0, keepdims=True),
            spread,
        )
        center = means[0:1]
        inverse = lax.rsqrt(means[1:2] - center * center + 1e-05)
        inv_std[pl.ds(frame, 1), :] = inverse
        unit = (shifted - center) * inverse
        normed[rows, :] = unit
        value = unit * gains + biases
        gate = jax.nn.sigmoid(value)
        scale[rows, :] = gate * (1.0 + value * (1.0 - gate)) * gains
        activated[rows, :] = (value * gate).astype(BF16)


def norm(latents, pose, table, gain, bias):
    return pl.pallas_call(
        norm_kernel,
        out_shape=(
            jax.ShapeDtypeStruct((ROWS, C), BF16),
            jax.ShapeDtypeStruct((ROWS, C), F32),
            jax.ShapeDtypeStruct((ROWS, C), F32),
            jax.ShapeDtypeStruct((2, C), F32),
        ),
        in_specs=vmem_specs(5),
        out_specs=tuple(vmem_specs(4)),
        compiler_params=pltpu.CompilerParams(vmem_limit_bytes=VLIM),
        cost_estimate=cost(500_000_000, 3_000_000),
        name="group_norm",
    )(latents, pose, table, gain, bias)


def columns_kernel(place, own, other, cols, padded, chunk):
    at_x, at_y, core = place[0], place[1], place[3]
    column = lax.rem(lax.broadcasted_iota(jnp.int32, (PIX, C), 0), WD)
    for frame in range(4):
        source = own if frame < 2 else other
        active = source[pl.ds((frame % 2) * PIX, PIX), :].astype(F32)
        for dx in range(3):
            if dx == 0:
                moved = jnp.where(column > 0, pltpu.roll(active, 1, 0), 0.0)
            elif dx == 1:
                moved = active
            else:
                moved = jnp.where(column < WD - 1, pltpu.roll(active, PIX - 1, 0), 0.0)
            padded[dx, frame, pl.ds(0, WD), :] = jnp.zeros((WD, C), BF16)
            padded[dx, frame, pl.ds(WD, PIX), :] = moved.astype(BF16)
            padded[dx, frame, pl.ds(WD + PIX, WD), :] = jnp.zeros((WD, C), BF16)
    chunk[...] = jnp.zeros_like(chunk)

    def lay_out(flow):
        for number, ((y, x), parts) in enumerate(segments(flow).items()):
            slot = number % 2
            if x == NX - 1:
                chunk[slot] = jnp.zeros((2 * ROWS, NZH * QROWS), BF16)
            for lane, tap, channel, count in parts:
                dy, dx = divmod(tap, 3)
                for frame in range(4):
                    chunk[slot, frame * PIX : (frame + 1) * PIX, lane : lane + count] = padded[
                        dx, frame, dy * WD : dy * WD + PIX, channel : channel + count
                    ]
            far_y, far_x = lax.rem(at_y + 4 - y, 4), lax.rem(at_x + 4 - x, 4)
            far, near = (far_y, far_x) if flow == 0 else (far_x, far_y)
            cols[far, :, pl.ds(pl.multiple_of(near * 256, 256), 256)] = chunk[slot]

    pl.when(core == 0)(lambda: lay_out(0))
    pl.when(core != 0)(lambda: lay_out(1))


def columns(place, own, other):
    return pl.pallas_call(
        columns_kernel,
        out_shape=jax.ShapeDtypeStruct((4, 2 * ROWS, 4 * NZH * QROWS), BF16),
        in_specs=SMEM_SPEC + vmem_specs(2),
        out_specs=vmem_specs(1)[0],
        scratch_shapes=[
            pltpu.VMEM((3, 4, PIX + 2 * WD, C), BF16),
            pltpu.VMEM((2, 2 * ROWS, NZH * QROWS), BF16),
        ],
        compiler_params=pltpu.CompilerParams(vmem_limit_bytes=VLIM),
        cost_estimate=cost(1_000_000_000, 8_000_000),
        name="window_columns",
    )(place, own, other)


def forward_call(kernel, layout, outs, operands, cols, pieces, name):
    count = len(layout)
    return pl.pallas_call(
        kernel,
        out_shape=(jax.ShapeDtypeStruct(outs[0], F32),) * outs[1]
        + (
            jax.ShapeDtypeStruct((count, 4, NZH, QROWS, C), BF16),
            jax.ShapeDtypeStruct((count, 4, NZH, TQ, C), BF16),
        ),
        in_specs=vmem_specs(len(operands)) + any_specs(1 + len(pieces)),
        out_specs=tuple(vmem_specs(outs[1]) + any_specs(1) + vmem_specs(1)),
        scratch_shapes=[
            pltpu.VMEM((count, 4, NZH, QROWS, C), BF16),
            pltpu.VMEM((count, 2 * ROWS, 4 * NZH * QROWS), BF16),
            pltpu.SemaphoreType.DMA((4 * count,)),
        ],
        compiler_params=pltpu.CompilerParams(vmem_limit_bytes=VLIM),
        cost_estimate=cost(4 * ROWS * 1024 * count * C, 3_000_000 * count),
        name=name,
    )(*operands, cols, *pieces)


def forward_first(cols, pieces):
    return forward_call(
        forward_first_kernel, FIRST_PART, ((2 * ROWS, C), 1), (), cols, pieces, "spatial_forward_first"
    )


def forward_last(start, cols, pieces):
    return forward_call(
        forward_last_kernel, LAST_PART, ((ROWS, C), 2), (start,), cols, pieces, "spatial_forward_last"
    )


def grad_terms(place, shift, part, came, cot_frames):
    shape = (NY, NZH, TPAD, C)
    return pl.pallas_call(
        grad_kernel,
        out_shape=(jax.ShapeDtypeStruct((ROWS, C), BF16),) * 2
        + (jax.ShapeDtypeStruct(shape, BF16),) * 2,
        in_specs=SMEM_SPEC + vmem_specs(6),
        out_specs=tuple(vmem_specs(4)),
        scratch_shapes=[pltpu.VMEM((3 * C + 8, C), F32)],
        compiler_params=pltpu.CompilerParams(vmem_limit_bytes=VLIM),
        cost_estimate=cost(2 * ROWS * 3 * C * C, 8_000_000),
        name="temporal_grad_terms",
    )(place, shift, part, came, *cot_frames)


def split_first_kernel(place, mine, came, own, *sends):
    x, y, core = place[0], place[1], place[3]

    @pl.when(core == 0)
    def _():
        for k in range(4):
            part = lax.rem(y + k, 4)
            value = (mine[part].astype(F32) + came[part].astype(F32)).reshape(4 * TPAD, C)
            if k == 0:
                own[...] = value
            else:
                sends[k - 1][...] = value.astype(BF16)

    @pl.when(core != 0)
    def _():
        for k in range(4):
            rows = pl.ds(pl.multiple_of(lax.rem(x + k, 4) * TQ, TQ), TQ)
            value = (mine[:, :, rows, :].astype(F32) + came[:, :, rows, :].astype(F32)).reshape(16 * TQ, C)
            if k == 0:
                own[...] = value
            else:
                sends[k - 1][...] = value.astype(BF16)


def split_first(place, mine, came):
    shape = (4 * TPAD, C)
    return pl.pallas_call(
        split_first_kernel,
        out_shape=(jax.ShapeDtypeStruct(shape, F32),) + (jax.ShapeDtypeStruct(shape, BF16),) * 3,
        in_specs=SMEM_SPEC + vmem_specs(2),
        out_specs=tuple(vmem_specs(4)),
        compiler_params=pltpu.CompilerParams(vmem_limit_bytes=VLIM),
        cost_estimate=cost(0, 4_000_000),
        name="grad_split_first",
    )(place, mine, came)


def split_second_kernel(place, held, first, second, third, own, *sends):
    x, y, core = place[0], place[1], place[3]
    own_sends = (own,) + tuple(sends)

    @pl.when(core == 0)
    def _():
        for k in range(4):
            for zh in range(NZH):
                start = zh * TPAD + lax.rem(x + k, 4) * TQ
                rows = pl.ds(pl.multiple_of(start, TQ), TQ)
                value = held[rows, :]
                for term in (first, second, third):
                    value += term[rows, :].astype(F32)
                own_sends[k][zh] = value

    @pl.when(core != 0)
    def _():
        for k in range(4):
            rows = pl.ds(pl.multiple_of(lax.rem(y + k, 4) * TPAD, TPAD), TPAD)
            value = held[rows, :]
            for term in (first, second, third):
                value += term[rows, :].astype(F32)
            own_sends[k][...] = value.reshape(NZH, TQ, C)


def split_second(place, held, terms):
    shape = (NZH, TQ, C)
    return pl.pallas_call(
        split_second_kernel,
        out_shape=(jax.ShapeDtypeStruct(shape, F32),) * 4,
        in_specs=SMEM_SPEC + vmem_specs(4),
        out_specs=tuple(vmem_specs(4)),
        compiler_params=pltpu.CompilerParams(vmem_limit_bytes=VLIM),
        cost_estimate=cost(0, 2_000_000),
        name="grad_split_second",
    )(place, held, *terms)


def split_third_kernel(place, held, first, second, third, *parts):
    zh = place[2]
    for k in range(4):
        part = lax.rem(zh + k, 4)
        parts[k][...] = held[part] + first[part] + second[part] + third[part]


def split_third(place, held, terms):
    return pl.pallas_call(
        split_third_kernel,
        out_shape=(jax.ShapeDtypeStruct((TQ, C), F32),) * 4,
        in_specs=SMEM_SPEC + vmem_specs(4),
        out_specs=tuple(vmem_specs(4)),
        cost_estimate=cost(0, 800_000),
        name="grad_split_third",
    )(place, held, *terms)


def slope_of(value):
    gate = jax.nn.sigmoid(value)
    return gate * (1.0 + value * (1.0 - gate))


def temporal_back_kernel(place, before, own, after, spatial_out, *rest):
    pieces, (back_spatial, weights, whole, wide, sems) = rest[:4], rest[4:]
    copies = load_copies(place, pieces, whole, sems, TQ)
    for copy in copies:
        copy.start()
    for copy in copies:
        copy.wait()
    for block in range(32):
        pair, core = divmod(block, 2)
        wide[pl.ds(block * TROWS, TPAD), :] = whole[pair // 4, core, pair % 4].astype(F32)
    back = jnp.zeros((ROWS, C), F32)
    for tap in range(3):
        weight = wide[pl.ds(tap * C, C), :].astype(BF16)
        weights[tap] = weight
        back += lax.dot_general(
            neighbour_rows(place, before, own, after, 2 - tap),
            weight,
            (((1,), (1,)), ((), ())),
            preferred_element_type=F32,
        )
    slope = slope_of(spatial_out[...].astype(F32))
    cot = own[...].astype(F32)
    back_spatial[...] = (cot + back * slope).astype(BF16)


def temporal_back(place, cot_frames, spatial_out, pieces):
    return pl.pallas_call(
        temporal_back_kernel,
        out_shape=(jax.ShapeDtypeStruct((ROWS, C), BF16), jax.ShapeDtypeStruct((3, C, C), BF16)),
        in_specs=SMEM_SPEC + vmem_specs(4) + any_specs(4),
        out_specs=tuple(vmem_specs(2)),
        scratch_shapes=[
            pltpu.VMEM((NY, NC, NZH, TPAD, C), BF16),
            pltpu.VMEM((3 * C + 8, C), F32),
            pltpu.SemaphoreType.DMA((32,)),
        ],
        compiler_params=pltpu.CompilerParams(vmem_limit_bytes=VLIM),
        cost_estimate=cost(6 * ROWS * C * C, 8_000_000),
        name="temporal_back",
    )(place, *cot_frames, spatial_out, *pieces)


def temporal_ahead_kernel(place, before, own, after, spatial_out, weights, mixed):
    ahead = spatial_out[...].astype(F32)
    for tap in range(3):
        ahead += jnp.dot(
            neighbour_rows(place, before, own, after, tap), weights[tap], preferred_element_type=F32
        )
    mixed[...] = ahead


def temporal_ahead(place, moved_frames, spatial_out, weights):
    return pl.pallas_call(
        temporal_ahead_kernel,
        out_shape=jax.ShapeDtypeStruct((ROWS, C), F32),
        in_specs=SMEM_SPEC + vmem_specs(5),
        out_specs=vmem_specs(1)[0],
        compiler_params=pltpu.CompilerParams(vmem_limit_bytes=VLIM),
        cost_estimate=cost(6 * ROWS * C * C, 5_000_000),
        name="temporal_ahead",
    )(place, *moved_frames, spatial_out, weights)


def tap_range(first, last):
    return first * C // SROWS, -(-last * C // SROWS)


def add_taps(dy, place, back_spatial, pieces, sums, whole, wide, sems):
    low, high = tap_range(3 * dy, 3 * dy + 3)
    first_y, last_y = low // (NZH * NC), (high - 1) // (NZH * NC)
    copies = load_copies(place, pieces, whole, sems, SQ)
    needed = []
    for own in (0, 1):
        for far in range(4):
            for near in range(4):
                from_y = origin(place, own, far, near)[0]
                needed.append(jnp.logical_and(from_y >= first_y, from_y <= last_y))
    for copy, need in zip(copies, needed):
        pl.when(need)(copy.start)
    for copy, need in zip(copies, needed):
        pl.when(need)(copy.wait)
    for block in range(low, high):
        pair, core = divmod(block, 2)
        wide[pl.ds((block - low) * SROWS, SPAD), :] = whole[pair // 4, core, pair % 4].astype(F32)
    column = lax.rem(lax.broadcasted_iota(jnp.int32, (ROWS, C), 0), WD)
    for dx in range(3):
        product = lax.dot_general(
            back_spatial[...],
            wide[pl.ds((3 * dy + dx) * C - low * SROWS, C), :].astype(BF16),
            (((1,), (1,)), ((), ())),
            preferred_element_type=F32,
        )
        if dx == 0:
            product = jnp.where(column < WD - 1, pltpu.roll(product, ROWS - 1, 0), 0.0)
        elif dx == 2:
            product = jnp.where(column > 0, pltpu.roll(product, 1, 0), 0.0)
        for frame in range(2):
            base = frame * PIX
            to = base + max(dy - 1, 0) * WD
            at = base + max(1 - dy, 0) * WD
            count = PIX - abs(dy - 1) * WD
            sums[pl.ds(to, count), :] += product[at : at + count, :]


def backward_first_kernel(place, back_spatial, *rest):
    pieces, (sums, whole, wide, sems) = rest[:4], rest[4:]
    sums[...] = jnp.zeros_like(sums)
    add_taps(0, place, back_spatial, pieces, sums, whole, wide, sems)


def backward_middle_kernel(place, back_spatial, start, *rest):
    pieces, (sums, whole, wide, sems) = rest[:4], rest[4:]
    sums[...] = start[...]
    add_taps(1, place, back_spatial, pieces, sums, whole, wide, sems)


def backward_last_kernel(place, back_spatial, start, normed, scale, inv_std, *rest):
    pieces, (latent_grad, sums, whole, wide, sems) = rest[:4], rest[4:]
    sums[...] = start[...]
    add_taps(2, place, back_spatial, pieces, sums, whole, wide, sems)
    spread = group_spread()
    for frame in range(2):
        rows = pl.ds(frame * PIX, PIX)
        back_normed = sums[rows, :] * scale[rows, :]
        unit = normed[rows, :]
        first = jnp.sum(back_normed, axis=0, keepdims=True)
        second = jnp.sum(back_normed * unit, axis=0, keepdims=True)
        means = group_means(first, second, spread)
        latent_grad[rows, :] = inv_std[pl.ds(frame, 1), :] * (
            back_normed - means[0:1] - unit * means[1:2]
        )


def tap_scratch(first, last):
    low, high = tap_range(first, last)
    return [
        pltpu.VMEM((NY, NC, NZH, SPAD, C), BF16),
        pltpu.VMEM(((high - low) * SROWS + 20, C), F32),
        pltpu.SemaphoreType.DMA((32,)),
    ]


def backward_taps(kernel, first, place, operands, pieces):
    last = first + 3
    shape = (ROWS, C)
    ends = last == 9
    return pl.pallas_call(
        kernel,
        out_shape=jax.ShapeDtypeStruct(shape, F32),
        in_specs=SMEM_SPEC + vmem_specs(len(operands)) + any_specs(4),
        out_specs=vmem_specs(1)[0],
        scratch_shapes=([pltpu.VMEM(shape, F32)] if ends else []) + tap_scratch(first, last),
        compiler_params=pltpu.CompilerParams(vmem_limit_bytes=VLIM),
        cost_estimate=cost(6 * ROWS * C * C, 8_000_000),
        name="spatial_backward_" + str(first),
    )(place, *operands, *pieces)


def halos(own):
    size = NX * NZL
    before = lax.ppermute(own[1], "frames", [(k, (k + 1) % size) for k in range(size)])
    after = lax.ppermute(own[0], "frames", [((k + 1) % size, k) for k in range(size)])
    return before, after


def gather_weights(place_x, spatial_weight, temporal_weight):
    x = place_x
    spatial = jnp.pad(spatial_weight, ((0, SPAD - SROWS), (0, 0)))
    temporal_rows = jnp.pad(temporal_weight, ((0, TPAD - TROWS), (0, 0)))
    quarter = jnp.concatenate(
        [
            lax.dynamic_slice_in_dim(spatial, x * SQ, SQ, 0),
            lax.dynamic_slice_in_dim(temporal_rows, x * TQ, TQ, 0),
        ]
    )
    return quarter


def per_device(
    latents,
    pose,
    timesteps,
    norm_gain,
    norm_bias,
    pose_table,
    time_weight,
    spatial_weight,
    temporal_weight,
    cotangent,
):
    frame_at = lax.axis_index("frames")
    row_at = lax.axis_index("dp")
    x = frame_at % NX
    y = row_at // (NZH * NC)
    zh = (row_at // NC) % NZH
    core = row_at % NC
    place = jnp.stack(
        [x, y, zh, core, frame_at > 0, frame_at < NX * NZL - 1], dtype=jnp.int32
    )

    quarter = gather_weights(x, spatial_weight, temporal_weight)
    came = [send(quarter, zh_step(k)) for k in (1, 2, 3)]
    cot_before, cot_after = halos(cotangent[0])
    *came, cot_before, cot_after = lax.optimization_barrier((*came, cot_before, cot_after))
    cot_frames = cot_before, cotangent.reshape(ROWS, C), cot_after
    column = in_order(quarter, came, zh)
    came = [send(column, xy_step(k)) for k in (1, 2, 3)]
    activated, normed, scale, inv_std = norm(
        latents.reshape(ROWS, C), pose[0], pose_table, norm_gain, norm_bias
    )
    activated_other = send(activated, core_swap)
    shift = time_shift(timesteps, time_weight)
    *came, activated_other, shift = lax.optimization_barrier((*came, activated_other, shift))
    low, high = jnp.stack([column, came[0]]), jnp.stack([came[1], came[2]])
    one_low, three_high = send(low, yx_step(1)), send(high, yx_step(3))
    one_high, three_low = send(high, yx_step(1)), send(low, yx_step(3))
    cols = columns(place, activated, activated_other)
    one_low, three_high, cols = lax.optimization_barrier((one_low, three_high, cols))
    two_low, two_high = send(one_low, yx_step(1)), send(three_high, yx_step(3))
    total, first_part, first_temporal = forward_first(
        cols, [low, high, one_low, one_high, three_low, three_high]
    )
    two_low, two_high, total = lax.optimization_barrier((two_low, two_high, total))
    part, part_other, last_part, last_temporal = forward_last(total, cols, [two_low, two_high])
    temporal_rows = [first_temporal, last_temporal]
    temporal_rows += [send(first_temporal, core_swap), send(last_temporal, core_swap)]
    came, *temporal_rows = lax.optimization_barrier((send(part_other, core_swap), *temporal_rows))
    spatial_out, moved, mine, other = grad_terms(place, shift, part, came, cot_frames)

    _, frames_dev, pixels, _ = latents.shape
    factor = 1.0 / math.sqrt(lax.axis_size("dp") * frames_dev * lax.axis_size("frames") * pixels)
    came = send(other, core_swap)
    held, *parts = split_first(place, mine, came)
    came = [send(part, yx_step(k + 1)) for k, part in enumerate(parts)]
    ready, frames_moved, _ = lax.optimization_barrier((spatial_out, moved, held))
    moved_before, moved_after = halos(frames_moved.reshape(2, PIX, C))
    back_spatial, weights = temporal_back(place, cot_frames, ready, temporal_rows)
    *came, back_spatial = lax.optimization_barrier((*came, back_spatial))

    held, *parts = split_second(place, held, came)
    came = [send(part, xy_step(k + 1)) for k, part in enumerate(parts)]
    moved_before, first_part, last_part, _ = lax.optimization_barrier(
        (moved_before, first_part, last_part, held)
    )
    pieces = [first_part, last_part, send(first_part, core_swap), send(last_part, core_swap)]
    mixed = temporal_ahead(place, (moved_before, moved, moved_after), spatial_out, weights)
    *came, mixed = lax.optimization_barrier((*came, mixed))

    held, *parts = split_third(place, held, came)
    came = [send(part, zh_step(k + 1)) for k, part in enumerate(parts)]
    ready, _ = lax.optimization_barrier((back_spatial, held))
    sums = backward_taps(backward_first_kernel, 0, place, [ready], pieces)
    *came, sums = lax.optimization_barrier((*came, sums))

    held = held + came[0] + came[1] + came[2]
    came = send(held, zl_swap)
    sums, _ = lax.optimization_barrier((sums, held))
    sums = backward_taps(backward_middle_kernel, 3, place, [ready, sums], pieces)
    came, sums = lax.optimization_barrier((came, sums))
    held = (held + came) * factor
    came = [send(held, x_step(k)) for k in (1, 2, 3)]
    sums, _ = lax.optimization_barrier((sums, held))
    latent_grad = backward_taps(
        backward_last_kernel, 6, place, [ready, sums, normed, scale, inv_std], pieces
    )
    *came, latent_grad = lax.optimization_barrier((*came, latent_grad))
    temporal_grad = in_order(held, came, x).reshape(TPAD, C)[:TROWS]
    shape = latents.shape
    return mixed.reshape(shape), latent_grad.reshape(shape), temporal_grad


def solution(mesh):
    placed = (
        P("dp", "frames", None, None),
        P("dp", "frames", None),
        P("dp"),
        P(),
        P(),
        P(),
        P(),
        P("dp", None),
        P("dp", None),
        P("dp", "frames", None, None),
    )
    return jax.shard_map(
        per_device,
        mesh=mesh,
        in_specs=placed,
        out_specs=(P("dp", "frames", None, None), P("dp", "frames", None, None), P("dp", None)),
        check_vma=False,
    )
```

```python
import math

import jax
import jax.numpy as jnp
from jax import lax
from jax.experimental import pallas as pl
from jax.experimental.pallas import tpu as pltpu
from jax.sharding import PartitionSpec as P

GROUP_CH = 40
HT = 9
WD = 16
PIX = HT * WD
C = 640
NX, NY, NZH, NZL, NC = 4, 4, 4, 2, 2
AXES = ("frames", "dp")
SROWS, SPAD, SQ = 180, 192, 48
TROWS, TPAD, TQ = 60, 64, 16
QROWS = SQ + TQ
ROWS = 2 * PIX
F32 = jnp.float32
BF16 = jnp.bfloat16
VLIM = 58 * 1024 * 1024


def coords():
    for zl in range(NZL):
        for x in range(NX):
            for y in range(NY):
                for zh in range(NZH):
                    for c in range(NC):
                        yield zl, x, y, zh, c


def index_of(zl, x, y, zh, c):
    return (zl * NX + x) * (NY * NZH * NC) + (y * NZH + zh) * NC + c


def routes(move):
    return [(index_of(*at), index_of(*move(*at))) for at in coords()]


def send(value, move):
    return lax.ppermute(value, AXES, routes(move))


def core_swap(zl, x, y, zh, c):
    return zl, x, y, zh, 1 - c


def zl_swap(zl, x, y, zh, c):
    return 1 - zl, x, y, zh, c


def zh_pair(k):
    return lambda zl, x, y, zh, c: (zl, x, y, zh ^ k, c)


def zh_step(k):
    return lambda zl, x, y, zh, c: (zl, x, y, (zh + k) % NZH, c)


def x_pair(k):
    return lambda zl, x, y, zh, c: (zl, x ^ k, y, zh, c)


def xy_step(k):
    return lambda zl, x, y, zh, c: (
        (zl, (x + k) % NX, y, zh, c) if c == 0 else (zl, x, (y + k) % NY, zh, c)
    )


def yx_step(k):
    return lambda zl, x, y, zh, c: (
        (zl, x, (y + k) % NY, zh, c) if c == 0 else (zl, (x + k) % NX, y, zh, c)
    )


def in_order(own, received, place):
    parts = [received[2], received[1], received[0], own]
    stacked = jnp.stack(parts + parts)
    return lax.dynamic_slice_in_dim(stacked, (3 - place) % 4, 4, axis=0)


def time_shift(timesteps, time_weight):
    half = time_weight.shape[0] // 2
    positions = jnp.arange(half, dtype=jnp.float32)
    frequencies = jnp.exp(-math.log(10000.0) * positions / half)
    angles = timesteps.astype(jnp.float32)[:, None] * frequencies[None, :]
    embedding = jnp.concatenate([jnp.cos(angles), jnp.sin(angles)], axis=-1)
    return jnp.dot(embedding, time_weight, precision=lax.Precision.HIGHEST)


FIRST_PART = (0, 1, 3)
LAST_PART = (2,)


def piece_of(pieces, own, far, near):
    if far in LAST_PART:
        return pieces[own * 2 + 1].at[LAST_PART.index(far), near]
    return pieces[own * 2].at[FIRST_PART.index(far), near]


def origin(place, own, far, near):
    x, y, core = place[0], place[1], place[3]
    flow = core if own == 0 else 1 - core
    from_y = lax.rem(y + 4 - jnp.where(flow == 0, far, near), 4)
    from_x = lax.rem(x + 4 - jnp.where(flow == 0, near, far), 4)
    return from_y, flow, from_x


def load_copies(place, pieces, whole, sems, rows):
    copies = []
    for own in (0, 1):
        for far in range(4):
            for near in range(4):
                from_y, flow, from_x = origin(place, own, far, near)
                copies.append(
                    pltpu.make_async_copy(
                        piece_of(pieces, own, far, near).at[:, pl.ds(0, rows), :],
                        whole.at[from_y, flow, :, pl.ds(pl.multiple_of(from_x * rows, rows), rows), :],
                        sems.at[len(copies)],
                    )
                )
    return copies


def conv_parts(cols, pieces, layout, rows, columns, kept, temporal_rows, sems):
    copies, keeps = [], []
    for k, far in enumerate(layout):
        copies.append(
            (
                pltpu.make_async_copy(pieces[2 * k], rows.at[k, pl.ds(0, 2)], sems.at[5 * k]),
                pltpu.make_async_copy(pieces[2 * k + 1], rows.at[k, pl.ds(2, 2)], sems.at[5 * k + 1]),
                pltpu.make_async_copy(
                    cols[0].at[far], columns.at[k, pl.ds(0, ROWS)], sems.at[5 * k + 2]
                ),
                pltpu.make_async_copy(
                    cols[1].at[far], columns.at[k, pl.ds(ROWS, ROWS)], sems.at[5 * k + 3]
                ),
            )
        )
        keeps.append(pltpu.make_async_copy(rows.at[k], kept.at[k], sems.at[5 * k + 4]))
    for group in copies:
        for copy in group:
            copy.start()
    for k, group in enumerate(copies):
        for copy in group:
            copy.wait()
        keeps[k].start()
        temporal_rows[k] = rows[k, :, :, pl.ds(SQ, TQ), :]
        yield jnp.dot(
            columns[k], rows[k].reshape(4 * NZH * QROWS, C), preferred_element_type=F32
        )
    for keep in keeps:
        keep.wait()


def forward_first_kernel(cols_own, cols_other, *rest):
    cols = cols_own, cols_other
    pieces, (total, kept, temporal_rows, rows, columns, sems) = rest[:6], rest[6:]
    parts = conv_parts(cols, pieces, FIRST_PART, rows, columns, kept, temporal_rows, sems)
    for k, product in enumerate(parts):
        if k == 0:
            total[...] = product
        else:
            total[...] += product


def forward_last_kernel(start, cols_own, cols_other, *rest):
    cols = cols_own, cols_other
    pieces, (own, other, kept, temporal_rows, rows, columns, sems) = rest[:2], rest[2:]
    for product in conv_parts(cols, pieces, LAST_PART, rows, columns, kept, temporal_rows, sems):
        own[...] = product[:ROWS] + start[pl.ds(0, ROWS), :]
        other[...] = product[ROWS:] + start[pl.ds(ROWS, ROWS), :]


def grad_kernel(place, shift, part, came, before, own, after, spatial_out, moved, mine, other, total):
    rounded = (part[...] + came[...] + shift[...]).astype(BF16)
    spatial_out[...] = rounded
    wide = rounded.astype(F32)
    left = (wide * jax.nn.sigmoid(wide)).astype(BF16)
    moved[...] = left
    core = place[3]
    right = jnp.concatenate(
        [neighbour_rows(place, before, own, after, 2 - tap) for tap in range(3)], axis=1
    )
    product = lax.dot_general(left, right, (((0,), (0,)), ((), ())), preferred_element_type=F32)
    for tap in range(3):
        total[pl.ds(tap * C, C), :] = product[:, tap * C : (tap + 1) * C]
    total[pl.ds(3 * C, 8), :] = jnp.zeros((8, C), F32)
    for block in range(32):
        spot = block // 2
        rows = total[pl.ds(block * TROWS, TPAD), :].astype(BF16)

        @pl.when(core == block % 2)
        def _():
            mine[spot // 4, spot % 4] = rows

        @pl.when(core != block % 2)
        def _():
            other[spot // 4, spot % 4] = rows


def neighbour_rows(place, before, own, after, tap):
    if tap == 1:
        return own[...]
    if tap == 0:
        edge = jnp.where(place[4] > 0, before[...], jnp.zeros((PIX, C), BF16))
        return jnp.concatenate([edge, own[pl.ds(0, PIX), :]], axis=0)
    edge = jnp.where(place[5] > 0, after[...], jnp.zeros((PIX, C), BF16))
    return jnp.concatenate([own[pl.ds(PIX, PIX), :], edge], axis=0)


def any_specs(count):
    return [pl.BlockSpec(memory_space=pl.ANY)] * count


def vmem_specs(count):
    return [pl.BlockSpec(memory_space=pltpu.VMEM)] * count


SMEM_SPEC = [pl.BlockSpec(memory_space=pltpu.SMEM)]


def cost(flops, moved):
    return pl.CostEstimate(flops=flops, bytes_accessed=moved, transcendentals=0)


def group_spread():
    group_r = lax.broadcasted_iota(jnp.int32, (C, C), 0) // GROUP_CH
    group_c = lax.broadcasted_iota(jnp.int32, (C, C), 1) // GROUP_CH
    return jnp.where(group_r == group_c, 1.0 / (PIX * GROUP_CH), 0.0).astype(F32)


def group_means(first, second, spread):
    both = jnp.concatenate([first, second, jnp.zeros((6, C), F32)], axis=0)
    return jnp.dot(both, spread, precision=lax.Precision.HIGHEST, preferred_element_type=F32)


def segments(core):
    found = {}
    for y in range(NY):
        for x in range(NX):
            parts = []
            for zh in range(NZH):
                block = (y * NZH + zh) * NC + core
                start = SROWS * block + SQ * x
                end = min(start + SQ, SROWS * (block + 1))
                lane = zh * QROWS
                while start < end:
                    tap, channel = divmod(start, C)
                    count = min(end - start, C - channel)
                    parts.append((lane, tap, channel, count))
                    start += count
                    lane += count
            found[y, x] = parts
    return found


def norm_kernel(latents, pose, table, gain, bias, activated, normed, scale, inv_std):
    kinds = lax.broadcasted_iota(jnp.int32, (table.shape[0], PIX), 0)
    gains = gain[...].reshape(1, C)
    biases = bias[...].reshape(1, C)
    spread = group_spread()
    for frame in range(2):
        rows = pl.ds(frame * PIX, PIX)
        onehot = (pose[pl.ds(frame, 1), :] == kinds).astype(F32)
        shifted = latents[rows, :].astype(F32) + lax.dot_general(
            onehot,
            table[...],
            (((0,), (0,)), ((), ())),
            precision=lax.Precision.HIGHEST,
            preferred_element_type=F32,
        )
        means = group_means(
            jnp.sum(shifted, axis=0, keepdims=True),
            jnp.sum(shifted * shifted, axis=0, keepdims=True),
            spread,
        )
        center = means[0:1]
        inverse = lax.rsqrt(means[1:2] - center * center + 1e-05)
        inv_std[pl.ds(frame, 1), :] = inverse
        unit = (shifted - center) * inverse
        normed[rows, :] = unit
        value = unit * gains + biases
        gate = jax.nn.sigmoid(value)
        scale[rows, :] = gate * (1.0 + value * (1.0 - gate)) * gains
        activated[rows, :] = (value * gate).astype(BF16)


def norm(latents, pose, table, gain, bias):
    return pl.pallas_call(
        norm_kernel,
        out_shape=(
            jax.ShapeDtypeStruct((ROWS, C), BF16),
            jax.ShapeDtypeStruct((ROWS, C), F32),
            jax.ShapeDtypeStruct((ROWS, C), F32),
            jax.ShapeDtypeStruct((2, C), F32),
        ),
        in_specs=vmem_specs(5),
        out_specs=tuple(vmem_specs(4)),
        compiler_params=pltpu.CompilerParams(vmem_limit_bytes=VLIM),
        cost_estimate=cost(500_000_000, 3_000_000),
        name="group_norm",
    )(latents, pose, table, gain, bias)


def columns_kernel(place, clip, cols, padded, chunk):
    at_x, at_y, core = place[0], place[1], place[3]
    column = lax.rem(lax.broadcasted_iota(jnp.int32, (PIX, C), 0), WD)
    for frame in range(2):
        active = clip[pl.ds(frame * PIX, PIX), :].astype(F32)
        for dx in range(3):
            if dx == 0:
                moved = jnp.where(column > 0, pltpu.roll(active, 1, 0), 0.0)
            elif dx == 1:
                moved = active
            else:
                moved = jnp.where(column < WD - 1, pltpu.roll(active, PIX - 1, 0), 0.0)
            padded[dx, frame, pl.ds(0, WD), :] = jnp.zeros((WD, C), BF16)
            padded[dx, frame, pl.ds(WD, PIX), :] = moved.astype(BF16)
            padded[dx, frame, pl.ds(WD + PIX, WD), :] = jnp.zeros((WD, C), BF16)
    chunk[...] = jnp.zeros_like(chunk)

    def lay_out(flow):
        for number, ((y, x), parts) in enumerate(segments(flow).items()):
            slot = number % 2
            if x == NX - 1:
                chunk[slot] = jnp.zeros((ROWS, NZH * QROWS), BF16)
            for lane, tap, channel, count in parts:
                dy, dx = divmod(tap, 3)
                for frame in range(2):
                    chunk[slot, frame * PIX : (frame + 1) * PIX, lane : lane + count] = padded[
                        dx, frame, dy * WD : dy * WD + PIX, channel : channel + count
                    ]
            far_y, far_x = lax.rem(at_y + 4 - y, 4), lax.rem(at_x + 4 - x, 4)
            far, near = (far_y, far_x) if flow == 0 else (far_x, far_y)
            cols[far, :, pl.ds(pl.multiple_of(near * 256, 256), 256)] = chunk[slot]

    pl.when(core == 0)(lambda: lay_out(0))
    pl.when(core != 0)(lambda: lay_out(1))


def columns(place, clip):
    return pl.pallas_call(
        columns_kernel,
        out_shape=jax.ShapeDtypeStruct((4, ROWS, 4 * NZH * QROWS), BF16),
        in_specs=SMEM_SPEC + vmem_specs(1),
        out_specs=vmem_specs(1)[0],
        scratch_shapes=[
            pltpu.VMEM((3, 2, PIX + 2 * WD, C), BF16),
            pltpu.VMEM((2, ROWS, NZH * QROWS), BF16),
        ],
        compiler_params=pltpu.CompilerParams(vmem_limit_bytes=VLIM),
        cost_estimate=cost(500_000_000, 4_000_000),
        name="window_columns",
    )(place, clip)


def forward_call(kernel, layout, outs, operands, cols, pieces, name):
    count = len(layout)
    return pl.pallas_call(
        kernel,
        out_shape=(jax.ShapeDtypeStruct(outs[0], F32),) * outs[1]
        + (
            jax.ShapeDtypeStruct((count, 4, NZH, QROWS, C), BF16),
            jax.ShapeDtypeStruct((count, 4, NZH, TQ, C), BF16),
        ),
        in_specs=vmem_specs(len(operands)) + any_specs(2 + len(pieces)),
        out_specs=tuple(vmem_specs(outs[1]) + any_specs(1) + vmem_specs(1)),
        scratch_shapes=[
            pltpu.VMEM((count, 4, NZH, QROWS, C), BF16),
            pltpu.VMEM((count, 2 * ROWS, 4 * NZH * QROWS), BF16),
            pltpu.SemaphoreType.DMA((5 * count,)),
        ],
        compiler_params=pltpu.CompilerParams(vmem_limit_bytes=VLIM),
        cost_estimate=cost(4 * ROWS * 1024 * count * C, 3_000_000 * count),
        name=name,
    )(*operands, *cols, *pieces)


def forward_first(cols, pieces):
    return forward_call(
        forward_first_kernel, FIRST_PART, ((2 * ROWS, C), 1), (), cols, pieces, "spatial_forward_first"
    )


def forward_last(start, cols, pieces):
    return forward_call(
        forward_last_kernel, LAST_PART, ((ROWS, C), 2), (start,), cols, pieces, "spatial_forward_last"
    )


def grad_terms(place, shift, part, came, cot_frames):
    shape = (NY, NZH, TPAD, C)
    return pl.pallas_call(
        grad_kernel,
        out_shape=(jax.ShapeDtypeStruct((ROWS, C), BF16),) * 2
        + (jax.ShapeDtypeStruct(shape, BF16),) * 2,
        in_specs=SMEM_SPEC + vmem_specs(6),
        out_specs=tuple(vmem_specs(4)),
        scratch_shapes=[pltpu.VMEM((3 * C + 8, C), F32)],
        compiler_params=pltpu.CompilerParams(vmem_limit_bytes=VLIM),
        cost_estimate=cost(2 * ROWS * 3 * C * C, 8_000_000),
        name="temporal_grad_terms",
    )(place, shift, part, came, *cot_frames)


def split_first_kernel(place, mine, came, own, *sends):
    x, y, core = place[0], place[1], place[3]

    @pl.when(core == 0)
    def _():
        for k in range(4):
            part = lax.rem(y + k, 4)
            value = (mine[part].astype(F32) + came[part].astype(F32)).reshape(4 * TPAD, C)
            if k == 0:
                own[...] = value
            else:
                sends[k - 1][...] = value.astype(BF16)

    @pl.when(core != 0)
    def _():
        for k in range(4):
            rows = pl.ds(pl.multiple_of(lax.rem(x + k, 4) * TQ, TQ), TQ)
            value = (mine[:, :, rows, :].astype(F32) + came[:, :, rows, :].astype(F32)).reshape(16 * TQ, C)
            if k == 0:
                own[...] = value
            else:
                sends[k - 1][...] = value.astype(BF16)


def split_first(place, mine, came):
    shape = (4 * TPAD, C)
    return pl.pallas_call(
        split_first_kernel,
        out_shape=(jax.ShapeDtypeStruct(shape, F32),) + (jax.ShapeDtypeStruct(shape, BF16),) * 3,
        in_specs=SMEM_SPEC + vmem_specs(2),
        out_specs=tuple(vmem_specs(4)),
        compiler_params=pltpu.CompilerParams(vmem_limit_bytes=VLIM),
        cost_estimate=cost(0, 4_000_000),
        name="grad_split_first",
    )(place, mine, came)


def split_second_kernel(place, held, first, second, third, own, *sends):
    x, y, core = place[0], place[1], place[3]
    own_sends = (own,) + tuple(sends)

    @pl.when(core == 0)
    def _():
        for k in range(4):
            for zh in range(NZH):
                start = zh * TPAD + lax.rem(x + k, 4) * TQ
                rows = pl.ds(pl.multiple_of(start, TQ), TQ)
                value = held[rows, :]
                for term in (first, second, third):
                    value += term[rows, :].astype(F32)
                own_sends[k][zh] = value

    @pl.when(core != 0)
    def _():
        for k in range(4):
            rows = pl.ds(pl.multiple_of(lax.rem(y + k, 4) * TPAD, TPAD), TPAD)
            value = held[rows, :]
            for term in (first, second, third):
                value += term[rows, :].astype(F32)
            own_sends[k][...] = value.reshape(NZH, TQ, C)


def split_second(place, held, terms):
    shape = (NZH, TQ, C)
    return pl.pallas_call(
        split_second_kernel,
        out_shape=(jax.ShapeDtypeStruct(shape, F32),) * 4,
        in_specs=SMEM_SPEC + vmem_specs(4),
        out_specs=tuple(vmem_specs(4)),
        compiler_params=pltpu.CompilerParams(vmem_limit_bytes=VLIM),
        cost_estimate=cost(0, 2_000_000),
        name="grad_split_second",
    )(place, held, *terms)


def split_third_kernel(place, held, first, second, third, keep, away):
    pair = place[2] // 2
    for k in range(2):
        for target, which in ((keep, pair), (away, 1 - pair)):
            part = 2 * which + k
            target[k] = held[part] + first[part] + second[part] + third[part]


def split_third(place, held, terms):
    return pl.pallas_call(
        split_third_kernel,
        out_shape=(jax.ShapeDtypeStruct((2, TQ, C), F32),) * 2,
        in_specs=SMEM_SPEC + vmem_specs(4),
        out_specs=tuple(vmem_specs(2)),
        cost_estimate=cost(0, 800_000),
        name="grad_split_third",
    )(place, held, *terms)


def slope_of(value):
    gate = jax.nn.sigmoid(value)
    return gate * (1.0 + value * (1.0 - gate))


def temporal_back_kernel(place, before, own, after, spatial_out, *rest):
    pieces, (back_spatial, weights, whole, wide, sems) = rest[:4], rest[4:]
    copies = load_copies(place, pieces, whole, sems, TQ)
    for copy in copies:
        copy.start()
    for copy in copies:
        copy.wait()
    for block in range(32):
        pair, core = divmod(block, 2)
        wide[pl.ds(block * TROWS, TPAD), :] = whole[pair // 4, core, pair % 4].astype(F32)
    back = jnp.zeros((ROWS, C), F32)
    for tap in range(3):
        weight = wide[pl.ds(tap * C, C), :].astype(BF16)
        weights[tap] = weight
        back += lax.dot_general(
            neighbour_rows(place, before, own, after, 2 - tap),
            weight,
            (((1,), (1,)), ((), ())),
            preferred_element_type=F32,
        )
    slope = slope_of(spatial_out[...].astype(F32))
    cot = own[...].astype(F32)
    back_spatial[...] = (cot + back * slope).astype(BF16)


def temporal_back(place, cot_frames, spatial_out, pieces):
    return pl.pallas_call(
        temporal_back_kernel,
        out_shape=(jax.ShapeDtypeStruct((ROWS, C), BF16), jax.ShapeDtypeStruct((3, C, C), BF16)),
        in_specs=SMEM_SPEC + vmem_specs(4) + any_specs(4),
        out_specs=tuple(vmem_specs(2)),
        scratch_shapes=[
            pltpu.VMEM((NY, NC, NZH, TPAD, C), BF16),
            pltpu.VMEM((3 * C + 8, C), F32),
            pltpu.SemaphoreType.DMA((32,)),
        ],
        compiler_params=pltpu.CompilerParams(vmem_limit_bytes=VLIM),
        cost_estimate=cost(6 * ROWS * C * C, 8_000_000),
        name="temporal_back",
    )(place, *cot_frames, spatial_out, *pieces)


def temporal_ahead_kernel(place, before, own, after, spatial_out, weights, mixed):
    ahead = spatial_out[...].astype(F32)
    for tap in range(3):
        ahead += jnp.dot(
            neighbour_rows(place, before, own, after, tap), weights[tap], preferred_element_type=F32
        )
    mixed[...] = ahead


def temporal_ahead(place, moved_frames, spatial_out, weights):
    return pl.pallas_call(
        temporal_ahead_kernel,
        out_shape=jax.ShapeDtypeStruct((ROWS, C), F32),
        in_specs=SMEM_SPEC + vmem_specs(5),
        out_specs=vmem_specs(1)[0],
        compiler_params=pltpu.CompilerParams(vmem_limit_bytes=VLIM),
        cost_estimate=cost(6 * ROWS * C * C, 5_000_000),
        name="temporal_ahead",
    )(place, *moved_frames, spatial_out, weights)


def tap_range(first, last):
    return first * C // SROWS, -(-last * C // SROWS)


def add_taps(dy, place, back_spatial, pieces, sums, whole, wide, sems):
    low, high = tap_range(3 * dy, 3 * dy + 3)
    first_y, last_y = low // (NZH * NC), (high - 1) // (NZH * NC)
    copies = load_copies(place, pieces, whole, sems, SQ)
    needed = []
    for own in (0, 1):
        for far in range(4):
            for near in range(4):
                from_y = origin(place, own, far, near)[0]
                needed.append(jnp.logical_and(from_y >= first_y, from_y <= last_y))
    for copy, need in zip(copies, needed):
        pl.when(need)(copy.start)
    for copy, need in zip(copies, needed):
        pl.when(need)(copy.wait)
    for block in range(low, high):
        pair, core = divmod(block, 2)
        wide[pl.ds((block - low) * SROWS, SPAD), :] = whole[pair // 4, core, pair % 4].astype(F32)
    column = lax.rem(lax.broadcasted_iota(jnp.int32, (ROWS, C), 0), WD)
    for dx in range(3):
        product = lax.dot_general(
            back_spatial[...],
            wide[pl.ds((3 * dy + dx) * C - low * SROWS, C), :].astype(BF16),
            (((1,), (1,)), ((), ())),
            preferred_element_type=F32,
        )
        if dx == 0:
            product = jnp.where(column < WD - 1, pltpu.roll(product, ROWS - 1, 0), 0.0)
        elif dx == 2:
            product = jnp.where(column > 0, pltpu.roll(product, 1, 0), 0.0)
        for frame in range(2):
            base = frame * PIX
            to = base + max(dy - 1, 0) * WD
            at = base + max(1 - dy, 0) * WD
            count = PIX - abs(dy - 1) * WD
            sums[pl.ds(to, count), :] += product[at : at + count, :]


def backward_first_kernel(place, back_spatial, *rest):
    pieces, (sums, whole, wide, sems) = rest[:4], rest[4:]
    sums[...] = jnp.zeros_like(sums)
    add_taps(0, place, back_spatial, pieces, sums, whole, wide, sems)


def backward_middle_kernel(place, back_spatial, start, *rest):
    pieces, (sums, whole, wide, sems) = rest[:4], rest[4:]
    sums[...] = start[...]
    add_taps(1, place, back_spatial, pieces, sums, whole, wide, sems)


def backward_last_kernel(place, back_spatial, start, normed, scale, inv_std, *rest):
    pieces, (latent_grad, sums, whole, wide, sems) = rest[:4], rest[4:]
    sums[...] = start[...]
    add_taps(2, place, back_spatial, pieces, sums, whole, wide, sems)
    spread = group_spread()
    for frame in range(2):
        rows = pl.ds(frame * PIX, PIX)
        back_normed = sums[rows, :] * scale[rows, :]
        unit = normed[rows, :]
        first = jnp.sum(back_normed, axis=0, keepdims=True)
        second = jnp.sum(back_normed * unit, axis=0, keepdims=True)
        means = group_means(first, second, spread)
        latent_grad[rows, :] = inv_std[pl.ds(frame, 1), :] * (
            back_normed - means[0:1] - unit * means[1:2]
        )


def tap_scratch(first, last):
    low, high = tap_range(first, last)
    return [
        pltpu.VMEM((NY, NC, NZH, SPAD, C), BF16),
        pltpu.VMEM(((high - low) * SROWS + 20, C), F32),
        pltpu.SemaphoreType.DMA((32,)),
    ]


def backward_taps(kernel, first, place, operands, pieces):
    last = first + 3
    shape = (ROWS, C)
    ends = last == 9
    return pl.pallas_call(
        kernel,
        out_shape=jax.ShapeDtypeStruct(shape, F32),
        in_specs=SMEM_SPEC + vmem_specs(len(operands)) + any_specs(4),
        out_specs=vmem_specs(1)[0],
        scratch_shapes=([pltpu.VMEM(shape, F32)] if ends else []) + tap_scratch(first, last),
        compiler_params=pltpu.CompilerParams(vmem_limit_bytes=VLIM),
        cost_estimate=cost(6 * ROWS * C * C, 8_000_000),
        name="spatial_backward_" + str(first),
    )(place, *operands, *pieces)


def halos(own):
    size = NX * NZL
    before = lax.ppermute(own[1], "frames", [(k, (k + 1) % size) for k in range(size)])
    after = lax.ppermute(own[0], "frames", [((k + 1) % size, k) for k in range(size)])
    return before, after


def gather_weights(place_x, spatial_weight, temporal_weight):
    x = place_x
    spatial = jnp.pad(spatial_weight, ((0, SPAD - SROWS), (0, 0)))
    temporal_rows = jnp.pad(temporal_weight, ((0, TPAD - TROWS), (0, 0)))
    quarter = jnp.concatenate(
        [
            lax.dynamic_slice_in_dim(spatial, x * SQ, SQ, 0),
            lax.dynamic_slice_in_dim(temporal_rows, x * TQ, TQ, 0),
        ]
    )
    return quarter


def per_device(
    latents,
    pose,
    timesteps,
    norm_gain,
    norm_bias,
    pose_table,
    time_weight,
    spatial_weight,
    temporal_weight,
    cotangent,
):
    frame_at = lax.axis_index("frames")
    row_at = lax.axis_index("dp")
    x = frame_at % NX
    y = row_at // (NZH * NC)
    zh = (row_at // NC) % NZH
    core = row_at % NC
    place = jnp.stack(
        [x, y, zh, core, frame_at > 0, frame_at < NX * NZL - 1], dtype=jnp.int32
    )

    quarter = gather_weights(x, spatial_weight, temporal_weight)
    came = [send(quarter, zh_step(k)) for k in (1, 2, 3)]
    column = in_order(quarter, came, zh)
    came = [send(column, xy_step(k)) for k in (1, 2, 3)]
    latents, _ = lax.optimization_barrier((latents, column))
    activated, normed, scale, inv_std = norm(
        latents.reshape(ROWS, C), pose[0], pose_table, norm_gain, norm_bias
    )
    activated_other = send(activated, core_swap)
    cot_own, _ = lax.optimization_barrier((cotangent, activated))
    cot_before, cot_after = halos(cot_own[0])
    cols_own = columns(place, activated)
    shift = time_shift(timesteps, time_weight)
    *came, activated_other, shift, cols_own, cot_before, cot_after = lax.optimization_barrier(
        (*came, activated_other, shift, cols_own, cot_before, cot_after)
    )
    cot_frames = cot_before, cotangent.reshape(ROWS, C), cot_after
    low, high = jnp.stack([column, came[0]]), jnp.stack([came[1], came[2]])
    one_low, three_high = send(low, yx_step(1)), send(high, yx_step(3))
    one_high, three_low = send(high, yx_step(1)), send(low, yx_step(3))
    activated_other, _ = lax.optimization_barrier((activated_other, low))
    cols_other = columns(place, activated_other)
    one_low, three_high, cols_other = lax.optimization_barrier((one_low, three_high, cols_other))
    cols = cols_own, cols_other
    two_low, two_high = send(one_low, yx_step(1)), send(three_high, yx_step(3))
    total, first_part, first_temporal = forward_first(
        cols, [low, high, one_low, one_high, three_low, three_high]
    )
    two_low, two_high, total = lax.optimization_barrier((two_low, two_high, total))
    part, part_other, last_part, last_temporal = forward_last(total, cols, [two_low, two_high])
    temporal_rows = [first_temporal, last_temporal]
    temporal_rows += [send(first_temporal, core_swap), send(last_temporal, core_swap)]
    came, *temporal_rows = lax.optimization_barrier((send(part_other, core_swap), *temporal_rows))
    spatial_out, moved, mine, other = grad_terms(place, shift, part, came, cot_frames)

    _, frames_dev, pixels, _ = latents.shape
    factor = 1.0 / math.sqrt(lax.axis_size("dp") * frames_dev * lax.axis_size("frames") * pixels)
    came = send(other, core_swap)
    held, *parts = split_first(place, mine, came)
    came = [send(part, yx_step(k + 1)) for k, part in enumerate(parts)]
    ready, frames_moved, _ = lax.optimization_barrier((spatial_out, moved, held))
    moved_before, moved_after = halos(frames_moved.reshape(2, PIX, C))
    back_spatial, weights = temporal_back(place, cot_frames, ready, temporal_rows)
    *came, back_spatial = lax.optimization_barrier((*came, back_spatial))

    held, *parts = split_second(place, held, came)
    came = [send(part, xy_step(k + 1)) for k, part in enumerate(parts)]
    first_part, last_part, _ = lax.optimization_barrier((first_part, last_part, held))
    pieces = [first_part, last_part, send(first_part, core_swap), send(last_part, core_swap)]

    keep, away = split_third(place, held, came)
    came = send(away, zh_pair(2))
    ready, _ = lax.optimization_barrier((back_spatial, keep))
    sums = backward_taps(backward_first_kernel, 0, place, [ready], pieces)
    came, sums = lax.optimization_barrier((came, sums))

    pair = keep + came
    held = lax.dynamic_index_in_dim(pair, zh % 2, keepdims=False)
    came = send(lax.dynamic_index_in_dim(pair, 1 - zh % 2, keepdims=False), zh_pair(1))
    sums, held = lax.optimization_barrier((sums, held))
    sums = backward_taps(backward_middle_kernel, 3, place, [ready, sums], pieces)
    came, sums = lax.optimization_barrier((came, sums))

    held = held + came
    came = send(held, zl_swap)
    moved_before, held = lax.optimization_barrier((moved_before, held))
    mixed = temporal_ahead(place, (moved_before, moved, moved_after), spatial_out, weights)
    came, mixed = lax.optimization_barrier((came, mixed))

    held = (held + came) * factor
    came = send(held, x_pair(1))
    sums, held = lax.optimization_barrier((sums, held))
    latent_grad = backward_taps(
        backward_last_kernel, 6, place, [ready, sums, normed, scale, inv_std], pieces
    )
    came, latent_grad = lax.optimization_barrier((came, latent_grad))
    lower = x % 2 == 0
    held = jnp.stack([jnp.where(lower, held, came), jnp.where(lower, came, held)])
    came = send(held, x_pair(2))
    lower = x < 2
    held = jnp.concatenate([jnp.where(lower, held, came), jnp.where(lower, came, held)])
    temporal_grad = held.reshape(TPAD, C)[:TROWS]
    shape = latents.shape
    return mixed.reshape(shape), latent_grad.reshape(shape), temporal_grad


def solution(mesh):
    placed = (
        P("dp", "frames", None, None),
        P("dp", "frames", None),
        P("dp"),
        P(),
        P(),
        P(),
        P(),
        P("dp", None),
        P("dp", None),
        P("dp", "frames", None, None),
    )
    return jax.shard_map(
        per_device,
        mesh=mesh,
        in_specs=placed,
        out_specs=(P("dp", "frames", None, None), P("dp", "frames", None, None), P("dp", None)),
        check_vma=False,
    )
```

```python
import math

import jax
import jax.numpy as jnp
from jax import lax
from jax.experimental import pallas as pl
from jax.experimental.pallas import tpu as pltpu
from jax.sharding import PartitionSpec as P

GROUP_CH = 40
HT = 9
WD = 16
PIX = HT * WD
C = 640
NX, NY, NZH, NZL, NC = 4, 4, 4, 2, 2
AXES = ("frames", "dp")
SROWS, SPAD, SQ = 180, 192, 48
TROWS, TPAD, TQ = 60, 64, 16
QROWS = SQ + TQ
ROWS = 2 * PIX
F32 = jnp.float32
BF16 = jnp.bfloat16
VLIM = 58 * 1024 * 1024


def coords():
    for zl in range(NZL):
        for x in range(NX):
            for y in range(NY):
                for zh in range(NZH):
                    for c in range(NC):
                        yield zl, x, y, zh, c


def index_of(zl, x, y, zh, c):
    return (zl * NX + x) * (NY * NZH * NC) + (y * NZH + zh) * NC + c


def routes(move):
    return [(index_of(*at), index_of(*move(*at))) for at in coords()]


def send(value, move):
    return lax.ppermute(value, AXES, routes(move))


def core_swap(zl, x, y, zh, c):
    return zl, x, y, zh, 1 - c


def zl_swap(zl, x, y, zh, c):
    return 1 - zl, x, y, zh, c


def zh_step(k):
    return lambda zl, x, y, zh, c: (zl, x, y, (zh + k) % NZH, c)


def x_step(k):
    return lambda zl, x, y, zh, c: (zl, (x + k) % NX, y, zh, c)


def xy_step(k):
    return lambda zl, x, y, zh, c: (
        (zl, (x + k) % NX, y, zh, c) if c == 0 else (zl, x, (y + k) % NY, zh, c)
    )


def yx_step(k):
    return lambda zl, x, y, zh, c: (
        (zl, x, (y + k) % NY, zh, c) if c == 0 else (zl, (x + k) % NX, y, zh, c)
    )


def in_order(own, received, place):
    parts = [received[2], received[1], received[0], own]
    stacked = jnp.stack(parts + parts)
    return lax.dynamic_slice_in_dim(stacked, (3 - place) % 4, 4, axis=0)


def time_shift(timesteps, time_weight):
    half = time_weight.shape[0] // 2
    positions = jnp.arange(half, dtype=jnp.float32)
    frequencies = jnp.exp(-math.log(10000.0) * positions / half)
    angles = timesteps.astype(jnp.float32)[:, None] * frequencies[None, :]
    embedding = jnp.concatenate([jnp.cos(angles), jnp.sin(angles)], axis=-1)
    return jnp.dot(embedding, time_weight, precision=lax.Precision.HIGHEST)


FIRST_PART = (0, 1, 3)
LAST_PART = (2,)


def piece_of(pieces, own, far, near):
    if far in LAST_PART:
        return pieces[own * 2 + 1].at[LAST_PART.index(far), near]
    return pieces[own * 2].at[FIRST_PART.index(far), near]


def origin(place, own, far, near):
    x, y, core = place[0], place[1], place[3]
    flow = core if own == 0 else 1 - core
    from_y = lax.rem(y + 4 - jnp.where(flow == 0, far, near), 4)
    from_x = lax.rem(x + 4 - jnp.where(flow == 0, near, far), 4)
    return from_y, flow, from_x


def load_copies(place, pieces, whole, sems, rows):
    copies = []
    for own in (0, 1):
        for far in range(4):
            for near in range(4):
                from_y, flow, from_x = origin(place, own, far, near)
                copies.append(
                    pltpu.make_async_copy(
                        piece_of(pieces, own, far, near).at[:, pl.ds(0, rows), :],
                        whole.at[from_y, flow, :, pl.ds(pl.multiple_of(from_x * rows, rows), rows), :],
                        sems.at[len(copies)],
                    )
                )
    return copies


def conv_parts(cols, pieces, layout, rows, columns, kept, temporal_rows, sems):
    copies, keeps = [], []
    for k, far in enumerate(layout):
        copies.append(
            (
                pltpu.make_async_copy(pieces[2 * k], rows.at[k, pl.ds(0, 2)], sems.at[5 * k]),
                pltpu.make_async_copy(pieces[2 * k + 1], rows.at[k, pl.ds(2, 2)], sems.at[5 * k + 1]),
                pltpu.make_async_copy(
                    cols[0].at[far], columns.at[k, pl.ds(0, ROWS)], sems.at[5 * k + 2]
                ),
                pltpu.make_async_copy(
                    cols[1].at[far], columns.at[k, pl.ds(ROWS, ROWS)], sems.at[5 * k + 3]
                ),
            )
        )
        keeps.append(pltpu.make_async_copy(rows.at[k], kept.at[k], sems.at[5 * k + 4]))
    for group in copies:
        for copy in group:
            copy.start()
    for k, group in enumerate(copies):
        for copy in group:
            copy.wait()
        keeps[k].start()
        temporal_rows[k] = rows[k, :, :, pl.ds(SQ, TQ), :]
        yield jnp.dot(
            columns[k], rows[k].reshape(4 * NZH * QROWS, C), preferred_element_type=F32
        )
    for keep in keeps:
        keep.wait()


def forward_first_kernel(cols_own, cols_other, *rest):
    cols = cols_own, cols_other
    pieces, (total, kept, temporal_rows, rows, columns, sems) = rest[:6], rest[6:]
    parts = conv_parts(cols, pieces, FIRST_PART, rows, columns, kept, temporal_rows, sems)
    for k, product in enumerate(parts):
        if k == 0:
            total[...] = product
        else:
            total[...] += product


def forward_last_kernel(start, cols_own, cols_other, *rest):
    cols = cols_own, cols_other
    pieces, (own, other, kept, temporal_rows, rows, columns, sems) = rest[:2], rest[2:]
    for product in conv_parts(cols, pieces, LAST_PART, rows, columns, kept, temporal_rows, sems):
        own[...] = product[:ROWS] + start[pl.ds(0, ROWS), :]
        other[...] = product[ROWS:] + start[pl.ds(ROWS, ROWS), :]


def grad_kernel(place, shift, part, came, before, own, after, spatial_out, moved, mine, other, total):
    rounded = (part[...] + came[...] + shift[...]).astype(BF16)
    spatial_out[...] = rounded
    wide = rounded.astype(F32)
    left = (wide * jax.nn.sigmoid(wide)).astype(BF16)
    moved[...] = left
    core = place[3]
    right = jnp.concatenate(
        [neighbour_rows(place, before, own, after, 2 - tap) for tap in range(3)], axis=1
    )
    product = lax.dot_general(left, right, (((0,), (0,)), ((), ())), preferred_element_type=F32)
    for tap in range(3):
        total[pl.ds(tap * C, C), :] = product[:, tap * C : (tap + 1) * C]
    total[pl.ds(3 * C, 8), :] = jnp.zeros((8, C), F32)
    for block in range(32):
        spot = block // 2
        rows = total[pl.ds(block * TROWS, TPAD), :].astype(BF16)

        @pl.when(core == block % 2)
        def _():
            mine[spot // 4, spot % 4] = rows

        @pl.when(core != block % 2)
        def _():
            other[spot // 4, spot % 4] = rows


def neighbour_rows(place, before, own, after, tap):
    if tap == 1:
        return own[...]
    if tap == 0:
        edge = jnp.where(place[4] > 0, before[...], jnp.zeros((PIX, C), BF16))
        return jnp.concatenate([edge, own[pl.ds(0, PIX), :]], axis=0)
    edge = jnp.where(place[5] > 0, after[...], jnp.zeros((PIX, C), BF16))
    return jnp.concatenate([own[pl.ds(PIX, PIX), :], edge], axis=0)


def any_specs(count):
    return [pl.BlockSpec(memory_space=pl.ANY)] * count


def vmem_specs(count):
    return [pl.BlockSpec(memory_space=pltpu.VMEM)] * count


SMEM_SPEC = [pl.BlockSpec(memory_space=pltpu.SMEM)]


def cost(flops, moved):
    return pl.CostEstimate(flops=flops, bytes_accessed=moved, transcendentals=0)


def group_spread():
    group_r = lax.broadcasted_iota(jnp.int32, (C, C), 0) // GROUP_CH
    group_c = lax.broadcasted_iota(jnp.int32, (C, C), 1) // GROUP_CH
    return jnp.where(group_r == group_c, 1.0 / (PIX * GROUP_CH), 0.0).astype(F32)


def group_means(first, second, spread):
    both = jnp.concatenate([first, second, jnp.zeros((6, C), F32)], axis=0)
    return jnp.dot(both, spread, precision=lax.Precision.HIGHEST, preferred_element_type=F32)


def segments(core):
    found = {}
    for y in range(NY):
        for x in range(NX):
            parts = []
            for zh in range(NZH):
                block = (y * NZH + zh) * NC + core
                start = SROWS * block + SQ * x
                end = min(start + SQ, SROWS * (block + 1))
                lane = zh * QROWS
                while start < end:
                    tap, channel = divmod(start, C)
                    count = min(end - start, C - channel)
                    parts.append((lane, tap, channel, count))
                    start += count
                    lane += count
            found[y, x] = parts
    return found


def norm_kernel(latents, pose, table, gain, bias, activated, normed, scale, inv_std):
    kinds = lax.broadcasted_iota(jnp.int32, (table.shape[0], PIX), 0)
    gains = gain[...].reshape(1, C)
    biases = bias[...].reshape(1, C)
    spread = group_spread()
    for frame in range(2):
        rows = pl.ds(frame * PIX, PIX)
        onehot = (pose[pl.ds(frame, 1), :] == kinds).astype(F32)
        shifted = latents[rows, :].astype(F32) + lax.dot_general(
            onehot,
            table[...],
            (((0,), (0,)), ((), ())),
            precision=lax.Precision.HIGHEST,
            preferred_element_type=F32,
        )
        means = group_means(
            jnp.sum(shifted, axis=0, keepdims=True),
            jnp.sum(shifted * shifted, axis=0, keepdims=True),
            spread,
        )
        center = means[0:1]
        inverse = lax.rsqrt(means[1:2] - center * center + 1e-05)
        inv_std[pl.ds(frame, 1), :] = inverse
        unit = (shifted - center) * inverse
        normed[rows, :] = unit
        value = unit * gains + biases
        gate = jax.nn.sigmoid(value)
        scale[rows, :] = gate * (1.0 + value * (1.0 - gate)) * gains
        activated[rows, :] = (value * gate).astype(BF16)


def norm(latents, pose, table, gain, bias):
    return pl.pallas_call(
        norm_kernel,
        out_shape=(
            jax.ShapeDtypeStruct((ROWS, C), BF16),
            jax.ShapeDtypeStruct((ROWS, C), F32),
            jax.ShapeDtypeStruct((ROWS, C), F32),
            jax.ShapeDtypeStruct((2, C), F32),
        ),
        in_specs=vmem_specs(5),
        out_specs=tuple(vmem_specs(4)),
        compiler_params=pltpu.CompilerParams(vmem_limit_bytes=VLIM),
        cost_estimate=cost(500_000_000, 3_000_000),
        name="group_norm",
    )(latents, pose, table, gain, bias)


def columns_kernel(place, clip, cols, padded, chunk):
    at_x, at_y, core = place[0], place[1], place[3]
    column = lax.rem(lax.broadcasted_iota(jnp.int32, (PIX, C), 0), WD)
    for frame in range(2):
        active = clip[pl.ds(frame * PIX, PIX), :].astype(F32)
        for dx in range(3):
            if dx == 0:
                moved = jnp.where(column > 0, pltpu.roll(active, 1, 0), 0.0)
            elif dx == 1:
                moved = active
            else:
                moved = jnp.where(column < WD - 1, pltpu.roll(active, PIX - 1, 0), 0.0)
            padded[dx, frame, pl.ds(0, WD), :] = jnp.zeros((WD, C), BF16)
            padded[dx, frame, pl.ds(WD, PIX), :] = moved.astype(BF16)
            padded[dx, frame, pl.ds(WD + PIX, WD), :] = jnp.zeros((WD, C), BF16)
    chunk[...] = jnp.zeros_like(chunk)

    def lay_out(flow):
        for number, ((y, x), parts) in enumerate(segments(flow).items()):
            slot = number % 2
            if x == NX - 1:
                chunk[slot] = jnp.zeros((ROWS, NZH * QROWS), BF16)
            for lane, tap, channel, count in parts:
                dy, dx = divmod(tap, 3)
                for frame in range(2):
                    chunk[slot, frame * PIX : (frame + 1) * PIX, lane : lane + count] = padded[
                        dx, frame, dy * WD : dy * WD + PIX, channel : channel + count
                    ]
            far_y, far_x = lax.rem(at_y + 4 - y, 4), lax.rem(at_x + 4 - x, 4)
            far, near = (far_y, far_x) if flow == 0 else (far_x, far_y)
            cols[far, :, pl.ds(pl.multiple_of(near * 256, 256), 256)] = chunk[slot]

    pl.when(core == 0)(lambda: lay_out(0))
    pl.when(core != 0)(lambda: lay_out(1))


def columns(place, clip):
    return pl.pallas_call(
        columns_kernel,
        out_shape=jax.ShapeDtypeStruct((4, ROWS, 4 * NZH * QROWS), BF16),
        in_specs=SMEM_SPEC + vmem_specs(1),
        out_specs=vmem_specs(1)[0],
        scratch_shapes=[
            pltpu.VMEM((3, 2, PIX + 2 * WD, C), BF16),
            pltpu.VMEM((2, ROWS, NZH * QROWS), BF16),
        ],
        compiler_params=pltpu.CompilerParams(vmem_limit_bytes=VLIM),
        cost_estimate=cost(500_000_000, 4_000_000),
        name="window_columns",
    )(place, clip)


def forward_call(kernel, layout, outs, operands, cols, pieces, name):
    count = len(layout)
    return pl.pallas_call(
        kernel,
        out_shape=(jax.ShapeDtypeStruct(outs[0], F32),) * outs[1]
        + (
            jax.ShapeDtypeStruct((count, 4, NZH, QROWS, C), BF16),
            jax.ShapeDtypeStruct((count, 4, NZH, TQ, C), BF16),
        ),
        in_specs=vmem_specs(len(operands)) + any_specs(2 + len(pieces)),
        out_specs=tuple(vmem_specs(outs[1]) + any_specs(1) + vmem_specs(1)),
        scratch_shapes=[
            pltpu.VMEM((count, 4, NZH, QROWS, C), BF16),
            pltpu.VMEM((count, 2 * ROWS, 4 * NZH * QROWS), BF16),
            pltpu.SemaphoreType.DMA((5 * count,)),
        ],
        compiler_params=pltpu.CompilerParams(vmem_limit_bytes=VLIM),
        cost_estimate=cost(4 * ROWS * 1024 * count * C, 3_000_000 * count),
        name=name,
    )(*operands, *cols, *pieces)


def forward_first(cols, pieces):
    return forward_call(
        forward_first_kernel, FIRST_PART, ((2 * ROWS, C), 1), (), cols, pieces, "spatial_forward_first"
    )


def forward_last(start, cols, pieces):
    return forward_call(
        forward_last_kernel, LAST_PART, ((ROWS, C), 2), (start,), cols, pieces, "spatial_forward_last"
    )


def grad_terms(place, shift, part, came, cot_frames):
    shape = (NY, NZH, TPAD, C)
    return pl.pallas_call(
        grad_kernel,
        out_shape=(jax.ShapeDtypeStruct((ROWS, C), BF16),) * 2
        + (jax.ShapeDtypeStruct(shape, BF16),) * 2,
        in_specs=SMEM_SPEC + vmem_specs(6),
        out_specs=tuple(vmem_specs(4)),
        scratch_shapes=[pltpu.VMEM((3 * C + 8, C), F32)],
        compiler_params=pltpu.CompilerParams(vmem_limit_bytes=VLIM),
        cost_estimate=cost(2 * ROWS * 3 * C * C, 8_000_000),
        name="temporal_grad_terms",
    )(place, shift, part, came, *cot_frames)


def split_first_kernel(place, mine, came, own, *sends):
    x, y, core = place[0], place[1], place[3]

    @pl.when(core == 0)
    def _():
        for k in range(4):
            part = lax.rem(y + k, 4)
            value = (mine[part].astype(F32) + came[part].astype(F32)).reshape(4 * TPAD, C)
            if k == 0:
                own[...] = value
            else:
                sends[k - 1][...] = value.astype(BF16)

    @pl.when(core != 0)
    def _():
        for k in range(4):
            rows = pl.ds(pl.multiple_of(lax.rem(x + k, 4) * TQ, TQ), TQ)
            value = (mine[:, :, rows, :].astype(F32) + came[:, :, rows, :].astype(F32)).reshape(16 * TQ, C)
            if k == 0:
                own[...] = value
            else:
                sends[k - 1][...] = value.astype(BF16)


def split_first(place, mine, came):
    shape = (4 * TPAD, C)
    return pl.pallas_call(
        split_first_kernel,
        out_shape=(jax.ShapeDtypeStruct(shape, F32),) + (jax.ShapeDtypeStruct(shape, BF16),) * 3,
        in_specs=SMEM_SPEC + vmem_specs(2),
        out_specs=tuple(vmem_specs(4)),
        compiler_params=pltpu.CompilerParams(vmem_limit_bytes=VLIM),
        cost_estimate=cost(0, 4_000_000),
        name="grad_split_first",
    )(place, mine, came)


def split_second_kernel(place, held, first, second, third, own, *sends):
    x, y, core = place[0], place[1], place[3]
    own_sends = (own,) + tuple(sends)

    @pl.when(core == 0)
    def _():
        for k in range(4):
            for zh in range(NZH):
                start = zh * TPAD + lax.rem(x + k, 4) * TQ
                rows = pl.ds(pl.multiple_of(start, TQ), TQ)
                value = held[rows, :]
                for term in (first, second, third):
                    value += term[rows, :].astype(F32)
                own_sends[k][zh] = value

    @pl.when(core != 0)
    def _():
        for k in range(4):
            rows = pl.ds(pl.multiple_of(lax.rem(y + k, 4) * TPAD, TPAD), TPAD)
            value = held[rows, :]
            for term in (first, second, third):
                value += term[rows, :].astype(F32)
            own_sends[k][...] = value.reshape(NZH, TQ, C)


def split_second(place, held, terms):
    shape = (NZH, TQ, C)
    return pl.pallas_call(
        split_second_kernel,
        out_shape=(jax.ShapeDtypeStruct(shape, F32),) * 4,
        in_specs=SMEM_SPEC + vmem_specs(4),
        out_specs=tuple(vmem_specs(4)),
        compiler_params=pltpu.CompilerParams(vmem_limit_bytes=VLIM),
        cost_estimate=cost(0, 2_000_000),
        name="grad_split_second",
    )(place, held, *terms)


def split_third_kernel(place, held, first, second, third, *parts):
    zh = place[2]
    for k in range(4):
        part = lax.rem(zh + k, 4)
        parts[k][...] = held[part] + first[part] + second[part] + third[part]


def split_third(place, held, terms):
    return pl.pallas_call(
        split_third_kernel,
        out_shape=(jax.ShapeDtypeStruct((TQ, C), F32),) * 4,
        in_specs=SMEM_SPEC + vmem_specs(4),
        out_specs=tuple(vmem_specs(4)),
        cost_estimate=cost(0, 800_000),
        name="grad_split_third",
    )(place, held, *terms)


def slope_of(value):
    gate = jax.nn.sigmoid(value)
    return gate * (1.0 + value * (1.0 - gate))


def temporal_back_kernel(place, before, own, after, spatial_out, *rest):
    pieces, (back_spatial, weights, whole, wide, sems) = rest[:4], rest[4:]
    copies = load_copies(place, pieces, whole, sems, TQ)
    for copy in copies:
        copy.start()
    for copy in copies:
        copy.wait()
    for block in range(32):
        pair, core = divmod(block, 2)
        wide[pl.ds(block * TROWS, TPAD), :] = whole[pair // 4, core, pair % 4].astype(F32)
    back = jnp.zeros((ROWS, C), F32)
    for tap in range(3):
        weight = wide[pl.ds(tap * C, C), :].astype(BF16)
        weights[tap] = weight
        back += lax.dot_general(
            neighbour_rows(place, before, own, after, 2 - tap),
            weight,
            (((1,), (1,)), ((), ())),
            preferred_element_type=F32,
        )
    slope = slope_of(spatial_out[...].astype(F32))
    cot = own[...].astype(F32)
    back_spatial[...] = (cot + back * slope).astype(BF16)


def temporal_back(place, cot_frames, spatial_out, pieces):
    return pl.pallas_call(
        temporal_back_kernel,
        out_shape=(jax.ShapeDtypeStruct((ROWS, C), BF16), jax.ShapeDtypeStruct((3, C, C), BF16)),
        in_specs=SMEM_SPEC + vmem_specs(4) + any_specs(4),
        out_specs=tuple(vmem_specs(2)),
        scratch_shapes=[
            pltpu.VMEM((NY, NC, NZH, TPAD, C), BF16),
            pltpu.VMEM((3 * C + 8, C), F32),
            pltpu.SemaphoreType.DMA((32,)),
        ],
        compiler_params=pltpu.CompilerParams(vmem_limit_bytes=VLIM),
        cost_estimate=cost(6 * ROWS * C * C, 8_000_000),
        name="temporal_back",
    )(place, *cot_frames, spatial_out, *pieces)


def temporal_ahead_kernel(place, before, own, after, spatial_out, weights, mixed):
    ahead = spatial_out[...].astype(F32)
    for tap in range(3):
        ahead += jnp.dot(
            neighbour_rows(place, before, own, after, tap), weights[tap], preferred_element_type=F32
        )
    mixed[...] = ahead


def temporal_ahead(place, moved_frames, spatial_out, weights):
    return pl.pallas_call(
        temporal_ahead_kernel,
        out_shape=jax.ShapeDtypeStruct((ROWS, C), F32),
        in_specs=SMEM_SPEC + vmem_specs(5),
        out_specs=vmem_specs(1)[0],
        compiler_params=pltpu.CompilerParams(vmem_limit_bytes=VLIM),
        cost_estimate=cost(6 * ROWS * C * C, 5_000_000),
        name="temporal_ahead",
    )(place, *moved_frames, spatial_out, weights)


def tap_range(first, last):
    return first * C // SROWS, -(-last * C // SROWS)


def add_taps(dy, place, back_spatial, pieces, sums, whole, wide, sems):
    low, high = tap_range(3 * dy, 3 * dy + 3)
    first_y, last_y = low // (NZH * NC), (high - 1) // (NZH * NC)
    copies = load_copies(place, pieces, whole, sems, SQ)
    needed = []
    for own in (0, 1):
        for far in range(4):
            for near in range(4):
                from_y = origin(place, own, far, near)[0]
                needed.append(jnp.logical_and(from_y >= first_y, from_y <= last_y))
    for copy, need in zip(copies, needed):
        pl.when(need)(copy.start)
    for copy, need in zip(copies, needed):
        pl.when(need)(copy.wait)
    for block in range(low, high):
        pair, core = divmod(block, 2)
        wide[pl.ds((block - low) * SROWS, SPAD), :] = whole[pair // 4, core, pair % 4].astype(F32)
    column = lax.rem(lax.broadcasted_iota(jnp.int32, (ROWS, C), 0), WD)
    for dx in range(3):
        product = lax.dot_general(
            back_spatial[...],
            wide[pl.ds((3 * dy + dx) * C - low * SROWS, C), :].astype(BF16),
            (((1,), (1,)), ((), ())),
            preferred_element_type=F32,
        )
        if dx == 0:
            product = jnp.where(column < WD - 1, pltpu.roll(product, ROWS - 1, 0), 0.0)
        elif dx == 2:
            product = jnp.where(column > 0, pltpu.roll(product, 1, 0), 0.0)
        for frame in range(2):
            base = frame * PIX
            to = base + max(dy - 1, 0) * WD
            at = base + max(1 - dy, 0) * WD
            count = PIX - abs(dy - 1) * WD
            sums[pl.ds(to, count), :] += product[at : at + count, :]


def backward_first_kernel(place, back_spatial, *rest):
    pieces, (sums, whole, wide, sems) = rest[:4], rest[4:]
    sums[...] = jnp.zeros_like(sums)
    add_taps(0, place, back_spatial, pieces, sums, whole, wide, sems)


def backward_middle_kernel(place, back_spatial, start, *rest):
    pieces, (sums, whole, wide, sems) = rest[:4], rest[4:]
    sums[...] = start[...]
    add_taps(1, place, back_spatial, pieces, sums, whole, wide, sems)


def backward_last_kernel(place, back_spatial, start, normed, scale, inv_std, *rest):
    pieces, (latent_grad, sums, whole, wide, sems) = rest[:4], rest[4:]
    sums[...] = start[...]
    add_taps(2, place, back_spatial, pieces, sums, whole, wide, sems)
    spread = group_spread()
    for frame in range(2):
        rows = pl.ds(frame * PIX, PIX)
        back_normed = sums[rows, :] * scale[rows, :]
        unit = normed[rows, :]
        first = jnp.sum(back_normed, axis=0, keepdims=True)
        second = jnp.sum(back_normed * unit, axis=0, keepdims=True)
        means = group_means(first, second, spread)
        latent_grad[rows, :] = inv_std[pl.ds(frame, 1), :] * (
            back_normed - means[0:1] - unit * means[1:2]
        )


def tap_scratch(first, last):
    low, high = tap_range(first, last)
    return [
        pltpu.VMEM((NY, NC, NZH, SPAD, C), BF16),
        pltpu.VMEM(((high - low) * SROWS + 20, C), F32),
        pltpu.SemaphoreType.DMA((32,)),
    ]


def backward_taps(kernel, first, place, operands, pieces):
    last = first + 3
    shape = (ROWS, C)
    ends = last == 9
    return pl.pallas_call(
        kernel,
        out_shape=jax.ShapeDtypeStruct(shape, F32),
        in_specs=SMEM_SPEC + vmem_specs(len(operands)) + any_specs(4),
        out_specs=vmem_specs(1)[0],
        scratch_shapes=([pltpu.VMEM(shape, F32)] if ends else []) + tap_scratch(first, last),
        compiler_params=pltpu.CompilerParams(vmem_limit_bytes=VLIM),
        cost_estimate=cost(6 * ROWS * C * C, 8_000_000),
        name="spatial_backward_" + str(first),
    )(place, *operands, *pieces)


def frame_before(last):
    size = NX * NZL
    return lax.ppermute(last, "frames", [(k, (k + 1) % size) for k in range(size)])


def frame_after(first):
    size = NX * NZL
    return lax.ppermute(first, "frames", [((k + 1) % size, k) for k in range(size)])


def halos(own):
    return frame_before(own[1]), frame_after(own[0])


def gather_weights(place_x, spatial_weight, temporal_weight):
    x = place_x
    spatial = jnp.pad(spatial_weight, ((0, SPAD - SROWS), (0, 0)))
    temporal_rows = jnp.pad(temporal_weight, ((0, TPAD - TROWS), (0, 0)))
    quarter = jnp.concatenate(
        [
            lax.dynamic_slice_in_dim(spatial, x * SQ, SQ, 0),
            lax.dynamic_slice_in_dim(temporal_rows, x * TQ, TQ, 0),
        ]
    )
    return quarter


def per_device(
    latents,
    pose,
    timesteps,
    norm_gain,
    norm_bias,
    pose_table,
    time_weight,
    spatial_weight,
    temporal_weight,
    cotangent,
):
    frame_at = lax.axis_index("frames")
    row_at = lax.axis_index("dp")
    x = frame_at % NX
    y = row_at // (NZH * NC)
    zh = (row_at // NC) % NZH
    core = row_at % NC
    place = jnp.stack(
        [x, y, zh, core, frame_at > 0, frame_at < NX * NZL - 1], dtype=jnp.int32
    )

    quarter = gather_weights(x, spatial_weight, temporal_weight)
    came = [send(quarter, zh_step(k)) for k in (1, 2, 3)]
    column = in_order(quarter, came, zh)
    came = [send(column, xy_step(k)) for k in (1, 2, 3)]
    activated, normed, scale, inv_std = norm(
        latents.reshape(ROWS, C), pose[0], pose_table, norm_gain, norm_bias
    )
    activated_other = send(activated, core_swap)
    shift = time_shift(timesteps, time_weight)
    cot_first, cot_last = cotangent[0, 0], cotangent[0, 1]
    activated, cot_last, activated_other, column = lax.optimization_barrier(
        (activated, cot_last, activated_other, column)
    )
    cols_own = columns(place, activated)
    cot_before = frame_before(cot_last)
    *came, shift, cols_own, cot_before = lax.optimization_barrier(
        (*came, shift, cols_own, cot_before)
    )
    low, high = jnp.stack([column, came[0]]), jnp.stack([came[1], came[2]])
    one_low, three_high = send(low, yx_step(1)), send(high, yx_step(3))
    one_high, three_low = send(high, yx_step(1)), send(low, yx_step(3))
    activated_other, cot_first, _ = lax.optimization_barrier((activated_other, cot_first, low))
    cot_after = frame_after(cot_first)
    cols_other = columns(place, activated_other)
    one_low, three_high, cols_other, cot_after = lax.optimization_barrier(
        (one_low, three_high, cols_other, cot_after)
    )
    cot_frames = cot_before, cotangent.reshape(ROWS, C), cot_after
    cols = cols_own, cols_other
    two_low, two_high = send(one_low, yx_step(1)), send(three_high, yx_step(3))
    total, first_part, first_temporal = forward_first(
        cols, [low, high, one_low, one_high, three_low, three_high]
    )
    two_low, two_high, total = lax.optimization_barrier((two_low, two_high, total))
    part, part_other, last_part, last_temporal = forward_last(total, cols, [two_low, two_high])
    temporal_rows = [first_temporal, last_temporal]
    temporal_rows += [send(first_temporal, core_swap), send(last_temporal, core_swap)]
    came, *temporal_rows = lax.optimization_barrier((send(part_other, core_swap), *temporal_rows))
    spatial_out, moved, mine, other = grad_terms(place, shift, part, came, cot_frames)

    _, frames_dev, pixels, _ = latents.shape
    factor = 1.0 / math.sqrt(lax.axis_size("dp") * frames_dev * lax.axis_size("frames") * pixels)
    came = send(other, core_swap)
    held, *parts = split_first(place, mine, came)
    came = [send(part, yx_step(k + 1)) for k, part in enumerate(parts)]
    ready, frames_moved, _ = lax.optimization_barrier((spatial_out, moved, held))
    moved_before, moved_after = halos(frames_moved.reshape(2, PIX, C))
    back_spatial, weights = temporal_back(place, cot_frames, ready, temporal_rows)
    *came, back_spatial, moved_before, moved_after = lax.optimization_barrier(
        (*came, back_spatial, moved_before, moved_after)
    )

    held, *parts = split_second(place, held, came)
    came = [send(part, xy_step(k + 1)) for k, part in enumerate(parts)]
    moved_before, first_part, last_part, _ = lax.optimization_barrier(
        (moved_before, first_part, last_part, held)
    )
    mixed = temporal_ahead(place, (moved_before, moved, moved_after), spatial_out, weights)
    pieces = [first_part, last_part, send(first_part, core_swap), send(last_part, core_swap)]
    *came, mixed = lax.optimization_barrier((*came, mixed))

    held, *parts = split_third(place, held, came)
    came = [send(part, zh_step(k + 1)) for k, part in enumerate(parts)]
    ready, _ = lax.optimization_barrier((back_spatial, held))
    sums = backward_taps(backward_first_kernel, 0, place, [ready], pieces)
    *came, sums = lax.optimization_barrier((*came, sums))

    held = held + came[0] + came[1] + came[2]
    came = send(held, zl_swap)
    sums, _ = lax.optimization_barrier((sums, held))
    sums = backward_taps(backward_middle_kernel, 3, place, [ready, sums], pieces)
    came, sums = lax.optimization_barrier((came, sums))
    held = (held + came) * factor
    came = [send(held, x_step(k)) for k in (1, 2, 3)]
    sums, _ = lax.optimization_barrier((sums, held))
    latent_grad = backward_taps(
        backward_last_kernel, 6, place, [ready, sums, normed, scale, inv_std], pieces
    )
    *came, latent_grad = lax.optimization_barrier((*came, latent_grad))
    temporal_grad = in_order(held, came, x).reshape(TPAD, C)[:TROWS]
    shape = latents.shape
    return mixed.reshape(shape), latent_grad.reshape(shape), temporal_grad


def solution(mesh):
    placed = (
        P("dp", "frames", None, None),
        P("dp", "frames", None),
        P("dp"),
        P(),
        P(),
        P(),
        P(),
        P("dp", None),
        P("dp", None),
        P("dp", "frames", None, None),
    )
    return jax.shard_map(
        per_device,
        mesh=mesh,
        in_specs=placed,
        out_specs=(P("dp", "frames", None, None), P("dp", "frames", None, None), P("dp", None)),
        check_vma=False,
    )
```

```python
import math

import jax
import jax.numpy as jnp
from jax import lax
from jax.experimental import pallas as pl
from jax.experimental.pallas import tpu as pltpu
from jax.sharding import PartitionSpec as P

GROUP_CH = 40
HT = 9
WD = 16
PIX = HT * WD
C = 640
NX, NY, NZH, NZL, NC = 4, 4, 4, 2, 2
AXES = ("frames", "dp")
SROWS, SPAD, SQ = 180, 192, 48
TROWS, TPAD, TQ = 60, 64, 16
QROWS = SQ + TQ
ROWS = 2 * PIX
F32 = jnp.float32
BF16 = jnp.bfloat16
VLIM = 58 * 1024 * 1024


def coords():
    for zl in range(NZL):
        for x in range(NX):
            for y in range(NY):
                for zh in range(NZH):
                    for c in range(NC):
                        yield zl, x, y, zh, c


def index_of(zl, x, y, zh, c):
    return (zl * NX + x) * (NY * NZH * NC) + (y * NZH + zh) * NC + c


def routes(move):
    return [(index_of(*at), index_of(*move(*at))) for at in coords()]


def send(value, move):
    return lax.ppermute(value, AXES, routes(move))


def core_swap(zl, x, y, zh, c):
    return zl, x, y, zh, 1 - c


def zl_swap(zl, x, y, zh, c):
    return 1 - zl, x, y, zh, c


def zh_step(k):
    return lambda zl, x, y, zh, c: (zl, x, y, (zh + k) % NZH, c)


def x_step(k):
    return lambda zl, x, y, zh, c: (zl, (x + k) % NX, y, zh, c)


def xy_step(k):
    return lambda zl, x, y, zh, c: (
        (zl, (x + k) % NX, y, zh, c) if c == 0 else (zl, x, (y + k) % NY, zh, c)
    )


def yx_step(k):
    return lambda zl, x, y, zh, c: (
        (zl, x, (y + k) % NY, zh, c) if c == 0 else (zl, (x + k) % NX, y, zh, c)
    )


def in_order(own, received, place):
    parts = [received[2], received[1], received[0], own]
    stacked = jnp.stack(parts + parts)
    return lax.dynamic_slice_in_dim(stacked, (3 - place) % 4, 4, axis=0)


def time_shift(timesteps, time_weight):
    half = time_weight.shape[0] // 2
    positions = jnp.arange(half, dtype=jnp.float32)
    frequencies = jnp.exp(-math.log(10000.0) * positions / half)
    angles = timesteps.astype(jnp.float32)[:, None] * frequencies[None, :]
    embedding = jnp.concatenate([jnp.cos(angles), jnp.sin(angles)], axis=-1)
    return jnp.dot(embedding, time_weight, precision=lax.Precision.HIGHEST)


FIRST_PART = (0, 1, 3)
LAST_PART = (2,)


def piece_of(pieces, own, far, near):
    if far in LAST_PART:
        return pieces[own * 2 + 1].at[LAST_PART.index(far), near]
    return pieces[own * 2].at[FIRST_PART.index(far), near]


def origin(place, own, far, near):
    x, y, core = place[0], place[1], place[3]
    flow = core if own == 0 else 1 - core
    from_y = lax.rem(y + 4 - jnp.where(flow == 0, far, near), 4)
    from_x = lax.rem(x + 4 - jnp.where(flow == 0, near, far), 4)
    return from_y, flow, from_x


def load_copies(place, pieces, whole, sems, rows):
    copies = []
    for own in (0, 1):
        for far in range(4):
            for near in range(4):
                from_y, flow, from_x = origin(place, own, far, near)
                copies.append(
                    pltpu.make_async_copy(
                        piece_of(pieces, own, far, near).at[:, pl.ds(0, rows), :],
                        whole.at[from_y, flow, :, pl.ds(pl.multiple_of(from_x * rows, rows), rows), :],
                        sems.at[len(copies)],
                    )
                )
    return copies


def conv_parts(cols, pieces, layout, rows, columns, kept, temporal_rows, sems):
    copies, keeps = [], []
    for k, far in enumerate(layout):
        copies.append(
            (
                pltpu.make_async_copy(pieces[2 * k], rows.at[k, pl.ds(0, 2)], sems.at[5 * k]),
                pltpu.make_async_copy(pieces[2 * k + 1], rows.at[k, pl.ds(2, 2)], sems.at[5 * k + 1]),
                pltpu.make_async_copy(
                    cols[0].at[far], columns.at[k, pl.ds(0, ROWS)], sems.at[5 * k + 2]
                ),
                pltpu.make_async_copy(
                    cols[1].at[far], columns.at[k, pl.ds(ROWS, ROWS)], sems.at[5 * k + 3]
                ),
            )
        )
        keeps.append(pltpu.make_async_copy(rows.at[k], kept.at[k], sems.at[5 * k + 4]))
    for group in copies:
        for copy in group:
            copy.start()
    for k, group in enumerate(copies):
        for copy in group:
            copy.wait()
        keeps[k].start()
        temporal_rows[k] = rows[k, :, :, pl.ds(SQ, TQ), :]
        yield jnp.dot(
            columns[k], rows[k].reshape(4 * NZH * QROWS, C), preferred_element_type=F32
        )
    for keep in keeps:
        keep.wait()


def forward_first_kernel(cols_own, cols_other, *rest):
    cols = cols_own, cols_other
    pieces, (total, kept, temporal_rows, rows, columns, sems) = rest[:6], rest[6:]
    parts = conv_parts(cols, pieces, FIRST_PART, rows, columns, kept, temporal_rows, sems)
    for k, product in enumerate(parts):
        if k == 0:
            total[...] = product
        else:
            total[...] += product


def forward_last_kernel(start, cols_own, cols_other, *rest):
    cols = cols_own, cols_other
    pieces, (own, other, kept, temporal_rows, rows, columns, sems) = rest[:2], rest[2:]
    for product in conv_parts(cols, pieces, LAST_PART, rows, columns, kept, temporal_rows, sems):
        own[...] = product[:ROWS] + start[pl.ds(0, ROWS), :]
        other[...] = product[ROWS:] + start[pl.ds(ROWS, ROWS), :]


def grad_kernel(place, shift, part, came, before, own, after, spatial_out, moved, mine, other, total):
    rounded = (part[...] + came[...] + shift[...]).astype(BF16)
    spatial_out[...] = rounded
    wide = rounded.astype(F32)
    left = (wide * jax.nn.sigmoid(wide)).astype(BF16)
    moved[...] = left
    core = place[3]
    right = jnp.concatenate(
        [neighbour_rows(place, before, own, after, 2 - tap) for tap in range(3)], axis=1
    )
    product = lax.dot_general(left, right, (((0,), (0,)), ((), ())), preferred_element_type=F32)
    for tap in range(3):
        total[pl.ds(tap * C, C), :] = product[:, tap * C : (tap + 1) * C]
    total[pl.ds(3 * C, 8), :] = jnp.zeros((8, C), F32)
    for block in range(32):
        spot = block // 2
        rows = total[pl.ds(block * TROWS, TPAD), :].astype(BF16)

        @pl.when(core == block % 2)
        def _():
            mine[spot // 4, spot % 4] = rows

        @pl.when(core != block % 2)
        def _():
            other[spot // 4, spot % 4] = rows


def neighbour_rows(place, before, own, after, tap):
    if tap == 1:
        return own[...]
    if tap == 0:
        edge = jnp.where(place[4] > 0, before[...], jnp.zeros((PIX, C), BF16))
        return jnp.concatenate([edge, own[pl.ds(0, PIX), :]], axis=0)
    edge = jnp.where(place[5] > 0, after[...], jnp.zeros((PIX, C), BF16))
    return jnp.concatenate([own[pl.ds(PIX, PIX), :], edge], axis=0)


def any_specs(count):
    return [pl.BlockSpec(memory_space=pl.ANY)] * count


def vmem_specs(count):
    return [pl.BlockSpec(memory_space=pltpu.VMEM)] * count


SMEM_SPEC = [pl.BlockSpec(memory_space=pltpu.SMEM)]


def cost(flops, moved):
    return pl.CostEstimate(flops=flops, bytes_accessed=moved, transcendentals=0)


def group_spread():
    group_r = lax.broadcasted_iota(jnp.int32, (C, C), 0) // GROUP_CH
    group_c = lax.broadcasted_iota(jnp.int32, (C, C), 1) // GROUP_CH
    return jnp.where(group_r == group_c, 1.0 / (PIX * GROUP_CH), 0.0).astype(F32)


def group_means(first, second, spread):
    both = jnp.concatenate([first, second, jnp.zeros((6, C), F32)], axis=0)
    return jnp.dot(both, spread, precision=lax.Precision.HIGHEST, preferred_element_type=F32)


def segments(core):
    found = {}
    for y in range(NY):
        for x in range(NX):
            parts = []
            for zh in range(NZH):
                block = (y * NZH + zh) * NC + core
                start = SROWS * block + SQ * x
                end = min(start + SQ, SROWS * (block + 1))
                lane = zh * QROWS
                while start < end:
                    tap, channel = divmod(start, C)
                    count = min(end - start, C - channel)
                    parts.append((lane, tap, channel, count))
                    start += count
                    lane += count
            found[y, x] = parts
    return found


def norm_kernel(latents, pose, table, gain, bias, activated, normed, scale, inv_std):
    kinds = lax.broadcasted_iota(jnp.int32, (table.shape[0], PIX), 0)
    gains = gain[...].reshape(1, C)
    biases = bias[...].reshape(1, C)
    spread = group_spread()
    for frame in range(2):
        rows = pl.ds(frame * PIX, PIX)
        onehot = (pose[pl.ds(frame, 1), :] == kinds).astype(F32)
        shifted = latents[rows, :].astype(F32) + lax.dot_general(
            onehot,
            table[...],
            (((0,), (0,)), ((), ())),
            precision=lax.Precision.HIGHEST,
            preferred_element_type=F32,
        )
        means = group_means(
            jnp.sum(shifted, axis=0, keepdims=True),
            jnp.sum(shifted * shifted, axis=0, keepdims=True),
            spread,
        )
        center = means[0:1]
        inverse = lax.rsqrt(means[1:2] - center * center + 1e-05)
        inv_std[pl.ds(frame, 1), :] = inverse
        unit = (shifted - center) * inverse
        normed[rows, :] = unit
        value = unit * gains + biases
        gate = jax.nn.sigmoid(value)
        scale[rows, :] = gate * (1.0 + value * (1.0 - gate)) * gains
        activated[rows, :] = (value * gate).astype(BF16)


def norm(latents, pose, table, gain, bias):
    return pl.pallas_call(
        norm_kernel,
        out_shape=(
            jax.ShapeDtypeStruct((ROWS, C), BF16),
            jax.ShapeDtypeStruct((ROWS, C), F32),
            jax.ShapeDtypeStruct((ROWS, C), F32),
            jax.ShapeDtypeStruct((2, C), F32),
        ),
        in_specs=vmem_specs(5),
        out_specs=tuple(vmem_specs(4)),
        compiler_params=pltpu.CompilerParams(vmem_limit_bytes=VLIM),
        cost_estimate=cost(500_000_000, 3_000_000),
        name="group_norm",
    )(latents, pose, table, gain, bias)


def columns_kernel(place, clip, cols, padded, chunk):
    at_x, at_y, core = place[0], place[1], place[3]
    column = lax.rem(lax.broadcasted_iota(jnp.int32, (PIX, C), 0), WD)
    for frame in range(2):
        active = clip[pl.ds(frame * PIX, PIX), :].astype(F32)
        for dx in range(3):
            if dx == 0:
                moved = jnp.where(column > 0, pltpu.roll(active, 1, 0), 0.0)
            elif dx == 1:
                moved = active
            else:
                moved = jnp.where(column < WD - 1, pltpu.roll(active, PIX - 1, 0), 0.0)
            padded[dx, frame, pl.ds(0, WD), :] = jnp.zeros((WD, C), BF16)
            padded[dx, frame, pl.ds(WD, PIX), :] = moved.astype(BF16)
            padded[dx, frame, pl.ds(WD + PIX, WD), :] = jnp.zeros((WD, C), BF16)
    chunk[...] = jnp.zeros_like(chunk)

    def lay_out(flow):
        for number, ((y, x), parts) in enumerate(segments(flow).items()):
            slot = number % 2
            if x == NX - 1:
                chunk[slot] = jnp.zeros((ROWS, NZH * QROWS), BF16)
            for lane, tap, channel, count in parts:
                dy, dx = divmod(tap, 3)
                for frame in range(2):
                    chunk[slot, frame * PIX : (frame + 1) * PIX, lane : lane + count] = padded[
                        dx, frame, dy * WD : dy * WD + PIX, channel : channel + count
                    ]
            far_y, far_x = lax.rem(at_y + 4 - y, 4), lax.rem(at_x + 4 - x, 4)
            far, near = (far_y, far_x) if flow == 0 else (far_x, far_y)
            cols[far, :, pl.ds(pl.multiple_of(near * 256, 256), 256)] = chunk[slot]

    pl.when(core == 0)(lambda: lay_out(0))
    pl.when(core != 0)(lambda: lay_out(1))


def columns(place, clip):
    return pl.pallas_call(
        columns_kernel,
        out_shape=jax.ShapeDtypeStruct((4, ROWS, 4 * NZH * QROWS), BF16),
        in_specs=SMEM_SPEC + vmem_specs(1),
        out_specs=vmem_specs(1)[0],
        scratch_shapes=[
            pltpu.VMEM((3, 2, PIX + 2 * WD, C), BF16),
            pltpu.VMEM((2, ROWS, NZH * QROWS), BF16),
        ],
        compiler_params=pltpu.CompilerParams(vmem_limit_bytes=VLIM),
        cost_estimate=cost(500_000_000, 4_000_000),
        name="window_columns",
    )(place, clip)


def forward_call(kernel, layout, outs, operands, cols, pieces, name):
    count = len(layout)
    return pl.pallas_call(
        kernel,
        out_shape=(jax.ShapeDtypeStruct(outs[0], F32),) * outs[1]
        + (
            jax.ShapeDtypeStruct((count, 4, NZH, QROWS, C), BF16),
            jax.ShapeDtypeStruct((count, 4, NZH, TQ, C), BF16),
        ),
        in_specs=vmem_specs(len(operands)) + any_specs(2 + len(pieces)),
        out_specs=tuple(vmem_specs(outs[1]) + any_specs(1) + vmem_specs(1)),
        scratch_shapes=[
            pltpu.VMEM((count, 4, NZH, QROWS, C), BF16),
            pltpu.VMEM((count, 2 * ROWS, 4 * NZH * QROWS), BF16),
            pltpu.SemaphoreType.DMA((5 * count,)),
        ],
        compiler_params=pltpu.CompilerParams(vmem_limit_bytes=VLIM),
        cost_estimate=cost(4 * ROWS * 1024 * count * C, 3_000_000 * count),
        name=name,
    )(*operands, *cols, *pieces)


def forward_first(cols, pieces):
    return forward_call(
        forward_first_kernel, FIRST_PART, ((2 * ROWS, C), 1), (), cols, pieces, "spatial_forward_first"
    )


def forward_last(start, cols, pieces):
    return forward_call(
        forward_last_kernel, LAST_PART, ((ROWS, C), 2), (start,), cols, pieces, "spatial_forward_last"
    )


def grad_terms(place, shift, part, came, cot_frames):
    shape = (NY, NZH, TPAD, C)
    return pl.pallas_call(
        grad_kernel,
        out_shape=(jax.ShapeDtypeStruct((ROWS, C), BF16),) * 2
        + (jax.ShapeDtypeStruct(shape, BF16),) * 2,
        in_specs=SMEM_SPEC + vmem_specs(6),
        out_specs=tuple(vmem_specs(4)),
        scratch_shapes=[pltpu.VMEM((3 * C + 8, C), F32)],
        compiler_params=pltpu.CompilerParams(vmem_limit_bytes=VLIM),
        cost_estimate=cost(2 * ROWS * 3 * C * C, 8_000_000),
        name="temporal_grad_terms",
    )(place, shift, part, came, *cot_frames)


def split_first_kernel(place, mine, came, own, *sends):
    x, y, core = place[0], place[1], place[3]

    @pl.when(core == 0)
    def _():
        for k in range(4):
            part = lax.rem(y + k, 4)
            value = (mine[part].astype(F32) + came[part].astype(F32)).reshape(4 * TPAD, C)
            if k == 0:
                own[...] = value
            else:
                sends[k - 1][...] = value.astype(BF16)

    @pl.when(core != 0)
    def _():
        for k in range(4):
            rows = pl.ds(pl.multiple_of(lax.rem(x + k, 4) * TQ, TQ), TQ)
            value = (mine[:, :, rows, :].astype(F32) + came[:, :, rows, :].astype(F32)).reshape(16 * TQ, C)
            if k == 0:
                own[...] = value
            else:
                sends[k - 1][...] = value.astype(BF16)


def split_first(place, mine, came):
    shape = (4 * TPAD, C)
    return pl.pallas_call(
        split_first_kernel,
        out_shape=(jax.ShapeDtypeStruct(shape, F32),) + (jax.ShapeDtypeStruct(shape, BF16),) * 3,
        in_specs=SMEM_SPEC + vmem_specs(2),
        out_specs=tuple(vmem_specs(4)),
        compiler_params=pltpu.CompilerParams(vmem_limit_bytes=VLIM),
        cost_estimate=cost(0, 4_000_000),
        name="grad_split_first",
    )(place, mine, came)


def split_second_kernel(place, held, first, second, third, own, *sends):
    x, y, core = place[0], place[1], place[3]
    own_sends = (own,) + tuple(sends)

    @pl.when(core == 0)
    def _():
        for k in range(4):
            for zh in range(NZH):
                start = zh * TPAD + lax.rem(x + k, 4) * TQ
                rows = pl.ds(pl.multiple_of(start, TQ), TQ)
                value = held[rows, :]
                for term in (first, second, third):
                    value += term[rows, :].astype(F32)
                own_sends[k][zh] = value

    @pl.when(core != 0)
    def _():
        for k in range(4):
            rows = pl.ds(pl.multiple_of(lax.rem(y + k, 4) * TPAD, TPAD), TPAD)
            value = held[rows, :]
            for term in (first, second, third):
                value += term[rows, :].astype(F32)
            own_sends[k][...] = value.reshape(NZH, TQ, C)


def split_second(place, held, terms):
    shape = (NZH, TQ, C)
    return pl.pallas_call(
        split_second_kernel,
        out_shape=(jax.ShapeDtypeStruct(shape, F32),) * 4,
        in_specs=SMEM_SPEC + vmem_specs(4),
        out_specs=tuple(vmem_specs(4)),
        compiler_params=pltpu.CompilerParams(vmem_limit_bytes=VLIM),
        cost_estimate=cost(0, 2_000_000),
        name="grad_split_second",
    )(place, held, *terms)


def split_third_kernel(place, held, first, second, third, *parts):
    zh = place[2]
    for k in range(4):
        part = lax.rem(zh + k, 4)
        parts[k][...] = held[part] + first[part] + second[part] + third[part]


def split_third(place, held, terms):
    return pl.pallas_call(
        split_third_kernel,
        out_shape=(jax.ShapeDtypeStruct((TQ, C), F32),) * 4,
        in_specs=SMEM_SPEC + vmem_specs(4),
        out_specs=tuple(vmem_specs(4)),
        cost_estimate=cost(0, 800_000),
        name="grad_split_third",
    )(place, held, *terms)


def slope_of(value):
    gate = jax.nn.sigmoid(value)
    return gate * (1.0 + value * (1.0 - gate))


def temporal_back_kernel(place, before, own, after, spatial_out, *rest):
    pieces, (back_spatial, weights, whole, wide, sems) = rest[:4], rest[4:]
    copies = load_copies(place, pieces, whole, sems, TQ)
    for copy in copies:
        copy.start()
    for copy in copies:
        copy.wait()
    for block in range(32):
        pair, core = divmod(block, 2)
        wide[pl.ds(block * TROWS, TPAD), :] = whole[pair // 4, core, pair % 4].astype(F32)
    back = jnp.zeros((ROWS, C), F32)
    for tap in range(3):
        weight = wide[pl.ds(tap * C, C), :].astype(BF16)
        weights[tap] = weight
        back += lax.dot_general(
            neighbour_rows(place, before, own, after, 2 - tap),
            weight,
            (((1,), (1,)), ((), ())),
            preferred_element_type=F32,
        )
    slope = slope_of(spatial_out[...].astype(F32))
    cot = own[...].astype(F32)
    back_spatial[...] = (cot + back * slope).astype(BF16)


def temporal_back(place, cot_frames, spatial_out, pieces):
    return pl.pallas_call(
        temporal_back_kernel,
        out_shape=(jax.ShapeDtypeStruct((ROWS, C), BF16), jax.ShapeDtypeStruct((3, C, C), BF16)),
        in_specs=SMEM_SPEC + vmem_specs(4) + any_specs(4),
        out_specs=tuple(vmem_specs(2)),
        scratch_shapes=[
            pltpu.VMEM((NY, NC, NZH, TPAD, C), BF16),
            pltpu.VMEM((3 * C + 8, C), F32),
            pltpu.SemaphoreType.DMA((32,)),
        ],
        compiler_params=pltpu.CompilerParams(vmem_limit_bytes=VLIM),
        cost_estimate=cost(6 * ROWS * C * C, 8_000_000),
        name="temporal_back",
    )(place, *cot_frames, spatial_out, *pieces)


def temporal_ahead_kernel(place, before, own, after, spatial_out, weights, mixed):
    ahead = spatial_out[...].astype(F32)
    for tap in range(3):
        ahead += jnp.dot(
            neighbour_rows(place, before, own, after, tap), weights[tap], preferred_element_type=F32
        )
    mixed[...] = ahead


def temporal_ahead(place, moved_frames, spatial_out, weights):
    return pl.pallas_call(
        temporal_ahead_kernel,
        out_shape=jax.ShapeDtypeStruct((ROWS, C), F32),
        in_specs=SMEM_SPEC + vmem_specs(5),
        out_specs=vmem_specs(1)[0],
        compiler_params=pltpu.CompilerParams(vmem_limit_bytes=VLIM),
        cost_estimate=cost(6 * ROWS * C * C, 5_000_000),
        name="temporal_ahead",
    )(place, *moved_frames, spatial_out, weights)


def tap_range(first, last):
    return first * C // SROWS, -(-last * C // SROWS)


def add_taps(dy, place, back_spatial, pieces, sums, whole, wide, sems):
    low, high = tap_range(3 * dy, 3 * dy + 3)
    first_y, last_y = low // (NZH * NC), (high - 1) // (NZH * NC)
    copies = load_copies(place, pieces, whole, sems, SQ)
    needed = []
    for own in (0, 1):
        for far in range(4):
            for near in range(4):
                from_y = origin(place, own, far, near)[0]
                needed.append(jnp.logical_and(from_y >= first_y, from_y <= last_y))
    for copy, need in zip(copies, needed):
        pl.when(need)(copy.start)
    for copy, need in zip(copies, needed):
        pl.when(need)(copy.wait)
    for block in range(low, high):
        pair, core = divmod(block, 2)
        wide[pl.ds((block - low) * SROWS, SPAD), :] = whole[pair // 4, core, pair % 4].astype(F32)
    column = lax.rem(lax.broadcasted_iota(jnp.int32, (ROWS, C), 0), WD)
    for dx in range(3):
        product = lax.dot_general(
            back_spatial[...],
            wide[pl.ds((3 * dy + dx) * C - low * SROWS, C), :].astype(BF16),
            (((1,), (1,)), ((), ())),
            preferred_element_type=F32,
        )
        if dx == 0:
            product = jnp.where(column < WD - 1, pltpu.roll(product, ROWS - 1, 0), 0.0)
        elif dx == 2:
            product = jnp.where(column > 0, pltpu.roll(product, 1, 0), 0.0)
        for frame in range(2):
            base = frame * PIX
            to = base + max(dy - 1, 0) * WD
            at = base + max(1 - dy, 0) * WD
            count = PIX - abs(dy - 1) * WD
            sums[pl.ds(to, count), :] += product[at : at + count, :]


def backward_first_kernel(place, back_spatial, *rest):
    pieces, (sums, whole, wide, sems) = rest[:4], rest[4:]
    sums[...] = jnp.zeros_like(sums)
    add_taps(0, place, back_spatial, pieces, sums, whole, wide, sems)


def backward_middle_kernel(place, back_spatial, start, *rest):
    pieces, (sums, whole, wide, sems) = rest[:4], rest[4:]
    sums[...] = start[...]
    add_taps(1, place, back_spatial, pieces, sums, whole, wide, sems)


def backward_last_kernel(place, back_spatial, start, normed, scale, inv_std, *rest):
    pieces, (latent_grad, sums, whole, wide, sems) = rest[:4], rest[4:]
    sums[...] = start[...]
    add_taps(2, place, back_spatial, pieces, sums, whole, wide, sems)
    spread = group_spread()
    for frame in range(2):
        rows = pl.ds(frame * PIX, PIX)
        back_normed = sums[rows, :] * scale[rows, :]
        unit = normed[rows, :]
        first = jnp.sum(back_normed, axis=0, keepdims=True)
        second = jnp.sum(back_normed * unit, axis=0, keepdims=True)
        means = group_means(first, second, spread)
        latent_grad[rows, :] = inv_std[pl.ds(frame, 1), :] * (
            back_normed - means[0:1] - unit * means[1:2]
        )


def tap_scratch(first, last):
    low, high = tap_range(first, last)
    return [
        pltpu.VMEM((NY, NC, NZH, SPAD, C), BF16),
        pltpu.VMEM(((high - low) * SROWS + 20, C), F32),
        pltpu.SemaphoreType.DMA((32,)),
    ]


def backward_taps(kernel, first, place, operands, pieces):
    last = first + 3
    shape = (ROWS, C)
    ends = last == 9
    return pl.pallas_call(
        kernel,
        out_shape=jax.ShapeDtypeStruct(shape, F32),
        in_specs=SMEM_SPEC + vmem_specs(len(operands)) + any_specs(4),
        out_specs=vmem_specs(1)[0],
        scratch_shapes=([pltpu.VMEM(shape, F32)] if ends else []) + tap_scratch(first, last),
        compiler_params=pltpu.CompilerParams(vmem_limit_bytes=VLIM),
        cost_estimate=cost(6 * ROWS * C * C, 8_000_000),
        name="spatial_backward_" + str(first),
    )(place, *operands, *pieces)


def frame_before(last):
    size = NX * NZL
    return lax.ppermute(last, "frames", [(k, (k + 1) % size) for k in range(size)])


def frame_after(first):
    size = NX * NZL
    return lax.ppermute(first, "frames", [((k + 1) % size, k) for k in range(size)])


def halos(own):
    return frame_before(own[1]), frame_after(own[0])


def gather_weights(place_x, spatial_weight, temporal_weight):
    x = place_x
    spatial = jnp.pad(spatial_weight, ((0, SPAD - SROWS), (0, 0)))
    temporal_rows = jnp.pad(temporal_weight, ((0, TPAD - TROWS), (0, 0)))
    quarter = jnp.concatenate(
        [
            lax.dynamic_slice_in_dim(spatial, x * SQ, SQ, 0),
            lax.dynamic_slice_in_dim(temporal_rows, x * TQ, TQ, 0),
        ]
    )
    return quarter


def per_device(
    latents,
    pose,
    timesteps,
    norm_gain,
    norm_bias,
    pose_table,
    time_weight,
    spatial_weight,
    temporal_weight,
    cotangent,
):
    frame_at = lax.axis_index("frames")
    row_at = lax.axis_index("dp")
    x = frame_at % NX
    y = row_at // (NZH * NC)
    zh = (row_at // NC) % NZH
    core = row_at % NC
    place = jnp.stack(
        [x, y, zh, core, frame_at > 0, frame_at < NX * NZL - 1], dtype=jnp.int32
    )

    quarter = gather_weights(x, spatial_weight, temporal_weight)
    came = [send(quarter, zh_step(k)) for k in (1, 2, 3)]
    column = in_order(quarter, came, zh)
    came = [send(column, xy_step(k)) for k in (1, 2, 3)]
    activated, normed, scale, inv_std = norm(
        latents.reshape(ROWS, C), pose[0], pose_table, norm_gain, norm_bias
    )
    activated_other = send(activated, core_swap)
    shift = time_shift(timesteps, time_weight)
    cot_first, cot_last = cotangent[0, 0], cotangent[0, 1]
    activated, cot_first, cot_last, activated_other, column = lax.optimization_barrier(
        (activated, cot_first, cot_last, activated_other, column)
    )
    cols_own = columns(place, activated)
    cot_before, cot_after = frame_before(cot_last), frame_after(cot_first)
    *came, shift, cols_own, cot_before, cot_after = lax.optimization_barrier(
        (*came, shift, cols_own, cot_before, cot_after)
    )
    low, high = jnp.stack([column, came[0]]), jnp.stack([came[1], came[2]])
    one_low, three_high = send(low, yx_step(1)), send(high, yx_step(3))
    one_high, three_low = send(high, yx_step(1)), send(low, yx_step(3))
    activated_other, _ = lax.optimization_barrier((activated_other, low))
    cols_other = columns(place, activated_other)
    one_low, three_high, cols_other = lax.optimization_barrier((one_low, three_high, cols_other))
    cot_frames = cot_before, cotangent.reshape(ROWS, C), cot_after
    cols = cols_own, cols_other
    two_low, two_high = send(one_low, yx_step(1)), send(three_high, yx_step(3))
    total, first_part, first_temporal = forward_first(
        cols, [low, high, one_low, one_high, three_low, three_high]
    )
    two_low, two_high, total = lax.optimization_barrier((two_low, two_high, total))
    part, part_other, last_part, last_temporal = forward_last(total, cols, [two_low, two_high])
    temporal_rows = [first_temporal, last_temporal]
    temporal_rows += [send(first_temporal, core_swap), send(last_temporal, core_swap)]
    came, *temporal_rows = lax.optimization_barrier((send(part_other, core_swap), *temporal_rows))
    spatial_out, moved, mine, other = grad_terms(place, shift, part, came, cot_frames)

    _, frames_dev, pixels, _ = latents.shape
    factor = 1.0 / math.sqrt(lax.axis_size("dp") * frames_dev * lax.axis_size("frames") * pixels)
    came = send(other, core_swap)
    held, *parts = split_first(place, mine, came)
    came = [send(part, yx_step(k + 1)) for k, part in enumerate(parts)]
    ready, frames_moved, _ = lax.optimization_barrier((spatial_out, moved, held))
    moved_before, moved_after = halos(frames_moved.reshape(2, PIX, C))
    back_spatial, weights = temporal_back(place, cot_frames, ready, temporal_rows)
    *came, back_spatial, moved_before, moved_after = lax.optimization_barrier(
        (*came, back_spatial, moved_before, moved_after)
    )

    held, *parts = split_second(place, held, came)
    came = [send(part, xy_step(k + 1)) for k, part in enumerate(parts)]
    moved_before, first_part, last_part, _ = lax.optimization_barrier(
        (moved_before, first_part, last_part, held)
    )
    mixed = temporal_ahead(place, (moved_before, moved, moved_after), spatial_out, weights)
    pieces = [first_part, last_part, send(first_part, core_swap), send(last_part, core_swap)]
    *came, mixed = lax.optimization_barrier((*came, mixed))

    held, *parts = split_third(place, held, came)
    came = [send(part, zh_step(k + 1)) for k, part in enumerate(parts)]
    ready, _ = lax.optimization_barrier((back_spatial, held))
    sums = backward_taps(backward_first_kernel, 0, place, [ready], pieces)
    *came, sums = lax.optimization_barrier((*came, sums))

    held = held + came[0] + came[1] + came[2]
    came = send(held, zl_swap)
    sums, _ = lax.optimization_barrier((sums, held))
    sums = backward_taps(backward_middle_kernel, 3, place, [ready, sums], pieces)
    came, sums = lax.optimization_barrier((came, sums))
    held = (held + came) * factor
    came = [send(held, x_step(k)) for k in (1, 2, 3)]
    sums, _ = lax.optimization_barrier((sums, held))
    latent_grad = backward_taps(
        backward_last_kernel, 6, place, [ready, sums, normed, scale, inv_std], pieces
    )
    *came, latent_grad = lax.optimization_barrier((*came, latent_grad))
    temporal_grad = in_order(held, came, x).reshape(TPAD, C)[:TROWS]
    shape = latents.shape
    return mixed.reshape(shape), latent_grad.reshape(shape), temporal_grad


def solution(mesh):
    placed = (
        P("dp", "frames", None, None),
        P("dp", "frames", None),
        P("dp"),
        P(),
        P(),
        P(),
        P(),
        P("dp", None),
        P("dp", None),
        P("dp", "frames", None, None),
    )
    return jax.shard_map(
        per_device,
        mesh=mesh,
        in_specs=placed,
        out_specs=(P("dp", "frames", None, None), P("dp", "frames", None, None), P("dp", None)),
        check_vma=False,
    )
```

```python
import math

import jax
import jax.numpy as jnp
from jax import lax
from jax.experimental import pallas as pl
from jax.experimental.pallas import tpu as pltpu
from jax.sharding import PartitionSpec as P

GROUP_CH = 40
HT = 9
WD = 16
PIX = HT * WD
C = 640
NX, NY, NZH, NZL, NC = 4, 4, 4, 2, 2
AXES = ("frames", "dp")
SROWS, SPAD, SQ = 180, 192, 48
TROWS, TPAD, TQ = 60, 64, 16
QROWS = SQ + TQ
ROWS = 2 * PIX
F32 = jnp.float32
BF16 = jnp.bfloat16
VLIM = 58 * 1024 * 1024


def coords():
    for zl in range(NZL):
        for x in range(NX):
            for y in range(NY):
                for zh in range(NZH):
                    for c in range(NC):
                        yield zl, x, y, zh, c


def index_of(zl, x, y, zh, c):
    return (zl * NX + x) * (NY * NZH * NC) + (y * NZH + zh) * NC + c


def routes(move):
    return [(index_of(*at), index_of(*move(*at))) for at in coords()]


def send(value, move):
    return lax.ppermute(value, AXES, routes(move))


def core_swap(zl, x, y, zh, c):
    return zl, x, y, zh, 1 - c


def zl_swap(zl, x, y, zh, c):
    return 1 - zl, x, y, zh, c


def zh_step(k):
    return lambda zl, x, y, zh, c: (zl, x, y, (zh + k) % NZH, c)


def x_step(k):
    return lambda zl, x, y, zh, c: (zl, (x + k) % NX, y, zh, c)


def xy_step(k):
    return lambda zl, x, y, zh, c: (
        (zl, (x + k) % NX, y, zh, c) if c == 0 else (zl, x, (y + k) % NY, zh, c)
    )


def yx_step(k):
    return lambda zl, x, y, zh, c: (
        (zl, x, (y + k) % NY, zh, c) if c == 0 else (zl, (x + k) % NX, y, zh, c)
    )


def in_order(own, received, place):
    parts = [received[2], received[1], received[0], own]
    stacked = jnp.stack(parts + parts)
    return lax.dynamic_slice_in_dim(stacked, (3 - place) % 4, 4, axis=0)


def time_shift(timesteps, time_weight):
    half = time_weight.shape[0] // 2
    positions = jnp.arange(half, dtype=jnp.float32)
    frequencies = jnp.exp(-math.log(10000.0) * positions / half)
    angles = timesteps.astype(jnp.float32)[:, None] * frequencies[None, :]
    embedding = jnp.concatenate([jnp.cos(angles), jnp.sin(angles)], axis=-1)
    return jnp.dot(embedding, time_weight, precision=lax.Precision.HIGHEST)


FIRST_PART = (0, 1, 3)
LAST_PART = (2,)


def piece_of(pieces, own, far, near):
    if far in LAST_PART:
        return pieces[own * 2 + 1].at[LAST_PART.index(far), near]
    return pieces[own * 2].at[FIRST_PART.index(far), near]


def origin(place, own, far, near):
    x, y, core = place[0], place[1], place[3]
    flow = core if own == 0 else 1 - core
    from_y = lax.rem(y + 4 - jnp.where(flow == 0, far, near), 4)
    from_x = lax.rem(x + 4 - jnp.where(flow == 0, near, far), 4)
    return from_y, flow, from_x


def load_copies(place, pieces, whole, sems, rows):
    copies = []
    for own in (0, 1):
        for far in range(4):
            for near in range(4):
                from_y, flow, from_x = origin(place, own, far, near)
                copies.append(
                    pltpu.make_async_copy(
                        piece_of(pieces, own, far, near).at[:, pl.ds(0, rows), :],
                        whole.at[from_y, flow, :, pl.ds(pl.multiple_of(from_x * rows, rows), rows), :],
                        sems.at[len(copies)],
                    )
                )
    return copies


def conv_parts(cols, pieces, layout, rows, columns, kept, temporal_rows, sems):
    copies, keeps = [], []
    for k, far in enumerate(layout):
        copies.append(
            (
                pltpu.make_async_copy(pieces[2 * k], rows.at[k, pl.ds(0, 2)], sems.at[5 * k]),
                pltpu.make_async_copy(pieces[2 * k + 1], rows.at[k, pl.ds(2, 2)], sems.at[5 * k + 1]),
                pltpu.make_async_copy(
                    cols[0].at[far], columns.at[k, pl.ds(0, ROWS)], sems.at[5 * k + 2]
                ),
                pltpu.make_async_copy(
                    cols[1].at[far], columns.at[k, pl.ds(ROWS, ROWS)], sems.at[5 * k + 3]
                ),
            )
        )
        keeps.append(pltpu.make_async_copy(rows.at[k], kept.at[k], sems.at[5 * k + 4]))
    for group in copies:
        for copy in group:
            copy.start()
    for k, group in enumerate(copies):
        for copy in group:
            copy.wait()
        keeps[k].start()
        temporal_rows[k] = rows[k, :, :, pl.ds(SQ, TQ), :]
        yield jnp.dot(
            columns[k], rows[k].reshape(4 * NZH * QROWS, C), preferred_element_type=F32
        )
    for keep in keeps:
        keep.wait()


def forward_first_kernel(cols_own, cols_other, *rest):
    cols = cols_own, cols_other
    pieces, (total, kept, temporal_rows, rows, columns, sems) = rest[:6], rest[6:]
    parts = conv_parts(cols, pieces, FIRST_PART, rows, columns, kept, temporal_rows, sems)
    for k, product in enumerate(parts):
        if k == 0:
            total[...] = product
        else:
            total[...] += product


def forward_last_kernel(start, cols_own, cols_other, *rest):
    cols = cols_own, cols_other
    pieces, (own, other, kept, temporal_rows, rows, columns, sems) = rest[:2], rest[2:]
    for product in conv_parts(cols, pieces, LAST_PART, rows, columns, kept, temporal_rows, sems):
        own[...] = product[:ROWS] + start[pl.ds(0, ROWS), :]
        other[...] = product[ROWS:] + start[pl.ds(ROWS, ROWS), :]


def grad_kernel(place, shift, part, came, before, own, after, spatial_out, moved, mine, other, total):
    rounded = (part[...] + came[...] + shift[...]).astype(BF16)
    spatial_out[...] = rounded
    wide = rounded.astype(F32)
    left = (wide * jax.nn.sigmoid(wide)).astype(BF16)
    moved[...] = left
    core = place[3]
    right = jnp.concatenate(
        [neighbour_rows(place, before, own, after, 2 - tap) for tap in range(3)], axis=1
    )
    product = lax.dot_general(left, right, (((0,), (0,)), ((), ())), preferred_element_type=F32)
    for tap in range(3):
        total[pl.ds(tap * C, C), :] = product[:, tap * C : (tap + 1) * C]
    total[pl.ds(3 * C, 8), :] = jnp.zeros((8, C), F32)
    for block in range(32):
        spot = block // 2
        rows = total[pl.ds(block * TROWS, TPAD), :].astype(BF16)

        @pl.when(core == block % 2)
        def _():
            mine[spot // 4, spot % 4] = rows

        @pl.when(core != block % 2)
        def _():
            other[spot // 4, spot % 4] = rows


def neighbour_rows(place, before, own, after, tap):
    if tap == 1:
        return own[...]
    if tap == 0:
        edge = jnp.where(place[4] > 0, before[...], jnp.zeros((PIX, C), BF16))
        return jnp.concatenate([edge, own[pl.ds(0, PIX), :]], axis=0)
    edge = jnp.where(place[5] > 0, after[...], jnp.zeros((PIX, C), BF16))
    return jnp.concatenate([own[pl.ds(PIX, PIX), :], edge], axis=0)


def any_specs(count):
    return [pl.BlockSpec(memory_space=pl.ANY)] * count


def vmem_specs(count):
    return [pl.BlockSpec(memory_space=pltpu.VMEM)] * count


SMEM_SPEC = [pl.BlockSpec(memory_space=pltpu.SMEM)]


def cost(flops, moved):
    return pl.CostEstimate(flops=flops, bytes_accessed=moved, transcendentals=0)


def group_spread():
    group_r = lax.broadcasted_iota(jnp.int32, (C, C), 0) // GROUP_CH
    group_c = lax.broadcasted_iota(jnp.int32, (C, C), 1) // GROUP_CH
    return jnp.where(group_r == group_c, 1.0 / (PIX * GROUP_CH), 0.0).astype(F32)


def group_means(first, second, spread):
    both = jnp.concatenate([first, second, jnp.zeros((6, C), F32)], axis=0)
    return jnp.dot(both, spread, precision=lax.Precision.HIGHEST, preferred_element_type=F32)


def segments(core):
    found = {}
    for y in range(NY):
        for x in range(NX):
            parts = []
            for zh in range(NZH):
                block = (y * NZH + zh) * NC + core
                start = SROWS * block + SQ * x
                end = min(start + SQ, SROWS * (block + 1))
                lane = zh * QROWS
                while start < end:
                    tap, channel = divmod(start, C)
                    count = min(end - start, C - channel)
                    parts.append((lane, tap, channel, count))
                    start += count
                    lane += count
            found[y, x] = parts
    return found


def norm_kernel(latents, pose, table, gain, bias, activated, normed, scale, inv_std):
    kinds = lax.broadcasted_iota(jnp.int32, (table.shape[0], PIX), 0)
    gains = gain[...].reshape(1, C)
    biases = bias[...].reshape(1, C)
    spread = group_spread()
    for frame in range(2):
        rows = pl.ds(frame * PIX, PIX)
        onehot = (pose[pl.ds(frame, 1), :] == kinds).astype(F32)
        shifted = latents[rows, :].astype(F32) + lax.dot_general(
            onehot,
            table[...],
            (((0,), (0,)), ((), ())),
            precision=lax.Precision.HIGHEST,
            preferred_element_type=F32,
        )
        means = group_means(
            jnp.sum(shifted, axis=0, keepdims=True),
            jnp.sum(shifted * shifted, axis=0, keepdims=True),
            spread,
        )
        center = means[0:1]
        inverse = lax.rsqrt(means[1:2] - center * center + 1e-05)
        inv_std[pl.ds(frame, 1), :] = inverse
        unit = (shifted - center) * inverse
        normed[rows, :] = unit
        value = unit * gains + biases
        gate = jax.nn.sigmoid(value)
        scale[rows, :] = gate * (1.0 + value * (1.0 - gate)) * gains
        activated[rows, :] = (value * gate).astype(BF16)


def norm(latents, pose, table, gain, bias):
    return pl.pallas_call(
        norm_kernel,
        out_shape=(
            jax.ShapeDtypeStruct((ROWS, C), BF16),
            jax.ShapeDtypeStruct((ROWS, C), F32),
            jax.ShapeDtypeStruct((ROWS, C), F32),
            jax.ShapeDtypeStruct((2, C), F32),
        ),
        in_specs=vmem_specs(5),
        out_specs=tuple(vmem_specs(4)),
        compiler_params=pltpu.CompilerParams(vmem_limit_bytes=VLIM),
        cost_estimate=cost(500_000_000, 3_000_000),
        name="group_norm",
    )(latents, pose, table, gain, bias)


def columns_kernel(place, clip, cols, padded, chunk):
    at_x, at_y, core = place[0], place[1], place[3]
    column = lax.rem(lax.broadcasted_iota(jnp.int32, (PIX, C), 0), WD)
    for frame in range(2):
        active = clip[pl.ds(frame * PIX, PIX), :].astype(F32)
        for dx in range(3):
            if dx == 0:
                moved = jnp.where(column > 0, pltpu.roll(active, 1, 0), 0.0)
            elif dx == 1:
                moved = active
            else:
                moved = jnp.where(column < WD - 1, pltpu.roll(active, PIX - 1, 0), 0.0)
            padded[dx, frame, pl.ds(0, WD), :] = jnp.zeros((WD, C), BF16)
            padded[dx, frame, pl.ds(WD, PIX), :] = moved.astype(BF16)
            padded[dx, frame, pl.ds(WD + PIX, WD), :] = jnp.zeros((WD, C), BF16)
    chunk[...] = jnp.zeros_like(chunk)

    def lay_out(flow):
        for number, ((y, x), parts) in enumerate(segments(flow).items()):
            slot = number % 2
            if x == NX - 1:
                chunk[slot] = jnp.zeros((ROWS, NZH * QROWS), BF16)
            for lane, tap, channel, count in parts:
                dy, dx = divmod(tap, 3)
                for frame in range(2):
                    chunk[slot, frame * PIX : (frame + 1) * PIX, lane : lane + count] = padded[
                        dx, frame, dy * WD : dy * WD + PIX, channel : channel + count
                    ]
            far_y, far_x = lax.rem(at_y + 4 - y, 4), lax.rem(at_x + 4 - x, 4)
            far, near = (far_y, far_x) if flow == 0 else (far_x, far_y)
            cols[far, :, pl.ds(pl.multiple_of(near * 256, 256), 256)] = chunk[slot]

    pl.when(core == 0)(lambda: lay_out(0))
    pl.when(core != 0)(lambda: lay_out(1))


def columns(place, clip):
    return pl.pallas_call(
        columns_kernel,
        out_shape=jax.ShapeDtypeStruct((4, ROWS, 4 * NZH * QROWS), BF16),
        in_specs=SMEM_SPEC + vmem_specs(1),
        out_specs=vmem_specs(1)[0],
        scratch_shapes=[
            pltpu.VMEM((3, 2, PIX + 2 * WD, C), BF16),
            pltpu.VMEM((2, ROWS, NZH * QROWS), BF16),
        ],
        compiler_params=pltpu.CompilerParams(vmem_limit_bytes=VLIM),
        cost_estimate=cost(500_000_000, 4_000_000),
        name="window_columns",
    )(place, clip)


def forward_call(kernel, layout, outs, operands, cols, pieces, name):
    count = len(layout)
    return pl.pallas_call(
        kernel,
        out_shape=(jax.ShapeDtypeStruct(outs[0], F32),) * outs[1]
        + (
            jax.ShapeDtypeStruct((count, 4, NZH, QROWS, C), BF16),
            jax.ShapeDtypeStruct((count, 4, NZH, TQ, C), BF16),
        ),
        in_specs=vmem_specs(len(operands)) + any_specs(2 + len(pieces)),
        out_specs=tuple(vmem_specs(outs[1]) + any_specs(1) + vmem_specs(1)),
        scratch_shapes=[
            pltpu.VMEM((count, 4, NZH, QROWS, C), BF16),
            pltpu.VMEM((count, 2 * ROWS, 4 * NZH * QROWS), BF16),
            pltpu.SemaphoreType.DMA((5 * count,)),
        ],
        compiler_params=pltpu.CompilerParams(vmem_limit_bytes=VLIM),
        cost_estimate=cost(4 * ROWS * 1024 * count * C, 3_000_000 * count),
        name=name,
    )(*operands, *cols, *pieces)


def forward_first(cols, pieces):
    return forward_call(
        forward_first_kernel, FIRST_PART, ((2 * ROWS, C), 1), (), cols, pieces, "spatial_forward_first"
    )


def forward_last(start, cols, pieces):
    return forward_call(
        forward_last_kernel, LAST_PART, ((ROWS, C), 2), (start,), cols, pieces, "spatial_forward_last"
    )


def grad_terms(place, shift, part, came, cot_frames):
    shape = (NY, NZH, TPAD, C)
    return pl.pallas_call(
        grad_kernel,
        out_shape=(jax.ShapeDtypeStruct((ROWS, C), BF16),) * 2
        + (jax.ShapeDtypeStruct(shape, BF16),) * 2,
        in_specs=SMEM_SPEC + vmem_specs(6),
        out_specs=tuple(vmem_specs(4)),
        scratch_shapes=[pltpu.VMEM((3 * C + 8, C), F32)],
        compiler_params=pltpu.CompilerParams(vmem_limit_bytes=VLIM),
        cost_estimate=cost(2 * ROWS * 3 * C * C, 8_000_000),
        name="temporal_grad_terms",
    )(place, shift, part, came, *cot_frames)


def split_first_kernel(place, mine, came, own, *sends):
    x, y, core = place[0], place[1], place[3]

    @pl.when(core == 0)
    def _():
        for k in range(4):
            part = lax.rem(y + k, 4)
            value = (mine[part].astype(F32) + came[part].astype(F32)).reshape(4 * TPAD, C)
            if k == 0:
                own[...] = value
            else:
                sends[k - 1][...] = value.astype(BF16)

    @pl.when(core != 0)
    def _():
        for k in range(4):
            rows = pl.ds(pl.multiple_of(lax.rem(x + k, 4) * TQ, TQ), TQ)
            value = (mine[:, :, rows, :].astype(F32) + came[:, :, rows, :].astype(F32)).reshape(16 * TQ, C)
            if k == 0:
                own[...] = value
            else:
                sends[k - 1][...] = value.astype(BF16)


def split_first(place, mine, came):
    shape = (4 * TPAD, C)
    return pl.pallas_call(
        split_first_kernel,
        out_shape=(jax.ShapeDtypeStruct(shape, F32),) + (jax.ShapeDtypeStruct(shape, BF16),) * 3,
        in_specs=SMEM_SPEC + vmem_specs(2),
        out_specs=tuple(vmem_specs(4)),
        compiler_params=pltpu.CompilerParams(vmem_limit_bytes=VLIM),
        cost_estimate=cost(0, 4_000_000),
        name="grad_split_first",
    )(place, mine, came)


def split_second_kernel(place, held, first, second, third, own, *sends):
    x, y, core = place[0], place[1], place[3]
    own_sends = (own,) + tuple(sends)

    @pl.when(core == 0)
    def _():
        for k in range(4):
            for zh in range(NZH):
                start = zh * TPAD + lax.rem(x + k, 4) * TQ
                rows = pl.ds(pl.multiple_of(start, TQ), TQ)
                value = held[rows, :]
                for term in (first, second, third):
                    value += term[rows, :].astype(F32)
                own_sends[k][zh] = value

    @pl.when(core != 0)
    def _():
        for k in range(4):
            rows = pl.ds(pl.multiple_of(lax.rem(y + k, 4) * TPAD, TPAD), TPAD)
            value = held[rows, :]
            for term in (first, second, third):
                value += term[rows, :].astype(F32)
            own_sends[k][...] = value.reshape(NZH, TQ, C)


def split_second(place, held, terms):
    shape = (NZH, TQ, C)
    return pl.pallas_call(
        split_second_kernel,
        out_shape=(jax.ShapeDtypeStruct(shape, F32),) * 4,
        in_specs=SMEM_SPEC + vmem_specs(4),
        out_specs=tuple(vmem_specs(4)),
        compiler_params=pltpu.CompilerParams(vmem_limit_bytes=VLIM),
        cost_estimate=cost(0, 2_000_000),
        name="grad_split_second",
    )(place, held, *terms)


def split_third_kernel(place, held, first, second, third, *parts):
    zh = place[2]
    for k in range(4):
        part = lax.rem(zh + k, 4)
        parts[k][...] = held[part] + first[part] + second[part] + third[part]


def split_third(place, held, terms):
    return pl.pallas_call(
        split_third_kernel,
        out_shape=(jax.ShapeDtypeStruct((TQ, C), F32),) * 4,
        in_specs=SMEM_SPEC + vmem_specs(4),
        out_specs=tuple(vmem_specs(4)),
        cost_estimate=cost(0, 800_000),
        name="grad_split_third",
    )(place, held, *terms)


def slope_of(value):
    gate = jax.nn.sigmoid(value)
    return gate * (1.0 + value * (1.0 - gate))


def temporal_back_kernel(place, before, own, after, spatial_out, *rest):
    pieces, (back_spatial, weights, whole, wide, sems) = rest[:4], rest[4:]
    copies = load_copies(place, pieces, whole, sems, TQ)
    for copy in copies:
        copy.start()
    for copy in copies:
        copy.wait()
    for block in range(32):
        pair, core = divmod(block, 2)
        wide[pl.ds(block * TROWS, TPAD), :] = whole[pair // 4, core, pair % 4].astype(F32)
    back = jnp.zeros((ROWS, C), F32)
    for tap in range(3):
        weight = wide[pl.ds(tap * C, C), :].astype(BF16)
        weights[tap] = weight
        back += lax.dot_general(
            neighbour_rows(place, before, own, after, 2 - tap),
            weight,
            (((1,), (1,)), ((), ())),
            preferred_element_type=F32,
        )
    slope = slope_of(spatial_out[...].astype(F32))
    cot = own[...].astype(F32)
    back_spatial[...] = (cot + back * slope).astype(BF16)


def temporal_back(place, cot_frames, spatial_out, pieces):
    return pl.pallas_call(
        temporal_back_kernel,
        out_shape=(jax.ShapeDtypeStruct((ROWS, C), BF16), jax.ShapeDtypeStruct((3, C, C), BF16)),
        in_specs=SMEM_SPEC + vmem_specs(4) + any_specs(4),
        out_specs=tuple(vmem_specs(2)),
        scratch_shapes=[
            pltpu.VMEM((NY, NC, NZH, TPAD, C), BF16),
            pltpu.VMEM((3 * C + 8, C), F32),
            pltpu.SemaphoreType.DMA((32,)),
        ],
        compiler_params=pltpu.CompilerParams(vmem_limit_bytes=VLIM),
        cost_estimate=cost(6 * ROWS * C * C, 8_000_000),
        name="temporal_back",
    )(place, *cot_frames, spatial_out, *pieces)


def temporal_ahead_kernel(place, before, own, after, spatial_out, weights, mixed):
    ahead = spatial_out[...].astype(F32)
    for tap in range(3):
        ahead += jnp.dot(
            neighbour_rows(place, before, own, after, tap), weights[tap], preferred_element_type=F32
        )
    mixed[...] = ahead


def temporal_ahead(place, moved_frames, spatial_out, weights):
    return pl.pallas_call(
        temporal_ahead_kernel,
        out_shape=jax.ShapeDtypeStruct((ROWS, C), F32),
        in_specs=SMEM_SPEC + vmem_specs(5),
        out_specs=vmem_specs(1)[0],
        compiler_params=pltpu.CompilerParams(vmem_limit_bytes=VLIM),
        cost_estimate=cost(6 * ROWS * C * C, 5_000_000),
        name="temporal_ahead",
    )(place, *moved_frames, spatial_out, weights)


def tap_range(first, last):
    return first * C // SROWS, -(-last * C // SROWS)


def add_taps(dy, place, back_spatial, pieces, sums, whole, wide, sems):
    low, high = tap_range(3 * dy, 3 * dy + 3)
    first_y, last_y = low // (NZH * NC), (high - 1) // (NZH * NC)
    copies = load_copies(place, pieces, whole, sems, SQ)
    needed = []
    for own in (0, 1):
        for far in range(4):
            for near in range(4):
                from_y = origin(place, own, far, near)[0]
                needed.append(jnp.logical_and(from_y >= first_y, from_y <= last_y))
    for copy, need in zip(copies, needed):
        pl.when(need)(copy.start)
    sources = [
        origin(place, own, far, near)[0] for own in (0, 1) for far in range(4) for near in range(4)
    ]
    for block in range(low, high):
        if block == low or block % (NZH * NC) == 0:
            for copy, source in zip(copies, sources):
                pl.when(source == block // (NZH * NC))(copy.wait)
        pair, core = divmod(block, 2)
        wide[pl.ds((block - low) * SROWS, SPAD), :] = whole[pair // 4, core, pair % 4].astype(F32)
    column = lax.rem(lax.broadcasted_iota(jnp.int32, (ROWS, C), 0), WD)
    for dx in range(3):
        product = lax.dot_general(
            back_spatial[...],
            wide[pl.ds((3 * dy + dx) * C - low * SROWS, C), :].astype(BF16),
            (((1,), (1,)), ((), ())),
            preferred_element_type=F32,
        )
        if dx == 0:
            product = jnp.where(column < WD - 1, pltpu.roll(product, ROWS - 1, 0), 0.0)
        elif dx == 2:
            product = jnp.where(column > 0, pltpu.roll(product, 1, 0), 0.0)
        for frame in range(2):
            base = frame * PIX
            to = base + max(dy - 1, 0) * WD
            at = base + max(1 - dy, 0) * WD
            count = PIX - abs(dy - 1) * WD
            sums[pl.ds(to, count), :] += product[at : at + count, :]


def backward_first_kernel(place, back_spatial, *rest):
    pieces, (sums, whole, wide, sems) = rest[:4], rest[4:]
    sums[...] = jnp.zeros_like(sums)
    add_taps(0, place, back_spatial, pieces, sums, whole, wide, sems)


def backward_middle_kernel(place, back_spatial, start, *rest):
    pieces, (sums, whole, wide, sems) = rest[:4], rest[4:]
    sums[...] = start[...]
    add_taps(1, place, back_spatial, pieces, sums, whole, wide, sems)


def backward_last_kernel(place, back_spatial, start, normed, scale, inv_std, *rest):
    pieces, (latent_grad, sums, whole, wide, sems) = rest[:4], rest[4:]
    sums[...] = start[...]
    add_taps(2, place, back_spatial, pieces, sums, whole, wide, sems)
    spread = group_spread()
    for frame in range(2):
        rows = pl.ds(frame * PIX, PIX)
        back_normed = sums[rows, :] * scale[rows, :]
        unit = normed[rows, :]
        first = jnp.sum(back_normed, axis=0, keepdims=True)
        second = jnp.sum(back_normed * unit, axis=0, keepdims=True)
        means = group_means(first, second, spread)
        latent_grad[rows, :] = inv_std[pl.ds(frame, 1), :] * (
            back_normed - means[0:1] - unit * means[1:2]
        )


def tap_scratch(first, last):
    low, high = tap_range(first, last)
    return [
        pltpu.VMEM((NY, NC, NZH, SPAD, C), BF16),
        pltpu.VMEM(((high - low) * SROWS + 20, C), F32),
        pltpu.SemaphoreType.DMA((32,)),
    ]


def backward_taps(kernel, first, place, operands, pieces):
    last = first + 3
    shape = (ROWS, C)
    ends = last == 9
    return pl.pallas_call(
        kernel,
        out_shape=jax.ShapeDtypeStruct(shape, F32),
        in_specs=SMEM_SPEC + vmem_specs(len(operands)) + any_specs(4),
        out_specs=vmem_specs(1)[0],
        scratch_shapes=([pltpu.VMEM(shape, F32)] if ends else []) + tap_scratch(first, last),
        compiler_params=pltpu.CompilerParams(vmem_limit_bytes=VLIM),
        cost_estimate=cost(6 * ROWS * C * C, 8_000_000),
        name="spatial_backward_" + str(first),
    )(place, *operands, *pieces)


def frame_before(last):
    size = NX * NZL
    return lax.ppermute(last, "frames", [(k, (k + 1) % size) for k in range(size)])


def frame_after(first):
    size = NX * NZL
    return lax.ppermute(first, "frames", [((k + 1) % size, k) for k in range(size)])


def halos(own):
    return frame_before(own[1]), frame_after(own[0])


def gather_weights(place_x, spatial_weight, temporal_weight):
    x = place_x
    spatial = jnp.pad(spatial_weight, ((0, SPAD - SROWS), (0, 0)))
    temporal_rows = jnp.pad(temporal_weight, ((0, TPAD - TROWS), (0, 0)))
    quarter = jnp.concatenate(
        [
            lax.dynamic_slice_in_dim(spatial, x * SQ, SQ, 0),
            lax.dynamic_slice_in_dim(temporal_rows, x * TQ, TQ, 0),
        ]
    )
    return quarter


def per_device(
    latents,
    pose,
    timesteps,
    norm_gain,
    norm_bias,
    pose_table,
    time_weight,
    spatial_weight,
    temporal_weight,
    cotangent,
):
    frame_at = lax.axis_index("frames")
    row_at = lax.axis_index("dp")
    x = frame_at % NX
    y = row_at // (NZH * NC)
    zh = (row_at // NC) % NZH
    core = row_at % NC
    place = jnp.stack(
        [x, y, zh, core, frame_at > 0, frame_at < NX * NZL - 1], dtype=jnp.int32
    )

    quarter = gather_weights(x, spatial_weight, temporal_weight)
    came = [send(quarter, zh_step(k)) for k in (1, 2, 3)]
    column = in_order(quarter, came, zh)
    came = [send(column, xy_step(k)) for k in (1, 2, 3)]
    activated, normed, scale, inv_std = norm(
        latents.reshape(ROWS, C), pose[0], pose_table, norm_gain, norm_bias
    )
    activated_other = send(activated, core_swap)
    cot_first, cot_last = cotangent[0, 0], cotangent[0, 1]
    activated, cot_last, activated_other, column = lax.optimization_barrier(
        (activated, cot_last, activated_other, column)
    )
    cols_own = columns(place, activated)
    cot_before = frame_before(cot_last)
    *came, cols_own, cot_before = lax.optimization_barrier((*came, cols_own, cot_before))
    low, high = jnp.stack([column, came[0]]), jnp.stack([came[1], came[2]])
    one_low, three_high = send(low, yx_step(1)), send(high, yx_step(3))
    one_high, three_low = send(high, yx_step(1)), send(low, yx_step(3))
    activated_other, cot_first, _ = lax.optimization_barrier((activated_other, cot_first, low))
    cot_after = frame_after(cot_first)
    cols_other = columns(place, activated_other)
    one_low, three_high, cols_other, cot_after = lax.optimization_barrier(
        (one_low, three_high, cols_other, cot_after)
    )
    cot_frames = cot_before, cotangent.reshape(ROWS, C), cot_after
    cols = cols_own, cols_other
    two_low, two_high = send(one_low, yx_step(1)), send(three_high, yx_step(3))
    total, first_part, first_temporal = forward_first(
        cols, [low, high, one_low, one_high, three_low, three_high]
    )
    two_low, two_high, total = lax.optimization_barrier((two_low, two_high, total))
    part, part_other, last_part, last_temporal = forward_last(total, cols, [two_low, two_high])
    timesteps, part = lax.optimization_barrier((timesteps, part))
    shift = time_shift(timesteps, time_weight)
    temporal_rows = [first_temporal, last_temporal]
    temporal_rows += [send(first_temporal, core_swap), send(last_temporal, core_swap)]
    came, *temporal_rows = lax.optimization_barrier((send(part_other, core_swap), *temporal_rows))
    spatial_out, moved, mine, other = grad_terms(place, shift, part, came, cot_frames)

    _, frames_dev, pixels, _ = latents.shape
    factor = 1.0 / math.sqrt(lax.axis_size("dp") * frames_dev * lax.axis_size("frames") * pixels)
    came = send(other, core_swap)
    held, *parts = split_first(place, mine, came)
    came = [send(part, yx_step(k + 1)) for k, part in enumerate(parts)]
    ready, frames_moved, _ = lax.optimization_barrier((spatial_out, moved, held))
    moved_before, moved_after = halos(frames_moved.reshape(2, PIX, C))
    back_spatial, weights = temporal_back(place, cot_frames, ready, temporal_rows)
    *came, back_spatial, moved_before, moved_after = lax.optimization_barrier(
        (*came, back_spatial, moved_before, moved_after)
    )

    held, *parts = split_second(place, held, came)
    came = [send(part, xy_step(k + 1)) for k, part in enumerate(parts)]
    moved_before, first_part, last_part, _ = lax.optimization_barrier(
        (moved_before, first_part, last_part, held)
    )
    mixed = temporal_ahead(place, (moved_before, moved, moved_after), spatial_out, weights)
    pieces = [first_part, last_part, send(first_part, core_swap), send(last_part, core_swap)]
    *came, mixed = lax.optimization_barrier((*came, mixed))

    held, *parts = split_third(place, held, came)
    came = [send(part, zh_step(k + 1)) for k, part in enumerate(parts)]
    ready, _ = lax.optimization_barrier((back_spatial, held))
    sums = backward_taps(backward_first_kernel, 0, place, [ready], pieces)
    *came, sums = lax.optimization_barrier((*came, sums))

    held = held + came[0] + came[1] + came[2]
    came = send(held, zl_swap)
    sums, _ = lax.optimization_barrier((sums, held))
    sums = backward_taps(backward_middle_kernel, 3, place, [ready, sums], pieces)
    came, sums = lax.optimization_barrier((came, sums))
    held = (held + came) * factor
    came = [send(held, x_step(k)) for k in (1, 2, 3)]
    sums, _ = lax.optimization_barrier((sums, held))
    latent_grad = backward_taps(
        backward_last_kernel, 6, place, [ready, sums, normed, scale, inv_std], pieces
    )
    *came, latent_grad = lax.optimization_barrier((*came, latent_grad))
    temporal_grad = in_order(held, came, x).reshape(TPAD, C)[:TROWS]
    shape = latents.shape
    return mixed.reshape(shape), latent_grad.reshape(shape), temporal_grad


def solution(mesh):
    placed = (
        P("dp", "frames", None, None),
        P("dp", "frames", None),
        P("dp"),
        P(),
        P(),
        P(),
        P(),
        P("dp", None),
        P("dp", None),
        P("dp", "frames", None, None),
    )
    return jax.shard_map(
        per_device,
        mesh=mesh,
        in_specs=placed,
        out_specs=(P("dp", "frames", None, None), P("dp", "frames", None, None), P("dp", None)),
        check_vma=False,
    )
```
